32 devices in a mesh: groups: 2 (over x), row: 8 (over z, y), col: 2 (over core).
Axes of the slice: x: 2, y: 2, z: 4, core: 2. Of those that a mesh axis runs over, the one named last changes fastest.
Arguments:
- vectors: bfloat16 [1024, 16, 64], P(('groups', 'row', 'col')), parts along dimension 0, may hold values from -6 to 6
- leaf_basis: bfloat16 [1024, 64, 64], P(('groups', 'row', 'col')), parts along dimension 0, may hold values from -0.75 to 0.75
- leaf_transfer: bfloat16 [1024, 64, 64], P(('groups', 'row', 'col')), parts along dimension 0, may hold values from -0.5 to 0.5
- pair_transfer: bfloat16 [512, 64, 64], P(('groups', 'row', 'col')), parts along dimension 0, may hold values from -0.5 to 0.5
- near_blocks: bfloat16 [3, 1024, 3, 64, 64], P(None, ('groups', 'row', 'col')), parts along dimension 1, may hold values from -0.4375 to 0.4375
- near_offset: int32 [1024, 3], P(('groups', 'row', 'col')), parts along dimension 0, may hold values from -2 to 2
- leaf_send: int32 [32, 5, 8], P(('groups', 'row', 'col')), parts along dimension 0, may hold values from 0 to 31
- leaf_list: int32 [1024, 4], P(('groups', 'row', 'col')), parts along dimension 0, may hold values from 0 to 39
- leaf_coupling: bfloat16 [3, 1024, 4, 64, 64], P(None, ('groups', 'row', 'col')), parts along dimension 1, may hold values from -0.375 to 0.375
- pair_send: int32 [32, 5, 2], P(('groups', 'row', 'col')), parts along dimension 0, may hold values from 0 to 15
- pair_list: int32 [512, 4], P(('groups', 'row', 'col')), parts along dimension 0, may hold values from 0 to 9
- pair_coupling: bfloat16 [3, 512, 4, 64, 64], P(None, ('groups', 'row', 'col')), parts along dimension 1, may hold values from -0.375 to 0.375
- top_list: int32 [256, 8], P(('groups', 'row', 'col')), parts along dimension 0, may hold values from 0 to 127
- top_coupling: bfloat16 [3, 256, 8, 64, 64], P(None, ('groups', 'row', 'col')), parts along dimension 1, may hold values from -0.25 to 0.25
Outputs:
- potential: bfloat16 [3, 1024, 16, 64], P(None, ('groups', 'row', 'col')), parts along dimension 1
The draws below stay inside these ranges and needn't reach their ends.
There are 2 independent parts, one for each index of `groups`. The reference program is written for one: setup_inputs(seed, part) draws one part's arguments, and reference() takes and returns one part's arrays. A program takes and returns all parts, laid end to end along the dimension named above; each array names one. Nothing has to cross between parts.
All inputs are finite; a program needn't handle non-finite values.
Results may differ from the reference program's by a relative error of at most 0.0058.
Values may be sent and summed in bfloat16 or wider, within the bound.
No kernel may reach another device: no remote copies, remote signals or barrier semaphores. Data moves between devices by JAX's collectives and lax.ppermute only.
A program may use at most 64 MiB of HBM per device.

```python
import jax
import jax.numpy as jnp

LEAF = 64
RANK = 64
VECS = 16
KERNELS = 3
LEAVES_DEV = 32
M0 = 4
M1 = 4
MT = 8
REACH = 2
WIN = 5
CAP0 = 8
CAP1 = 2
NEAR = 3
HW = 2
DEVS = 16
NLEAF = 512
NPAIR = 256
NTOP = 128


def touch_ends(array, key, low, largest):
    spot = [jax.random.randint(jax.random.fold_in(key, axis), (), 0, length) for axis, length in enumerate(array.shape)]
    widest = array.shape.index(max(array.shape))
    neighbour = spot[:widest] + [(spot[widest] + 1) % array.shape[widest]] + spot[widest + 1:]
    return array.at[tuple(spot)].set(low).at[tuple(neighbour)].set(largest)


def block_scale(stream_key, extent, shards, least, largest):
    gain = 1.0
    for position, blocks in shards:
        heights = jax.random.uniform(jax.random.fold_in(jax.random.fold_in(stream_key, 6), position), (blocks,), jnp.float32, least / len(shards), largest / len(shards))
        gain = gain * jnp.repeat(jnp.exp(heights), extent[position] // blocks).reshape((-1,) + (1,) * (len(extent) - 1 - position))
    return gain


def bell_draw(key, dims, deviation, limit, shards=(), kind=jnp.bfloat16):
    gain = block_scale(key, dims, shards, -0.22, 0.18) if shards else 1.0
    entries = jax.random.normal(key, dims, jnp.float32) * deviation * gain
    return jnp.minimum(jnp.maximum(entries, -limit), limit).astype(kind)


def setup_inputs(seed: int = 0, part: int = 0) -> dict:
    keys = jax.random.split(jax.random.key(seed), 15)
    own_keys = jax.random.split(jax.random.fold_in(keys[14], part), 15)
    return {
        "vectors": bell_draw(own_keys[0], (NLEAF, VECS, LEAF), 1.0, 6.0, ((0, 16),)),
        "leaf_basis": bell_draw(own_keys[1], (NLEAF, LEAF, RANK), LEAF ** -0.5, 0.75, ((0, 16),)),
        "leaf_transfer": bell_draw(own_keys[2], (NLEAF, RANK, RANK), (2 * RANK) ** -0.5, 0.5, ((0, 16),)),
        "pair_transfer": bell_draw(own_keys[3], (NPAIR, RANK, RANK), (2 * RANK) ** -0.5, 0.5, ((0, 16),)),
        "near_blocks": bell_draw(own_keys[4], (KERNELS, NLEAF, NEAR, LEAF, LEAF), (NEAR * LEAF) ** -0.5, 0.4375, ((1, 16),)),
        "near_offset": touch_ends(jax.random.randint(own_keys[5], (NLEAF, NEAR), 0 - HW, HW + 1), jax.random.fold_in(own_keys[5], 1), 0 - HW, HW).astype(jnp.int32),
        "leaf_send": touch_ends(jax.random.randint(own_keys[6], (DEVS, WIN, CAP0), 0, LEAVES_DEV), jax.random.fold_in(own_keys[6], 1), 0, LEAVES_DEV - 1).astype(jnp.int32),
        "leaf_list": touch_ends(jax.random.randint(own_keys[7], (NLEAF, M0), 0, WIN * CAP0), jax.random.fold_in(own_keys[7], 1), 0, (WIN * CAP0) - 1).astype(jnp.int32),
        "leaf_coupling": bell_draw(own_keys[8], (KERNELS, NLEAF, M0, RANK, RANK), (M0 * RANK) ** -0.5, 0.375, ((1, 16),)),
        "pair_send": touch_ends(jax.random.randint(own_keys[9], (DEVS, WIN, CAP1), 0, LEAVES_DEV // 2), jax.random.fold_in(own_keys[9], 1), 0, (LEAVES_DEV // 2) - 1).astype(jnp.int32),
        "pair_list": touch_ends(jax.random.randint(own_keys[10], (NPAIR, M1), 0, WIN * CAP1), jax.random.fold_in(own_keys[10], 1), 0, (WIN * CAP1) - 1).astype(jnp.int32),
        "pair_coupling": bell_draw(own_keys[11], (KERNELS, NPAIR, M1, RANK, RANK), (M1 * RANK) ** -0.5, 0.375, ((1, 16),)),
        "top_list": touch_ends(jax.random.randint(own_keys[12], (NTOP, MT), 0, NTOP), jax.random.fold_in(own_keys[12], 1), 0, NTOP - 1).astype(jnp.int32),
        "top_coupling": bell_draw(own_keys[13], (KERNELS, NTOP, MT, RANK, RANK), (MT * RANK) ** -0.5, 0.25, ((1, 16),)),
    }


def reference(vectors, leaf_basis, leaf_transfer, pair_transfer, near_blocks, near_offset, leaf_send, leaf_list, leaf_coupling, pair_send, pair_list, pair_coupling, top_list, top_coupling):
    f32 = jnp.float32
    bf = jnp.bfloat16
    tiles = vectors.astype(f32)
    basis = leaf_basis.astype(f32)
    trans_leaf = leaf_transfer.astype(f32)
    trans_pair = pair_transfer.astype(f32)
    up0 = jnp.einsum('tvp,tpr->tvr', tiles, basis).astype(bf)
    up1 = jnp.einsum('tvr,trs->tvs', up0.astype(f32), trans_leaf).reshape(NPAIR, 2, VECS, RANK).sum(1).astype(bf)
    up2 = jnp.einsum('tvr,trs->tvs', up1.astype(f32), trans_pair).reshape(NTOP, 2, VECS, RANK).sum(1).astype(bf)
    owner0 = (jnp.arange(NLEAF, dtype=jnp.int32) // LEAVES_DEV)[:, None]
    offset0 = leaf_list // CAP0
    src_dev0 = jnp.mod(owner0 + offset0 - REACH, DEVS).astype(jnp.int32)
    src0 = src_dev0 * LEAVES_DEV + leaf_send[src_dev0, offset0, leaf_list % CAP0]
    rows0 = up0[src0].astype(f32)
    owner1 = (jnp.arange(NPAIR, dtype=jnp.int32) // (LEAVES_DEV // 2))[:, None]
    offset1 = pair_list // CAP1
    src_dev1 = jnp.mod(owner1 + offset1 - REACH, DEVS).astype(jnp.int32)
    src1 = src_dev1 * (LEAVES_DEV // 2) + pair_send[src_dev1, offset1, pair_list % CAP1]
    rows1 = up1[src1].astype(f32)
    rows2 = up2[top_list].astype(f32)
    padded = jnp.pad(tiles, ((HW, HW), (0, 0), (0, 0)))
    near_index = jnp.arange(NLEAF, dtype=jnp.int32)[:, None] + HW + near_offset
    neighbours = padded[near_index]
    results = []
    for kernel in range(KERNELS):
        far0 = jnp.einsum('tmrs,tmvs->tvr', leaf_coupling[kernel].astype(f32), rows0)
        far1 = jnp.einsum('tmrs,tmvs->tvr', pair_coupling[kernel].astype(f32), rows1)
        far2 = jnp.einsum('tmrs,tmvs->tvr', top_coupling[kernel].astype(f32), rows2)
        down2 = far2.astype(bf).astype(f32)
        down1 = (far1 + jnp.einsum('trs,tvs->tvr', trans_pair, jnp.repeat(down2, 2, axis=0))).astype(bf).astype(f32)
        down0 = (far0 + jnp.einsum('trs,tvs->tvr', trans_leaf, jnp.repeat(down1, 2, axis=0))).astype(bf).astype(f32)
        far_points = jnp.einsum('tpr,tvr->tvp', basis, down0)
        near = jnp.einsum('tnpq,tnvq->tvp', near_blocks[kernel].astype(f32), neighbours)
        results.append((far_points + near).astype(bf))
    return jnp.stack(results, axis=0)
```

```python
import functools

import jax
import jax.numpy as jnp
from jax import lax
from jax.experimental import pallas as pl
from jax.experimental.pallas import tpu as pltpu
from jax.sharding import PartitionSpec as P

REACH = 2
WIN = 2 * REACH + 1
HW = 2
AXES = ("row", "col")
F32 = jnp.float32
BF = jnp.bfloat16
NT = (((1,), (1,)), ((), ()))
LIMIT = 40 * 1024 * 1024

VMEM = pltpu.VMEM
SMEM = pltpu.SMEM


def side_by_side(left, right):
    return jnp.concatenate([left, right], axis=1)


def weights_of(ref, *place):
    return jnp.concatenate([ref[(k,) + place] for k in range(ref.shape[0])], axis=0)


def by_kernel(wide, rank):
    count = wide.shape[1] // rank
    return jnp.concatenate([wide[:, k * rank:(k + 1) * rank] for k in range(count)], axis=0)


def up_body(lsend, psend, vec, basis, ltr, ptr, top, own, sib, cross, fwd, back, low, mid):
    leaves, _, rank = vec.shape
    col = lax.axis_index("col")
    cap0 = lsend.shape[2]
    cap1 = psend.shape[1]
    for t in range(leaves):
        low[t] = jnp.dot(vec[t], basis[t], preferred_element_type=F32).astype(BF)
    for j in range(leaves // 2):
        both = side_by_side(low[2 * j], low[2 * j + 1])
        weights = ltr[2 * j:2 * j + 2].reshape(2 * rank, rank)
        mid[j] = jnp.dot(both, weights, preferred_element_type=F32).astype(BF)
    for i in range(leaves // 8):
        pieces = []
        for half in range(2):
            j = 4 * i + 2 * half
            both = side_by_side(mid[j], mid[j + 1])
            weights = ptr[j:j + 2].reshape(2 * rank, rank)
            pieces.append(jnp.dot(both, weights, preferred_element_type=F32).astype(BF))
        top[i] = side_by_side(*pieces)

    def pack(out, place):
        for c in range(cap0 // 2):
            out[c] = side_by_side(low[lsend[place, 0, 2 * c]], low[lsend[place, 0, 2 * c + 1]])
        for c in range(cap1 // 2):
            out[cap0 // 2 + c] = side_by_side(
                mid[psend[0, 2 * c, place]], mid[psend[0, 2 * c + 1, place]]
            )

    def pack_halo(out, start):
        out[(cap0 + cap1) // 2] = side_by_side(vec[start], vec[start + 1])

    pack(own, REACH)
    pack(fwd, 0)
    pack(back, 4)
    pack(sib, 1 + 2 * col)
    pack_halo(sib, (1 - col) * (leaves - HW))
    pack(cross, 3 - 2 * col)
    pack_halo(cross, col * (leaves - HW))


def up_pass(lsend, psend, vec, basis, ltr, ptr):
    leaves, vecs, rank = vec.shape
    blocks = (lsend.shape[2] + psend.shape[1]) // 2
    shape = lambda n: jax.ShapeDtypeStruct((n, vecs, 2 * rank), BF)
    return pl.pallas_call(
        up_body,
        out_shape=[shape(leaves // 8), shape(blocks), shape(blocks + 1), shape(blocks + 1), shape(blocks), shape(blocks)],
        in_specs=[pl.BlockSpec(memory_space=SMEM)] * 2 + [pl.BlockSpec(memory_space=VMEM)] * 4,
        out_specs=[pl.BlockSpec(memory_space=VMEM)] * 6,
        scratch_shapes=[VMEM((leaves, vecs, rank), BF), VMEM((leaves // 2, vecs, rank), BF)],
        compiler_params=pltpu.CompilerParams(vmem_limit_bytes=LIMIT),
        cost_estimate=pl.CostEstimate(flops=10_000_000, bytes_accessed=3_000_000, transcendentals=0),
        name="up",
    )(lsend, psend, vec, basis, ltr, ptr)


def near_body(offsets, vec, blocks, out, padded):
    step = pl.program_id(0)
    count = blocks.shape[1]
    leaves, vecs, rank = vec.shape

    @pl.when(step == 0)
    def _():
        padded[0:HW] = jnp.zeros((HW, vecs, rank), BF)
        padded[HW:HW + leaves] = vec[...]
        padded[HW + leaves:] = jnp.zeros((HW, vecs, rank), BF)

    for q in range(count):
        t = step * count + q
        total = None
        for n in range(blocks.shape[2]):
            rows = padded[t + HW + offsets[n, t]]
            part = lax.dot_general(rows, weights_of(blocks, q, n), NT, preferred_element_type=F32)
            total = part if total is None else total + part
        out[q] = by_kernel(total, rank)


def near_pass(offsets, vec, blocks, per):
    kernels, leaves, near, rank, _ = blocks.shape
    vecs = vec.shape[1]
    return pl.pallas_call(
        near_body,
        grid=(leaves // per,),
        out_shape=jax.ShapeDtypeStruct((leaves, kernels * vecs, rank), F32),
        in_specs=[
            pl.BlockSpec(memory_space=SMEM),
            pl.BlockSpec(memory_space=VMEM),
            pl.BlockSpec((kernels, per, near, rank, rank), lambda i: (0, i, 0, 0, 0)),
        ],
        out_specs=pl.BlockSpec((per, kernels * vecs, rank), lambda i: (i, 0, 0)),
        scratch_shapes=[VMEM((leaves + 2 * HW, vecs, rank), BF)],
        compiler_params=pltpu.CompilerParams(vmem_limit_bytes=LIMIT),
        cost_estimate=pl.CostEstimate(flops=40_000_000, bytes_accessed=12_000_000, transcendentals=0),
        name="near",
    )(offsets, vec, blocks)


def far_body(llist, plist, offsets, own, sib, cross, fwd, back, leaf, pair, first, last, nears, far0, far1, edge,
             wleaf, wpair, halo):
    step = pl.program_id(0)
    per = leaf.shape[1]
    _, vecs, rank = wleaf.shape
    cap0 = wleaf.shape[0] // WIN
    cap1 = wpair.shape[0] // WIN
    leaves = offsets.shape[1]
    heads = first.shape[1]

    @pl.when(step == 0)
    def _():
        col = lax.axis_index("col")
        place = lax.axis_index("row") * lax.axis_size("col") + col
        last_place = lax.axis_size("row") * lax.axis_size("col") - 1

        def unpack(block, slot):
            for c in range(cap0 // 2):
                row = block[c]
                wleaf[slot * cap0 + 2 * c] = row[:, :rank]
                wleaf[slot * cap0 + 2 * c + 1] = row[:, rank:]
            for c in range(cap1 // 2):
                row = block[cap0 // 2 + c]
                wpair[slot * cap1 + 2 * c] = row[:, :rank]
                wpair[slot * cap1 + 2 * c + 1] = row[:, rank:]

        unpack(own, REACH)
        unpack(fwd, 0)
        unpack(back, 4)
        unpack(sib, 3 - 2 * col)
        unpack(cross, 1 + 2 * col)
        row = sib[(cap0 + cap1) // 2]
        halo[2 - 2 * col] = row[:, :rank]
        halo[3 - 2 * col] = row[:, rank:]
        row = cross[(cap0 + cap1) // 2]
        halo[2 * col] = row[:, :rank]
        halo[2 * col + 1] = row[:, rank:]
        zero = jnp.zeros((HW, vecs, rank), BF)
        halo[2 * HW:] = zero

        @pl.when(place == 0)
        def _():
            halo[0:HW] = zero

        @pl.when(place == last_place)
        def _():
            halo[HW:2 * HW] = zero

        for q in range(heads):
            total = None
            for n in range(first.shape[2]):
                at = q + offsets[n, q]
                rows = halo[jnp.where(at < 0, at + HW, 2 * HW)]
                part = lax.dot_general(rows, weights_of(first, q, n), NT, preferred_element_type=F32)
                total = part if total is None else total + part
            edge[q] = nears[0, q] + by_kernel(total, rank)
            total = None
            t = leaves - heads + q
            for n in range(last.shape[2]):
                at = t + offsets[n, t]
                rows = halo[jnp.where(at >= leaves, at - leaves + HW, 2 * HW)]
                part = lax.dot_general(rows, weights_of(last, q, n), NT, preferred_element_type=F32)
                total = part if total is None else total + part
            edge[heads + q] = nears[1, q] + by_kernel(total, rank)

    for q in range(per):
        t = step * per + q
        total = None
        for m in range(leaf.shape[2]):
            rows = wleaf[llist[m, t]]
            part = lax.dot_general(rows, weights_of(leaf, q, m), NT, preferred_element_type=F32)
            total = part if total is None else total + part
        far0[q] = by_kernel(total, rank)
    for q in range(per // 2):
        t = step * (per // 2) + q
        total = None
        for m in range(pair.shape[2]):
            rows = wpair[plist[m, t]]
            part = lax.dot_general(rows, weights_of(pair, q, m), NT, preferred_element_type=F32)
            total = part if total is None else total + part
        far1[q] = by_kernel(total, rank)


def far_pass(llist, plist, offsets, own, sib, cross, fwd, back, leaf, pair, near_blocks, nears, per, cap0, cap1):
    kernels, leaves, partners, rank, _ = leaf.shape
    vecs = own.shape[1]
    near = near_blocks.shape[2]
    ends = leaves // HW
    whole = pl.BlockSpec(memory_space=VMEM)
    rows = kernels * vecs
    ends_of_near = jnp.stack([nears[:HW], nears[leaves - HW:]])
    return pl.pallas_call(
        far_body,
        grid=(leaves // per,),
        out_shape=[
            jax.ShapeDtypeStruct((leaves, rows, rank), F32),
            jax.ShapeDtypeStruct((leaves // 2, rows, rank), F32),
            jax.ShapeDtypeStruct((2 * HW, rows, rank), F32),
        ],
        in_specs=[pl.BlockSpec(memory_space=SMEM)] * 3 + [whole] * 5 + [
            pl.BlockSpec((kernels, per, partners, rank, rank), lambda i: (0, i, 0, 0, 0)),
            pl.BlockSpec((kernels, per // 2, pair.shape[2], rank, rank), lambda i: (0, i, 0, 0, 0)),
            pl.BlockSpec((kernels, HW, near, rank, rank), lambda i: (0, 0, 0, 0, 0)),
            pl.BlockSpec((kernels, HW, near, rank, rank), lambda i: (0, ends - 1, 0, 0, 0)),
            whole,
        ],
        out_specs=[
            pl.BlockSpec((per, rows, rank), lambda i: (i, 0, 0)),
            pl.BlockSpec((per // 2, rows, rank), lambda i: (i, 0, 0)),
            pl.BlockSpec((2 * HW, rows, rank), lambda i: (0, 0, 0)),
        ],
        scratch_shapes=[
            VMEM((WIN * cap0, vecs, rank), BF),
            VMEM((WIN * cap1, vecs, rank), BF),
            VMEM((3 * HW, vecs, rank), BF),
        ],
        compiler_params=pltpu.CompilerParams(vmem_limit_bytes=LIMIT),
        cost_estimate=pl.CostEstimate(flops=80_000_000, bytes_accessed=18_000_000, transcendentals=0),
        name="far",
    )(llist, plist, offsets, own, sib, cross, fwd, back, leaf, pair, near_blocks, near_blocks, ends_of_near)


def down_body(tlist, tops, coupling, ptr, ltr, basis, far1, far0, nears, edge, out, held):
    step = pl.program_id(0)
    steps = pl.num_programs(0)
    per = coupling.shape[1]
    rank = basis.shape[2]
    vecs = tops.shape[1]
    kernels = coupling.shape[0]

    @pl.when(step == 0)
    def _():
        for i in range(tops.shape[0]):
            row = tops[i]
            held[2 * i] = row[:, :rank]
            held[2 * i + 1] = row[:, rank:]

    for q in range(per):
        i = step * per + q
        total = None
        for m in range(coupling.shape[2]):
            rows = held[tlist[i, m]]
            part = lax.dot_general(rows, weights_of(coupling, q, m), NT, preferred_element_type=F32)
            total = part if total is None else total + part
        down2 = by_kernel(total, rank).astype(BF)
        for a in range(2):
            j = 2 * q + a
            down1 = (far1[j] + lax.dot_general(down2, ptr[j], NT, preferred_element_type=F32)).astype(BF)
            for b in range(2):
                t = 2 * j + b
                down0 = (far0[t] + lax.dot_general(down1, ltr[t], NT, preferred_element_type=F32)).astype(BF)
                points = lax.dot_general(down0, basis[t], NT, preferred_element_type=F32)
                base = nears[t]
                if t < HW:
                    base = jnp.where(step == 0, edge[t], base)
                if t >= 4 * per - HW:
                    base = jnp.where(step == steps - 1, edge[HW + t - (4 * per - HW)], base)
                points = (points + base).astype(BF)
                for k in range(kernels):
                    out[k, t] = points[k * vecs:(k + 1) * vecs]


def down_pass(tlist, tops, coupling, ptr, ltr, basis, far1, far0, nears, edge, per):
    kernels, count, partners, rank, _ = coupling.shape
    vecs = tops.shape[1]
    leaves = basis.shape[0]
    rows = kernels * vecs
    whole = pl.BlockSpec(memory_space=VMEM)
    return pl.pallas_call(
        down_body,
        grid=(count // per,),
        out_shape=jax.ShapeDtypeStruct((kernels, leaves, vecs, rank), BF),
        in_specs=[
            pl.BlockSpec(memory_space=SMEM),
            whole,
            pl.BlockSpec((kernels, per, partners, rank, rank), lambda i: (0, i, 0, 0, 0)),
            pl.BlockSpec((2 * per, rank, rank), lambda i: (i, 0, 0)),
            pl.BlockSpec((4 * per, rank, rank), lambda i: (i, 0, 0)),
            pl.BlockSpec((4 * per, rank, rank), lambda i: (i, 0, 0)),
            pl.BlockSpec((2 * per, rows, rank), lambda i: (i, 0, 0)),
            pl.BlockSpec((4 * per, rows, rank), lambda i: (i, 0, 0)),
            pl.BlockSpec((4 * per, rows, rank), lambda i: (i, 0, 0)),
            whole,
        ],
        out_specs=pl.BlockSpec((kernels, 4 * per, vecs, rank), lambda i: (0, i, 0, 0)),
        scratch_shapes=[VMEM((2 * tops.shape[0], vecs, rank), BF)],
        compiler_params=pltpu.CompilerParams(vmem_limit_bytes=LIMIT),
        cost_estimate=pl.CostEstimate(flops=40_000_000, bytes_accessed=8_000_000, transcendentals=0),
        name="down",
    )(tlist, tops, coupling, ptr, ltr, basis, far1, far0, nears, edge)


def sent(block, pairs):
    return lax.ppermute(block, AXES, pairs)


def on_device(
    vectors,
    leaf_basis,
    leaf_transfer,
    pair_transfer,
    near_blocks,
    near_offset,
    leaf_send,
    leaf_list,
    leaf_coupling,
    pair_send,
    pair_list,
    pair_coupling,
    top_list,
    top_coupling,
):
    devs = lax.axis_size("row") * lax.axis_size("col")
    cap0, cap1 = leaf_send.shape[2], pair_send.shape[2]
    lsend = jnp.transpose(leaf_send, (1, 0, 2))
    psend = jnp.transpose(pair_send, (0, 2, 1))
    offsets = near_offset.T
    llist = leaf_list.T
    plist = pair_list.T
    top, own, sib, cross, fwd, back = up_pass(lsend, psend, vectors, leaf_basis, leaf_transfer, pair_transfer)
    ring = range(devs)
    sib = sent(sib, [(d, d ^ 1) for d in ring])
    cross = sent(cross, [(d, (d + 1 if d % 2 else d - 1) % devs) for d in ring])
    fwd = sent(fwd, [(d, (d + 2) % devs) for d in ring])
    back = sent(back, [(d, (d - 2) % devs) for d in ring])
    tops = lax.all_gather(top, AXES, axis=0, tiled=True)
    nears = near_pass(offsets, vectors, near_blocks, 4)
    far0, far1, edge = far_pass(
        llist, plist, offsets, own, sib, cross, fwd, back, leaf_coupling, pair_coupling, near_blocks, nears, 4, cap0, cap1
    )
    return down_pass(
        top_list, tops, top_coupling, pair_transfer, leaf_transfer, leaf_basis, far1, far0, nears, edge, 2
    )


def solution(mesh):
    placed = P(("groups", "row", "col"))
    behind = P(None, ("groups", "row", "col"))
    return jax.shard_map(
        on_device,
        mesh=mesh,
        in_specs=(
            placed, placed, placed, placed, behind, placed, placed, placed, behind, placed, placed, behind, placed, behind,
        ),
        out_specs=behind,
        check_vma=False,
    )
```

```python
import jax
import jax.numpy as jnp
from jax import lax
from jax.experimental import pallas as pl
from jax.experimental.pallas import tpu as pltpu
from jax.sharding import PartitionSpec as P

REACH = 2
WIN = 2 * REACH + 1
HW = 2
AXES = ("row", "col")
F32 = jnp.float32
BF = jnp.bfloat16
LIMIT = 56 * 1024 * 1024

VMEM = pltpu.VMEM
SMEM = pltpu.SMEM
DMA = pltpu.SemaphoreType.DMA
HERE = pl.BlockSpec(memory_space=pl.ANY)
SCALARS = pl.BlockSpec(memory_space=SMEM)
WHOLE = pl.BlockSpec(memory_space=VMEM)


def dot(left, right):
    return jnp.dot(left, right, preferred_element_type=F32)


def beside(*parts):
    return jnp.concatenate(parts, axis=1)


def above(*parts):
    return jnp.concatenate(parts, axis=0)


def turned(block):
    return block.astype(F32).T.astype(BF)


def row_of_blocks(ref, q):
    kernels, _, partners, _, _ = ref.shape
    return beside(*[above(*[ref[k, q, m] for k in range(kernels)]) for m in range(partners)])


def kernels_beside(tall, rank):
    return beside(*[tall[k * rank:(k + 1) * rank] for k in range(tall.shape[0] // rank)])


def copies(pairs, sems):
    made = [pltpu.make_async_copy(src, dst, sems.at[i]) for i, (src, dst) in enumerate(pairs)]
    for copy in made:
        copy.start()
    return made


def up_body(lsend, psend, vec_h, basis_h, ltr_h, ptr_h, tops, own, sib, cross, fwd, back,
            vec, basis, ltr, ptr, low, mid, sems):
    leaves, vecs, rank = vec.shape
    col = lax.axis_index("col")
    cap0 = lsend.shape[2]
    cap1 = psend.shape[1]
    made = copies([(vec_h, vec), (basis_h, basis), (ltr_h, ltr), (ptr_h, ptr)], sems)
    made[0].wait()
    made[1].wait()
    for t in range(leaves):
        low[t] = dot(vec[t], basis[t]).astype(BF)
    made[2].wait()
    for j in range(leaves // 2):
        mid[j] = dot(
            beside(low[2 * j], low[2 * j + 1]), ltr[2 * j:2 * j + 2].reshape(2 * rank, rank)
        ).astype(BF)
    made[3].wait()
    high = []
    for i in range(leaves // 4):
        high.append(
            dot(beside(mid[2 * i], mid[2 * i + 1]), ptr[2 * i:2 * i + 2].reshape(2 * rank, rank))
        )
    turned_tops = above(*high).T.astype(BF)
    for row in range(tops.shape[0]):
        tops[row] = turned_tops

    def pack(out, place):
        out[0:rank] = turned(above(*[low[lsend[place, 0, c]] for c in range(cap0)]))
        out[rank:rank + vecs] = beside(*[mid[psend[0, c, place]] for c in range(cap1)])

    def pack_halo(out, start):
        out[rank + vecs:] = beside(*[vec[start + h] for h in range(HW)])

    pack(sib, 1 + 2 * col)
    pack_halo(sib, (1 - col) * (leaves - HW))
    pack(cross, 3 - 2 * col)
    pack_halo(cross, col * (leaves - HW))
    pack(fwd, 0)
    pack(back, 4)
    pack(own, REACH)


def up_pass(lsend, psend, vec, basis, ltr, ptr, rows):
    leaves, vecs, rank = vec.shape
    wide = lsend.shape[2] * vecs
    shape = lambda *n: jax.ShapeDtypeStruct(n, BF)
    short, tall = shape(rank + vecs, wide), shape(rank + 2 * vecs, wide)
    return pl.pallas_call(
        up_body,
        out_shape=[shape(rows, rank, leaves // 4 * vecs), short, tall, tall, short, short],
        in_specs=[SCALARS] * 2 + [HERE] * 4,
        out_specs=[WHOLE] * 6,
        scratch_shapes=[
            VMEM(vec.shape, BF), VMEM(basis.shape, BF), VMEM(ltr.shape, BF), VMEM(ptr.shape, BF),
            VMEM((leaves, vecs, rank), BF), VMEM((leaves // 2, vecs, rank), BF), DMA((4,)),
        ],
        compiler_params=pltpu.CompilerParams(vmem_limit_bytes=LIMIT),
        cost_estimate=pl.CostEstimate(flops=10_000_000, bytes_accessed=3_000_000, transcendentals=0),
        name="up",
    )(lsend, psend, vec, basis, ltr, ptr)


def near_body(offsets, vec_h, blocks_h, out, vec, blocks, padded, sems, chunk_sems):
    leaves, vecs, rank = vec.shape
    kernels = blocks.shape[0]
    chunks = chunk_sems.shape[0]
    per = leaves // chunks

    def chunk(c):
        part = pl.ds(c * per, per)
        return pltpu.make_async_copy(blocks_h.at[:, part], blocks.at[:, part], chunk_sems.at[c])

    made = copies([(vec_h, vec)], sems)
    for c in range(chunks):
        chunk(c).start()
    made[0].wait()
    zero = jnp.zeros((HW, rank, vecs), BF)
    padded[0:HW] = zero
    padded[HW + leaves:] = zero
    group = 128 // vecs
    for g in range(leaves // group):
        wide = turned(above(*[vec[g * group + c] for c in range(group)]))
        for c in range(group):
            padded[HW + g * group + c] = wide[:, c * vecs:(c + 1) * vecs]

    def body(c, _):
        chunk(c).wait()
        for q in range(per):
            t = c * per + q
            rows = above(*[padded[t + HW + offsets[n, t]] for n in range(blocks.shape[2])])
            out[t] = kernels_beside(dot(row_of_blocks(blocks, t), rows), rank)
        return 0

    lax.fori_loop(0, chunks, body, 0)


def near_pass(offsets, vec, blocks, chunks):
    kernels, leaves, near, rank, _ = blocks.shape
    vecs = vec.shape[1]
    return pl.pallas_call(
        near_body,
        out_shape=jax.ShapeDtypeStruct((leaves, rank, kernels * vecs), F32),
        in_specs=[SCALARS, HERE, HERE],
        out_specs=WHOLE,
        scratch_shapes=[
            VMEM(vec.shape, BF), VMEM(blocks.shape, BF), VMEM((leaves + 2 * HW, rank, vecs), BF), DMA((1,)), DMA((chunks,)),
        ],
        compiler_params=pltpu.CompilerParams(vmem_limit_bytes=LIMIT),
        cost_estimate=pl.CostEstimate(flops=40_000_000, bytes_accessed=12_000_000, transcendentals=0),
        name="near",
    )(offsets, vec, blocks)


def far_body(llist, plist, offsets, own_h, sib_h, cross_h, fwd_h, back_h, leaf_h, pair_h, near_h, far0, far1, edge,
             own, sib, cross, fwd, back, leaf, pair, first, last, wleaf, wpair, halo, sems, leaf_sems, pair_sems):
    leaves = offsets.shape[1]
    _, rank, vecs = wleaf.shape
    cap0 = wleaf.shape[0] // WIN
    cap1 = wpair.shape[0] // WIN
    heads = first.shape[1]
    chunks = leaf_sems.shape[0]
    per = leaves // chunks
    col = lax.axis_index("col")
    place = lax.axis_index("row") * lax.axis_size("col") + col
    last_place = lax.axis_size("row") * lax.axis_size("col") - 1

    def leaf_chunk(c):
        part = pl.ds(c * per, per)
        return pltpu.make_async_copy(leaf_h.at[:, part], leaf.at[:, part], leaf_sems.at[c])

    def pair_chunk(c):
        part = pl.ds(c * (per // 2), per // 2)
        return pltpu.make_async_copy(pair_h.at[:, part], pair.at[:, part], pair_sems.at[c])

    made = copies(
        [
            (own_h, own), (sib_h, sib), (cross_h, cross), (fwd_h, fwd), (back_h, back),
            (near_h.at[:, pl.ds(0, heads)], first), (near_h.at[:, pl.ds(leaves - heads, heads)], last),
        ],
        sems,
    )
    for c in range(chunks):
        leaf_chunk(c).start()
        pair_chunk(c).start()
    for copy in made:
        copy.wait()

    def unpack(block, slot):
        for c in range(cap0):
            wleaf[slot * cap0 + c] = block[0:rank, c * vecs:(c + 1) * vecs]
        both = turned(block[rank:rank + vecs, :])
        for c in range(cap1):
            wpair[slot * cap1 + c] = both[c * rank:(c + 1) * rank]

    unpack(own, REACH)
    unpack(fwd, 0)
    unpack(back, 4)
    unpack(sib, 3 - 2 * col)
    unpack(cross, 1 + 2 * col)
    zero = jnp.zeros((rank, vecs), BF)
    for block, slot in ((sib, HW - HW * col), (cross, HW * col)):
        both = turned(block[rank + vecs:, :])
        outside = (place == 0) & (slot == 0) | (place == last_place) & (slot == HW)
        for h in range(HW):
            halo[slot + h] = jnp.where(outside, zero, both[h * rank:(h + 1) * rank])
    halo[2 * HW] = zero

    for q in range(heads):
        spots = [q + offsets[n, q] for n in range(first.shape[2])]
        rows = above(*[halo[jnp.where(at < 0, at + HW, 2 * HW)] for at in spots])
        edge[q] = kernels_beside(dot(row_of_blocks(first, q), rows), rank)
        t = leaves - heads + q
        spots = [t + offsets[n, t] for n in range(last.shape[2])]
        rows = above(*[halo[jnp.where(at >= leaves, at - leaves + HW, 2 * HW)] for at in spots])
        edge[heads + q] = kernels_beside(dot(row_of_blocks(last, q), rows), rank)

    def body(c, _):
        leaf_chunk(c).wait()
        pair_chunk(c).wait()
        for q in range(per):
            t = c * per + q
            rows = above(*[wleaf[llist[m, t]] for m in range(leaf.shape[2])])
            far0[t] = kernels_beside(dot(row_of_blocks(leaf, t), rows), rank)
        for q in range(per // 2):
            j = c * (per // 2) + q
            rows = above(*[wpair[plist[m, j]] for m in range(pair.shape[2])])
            far1[j] = kernels_beside(dot(row_of_blocks(pair, j), rows), rank)
        return 0

    lax.fori_loop(0, chunks, body, 0)


def far_pass(llist, plist, offsets, own, sib, cross, fwd, back, leaf, pair, near, chunks, cap0, cap1):
    kernels, leaves, partners, rank, _ = leaf.shape
    vecs = own.shape[0] - rank
    lanes = kernels * vecs
    ends = (kernels, HW) + near.shape[2:]
    return pl.pallas_call(
        far_body,
        out_shape=[
            jax.ShapeDtypeStruct((leaves, rank, lanes), F32),
            jax.ShapeDtypeStruct((leaves // 2, rank, lanes), F32),
            jax.ShapeDtypeStruct((2 * HW, rank, lanes), F32),
        ],
        in_specs=[SCALARS] * 3 + [HERE] * 8,
        out_specs=[WHOLE] * 3,
        scratch_shapes=[VMEM(x.shape, BF) for x in (own, sib, cross, fwd, back, leaf, pair)] + [
            VMEM(ends, BF), VMEM(ends, BF),
            VMEM((WIN * cap0, rank, vecs), BF), VMEM((WIN * cap1, rank, vecs), BF), VMEM((2 * HW + 1, rank, vecs), BF),
            DMA((7,)), DMA((chunks,)), DMA((chunks,)),
        ],
        compiler_params=pltpu.CompilerParams(vmem_limit_bytes=LIMIT),
        cost_estimate=pl.CostEstimate(flops=80_000_000, bytes_accessed=18_000_000, transcendentals=0),
        name="far",
    )(llist, plist, offsets, own, sib, cross, fwd, back, leaf, pair, near)


def down_body(tlist, mine_h, theirs_h, coupling_h, ptr_h, ltr_h, basis_h, far1_h, far0_h, near_h, edge_h, out,
              tops, coupling, ptr, ltr, basis, far1, far0, near, edge, sems, top_sems):
    kernels, count, partners, rank, _ = coupling.shape
    leaves = basis.shape[0]
    vecs = edge.shape[2] // kernels
    per_dev = tops.shape[3] // vecs
    col = lax.axis_index("col")
    made = copies([(mine_h, tops.at[:, col]), (theirs_h, tops.at[:, 1 - col])], sems)
    chunk = [
        pltpu.make_async_copy(coupling_h.at[:, pl.ds(i, 1)], coupling.at[:, pl.ds(i, 1)], top_sems.at[i])
        for i in range(count)
    ]
    for copy in chunk:
        copy.start()
    rest = copies(
        [
            (ptr_h, ptr), (far1_h, far1), (ltr_h, ltr), (far0_h, far0), (basis_h, basis), (near_h, near), (edge_h, edge),
        ],
        sems.at[pl.ds(2, 7)],
    )
    for copy in made:
        copy.wait()

    def partner(e):
        d = e // per_dev
        block = tops[d // 2, d % 2].astype(F32)
        shift = (per_dev - e % per_dev) % per_dev * vecs
        return pltpu.roll(block, shift, 1).astype(BF)

    down2 = []
    for i in range(count):
        chunk[i].wait()
        rows = above(*[partner(tlist[i, m]) for m in range(partners)])
        total = dot(row_of_blocks(coupling, i), rows)[:, :vecs]
        down2.append(kernels_beside(total, rank).astype(BF))
    rest[0].wait()
    rest[1].wait()
    down1 = []
    for i in range(count):
        both = dot(ptr[2 * i:2 * i + 2].reshape(2 * rank, rank), down2[i])
        for a in range(2):
            down1.append((far1[2 * i + a] + both[a * rank:(a + 1) * rank]).astype(BF))
    rest[2].wait()
    rest[3].wait()
    down0 = []
    for j in range(2 * count):
        both = dot(ltr[2 * j:2 * j + 2].reshape(2 * rank, rank), down1[j])
        for a in range(2):
            down0.append((far0[2 * j + a] + both[a * rank:(a + 1) * rank]).astype(BF))
    for copy in rest[4:]:
        copy.wait()
    for t in range(leaves):
        points = dot(basis[t], down0[t]) + near[t]
        if t < HW:
            points = points + edge[t]
        if t >= leaves - HW:
            points = points + edge[HW + t - (leaves - HW)]
        points = points.T.astype(BF)
        for k in range(kernels):
            out[k, t] = points[k * vecs:(k + 1) * vecs]


def down_pass(tlist, mine, theirs, coupling, ptr, ltr, basis, far1, far0, near, edge):
    kernels, count, partners, rank, _ = coupling.shape
    leaves = basis.shape[0]
    vecs = near.shape[2] // kernels
    rows, _, wide = mine.shape
    return pl.pallas_call(
        down_body,
        out_shape=jax.ShapeDtypeStruct((kernels, leaves, vecs, rank), BF),
        in_specs=[SCALARS] + [HERE] * 10,
        out_specs=WHOLE,
        scratch_shapes=[VMEM((rows, 2, rank, wide), BF)]
        + [VMEM(x.shape, x.dtype) for x in (coupling, ptr, ltr, basis, far1, far0, near, edge)]
        + [DMA((9,)), DMA((count,))],
        compiler_params=pltpu.CompilerParams(vmem_limit_bytes=LIMIT),
        cost_estimate=pl.CostEstimate(flops=40_000_000, bytes_accessed=8_000_000, transcendentals=0),
        name="down",
    )(tlist, mine, theirs, coupling, ptr, ltr, basis, far1, far0, near, edge)


def on_device(
    vectors,
    leaf_basis,
    leaf_transfer,
    pair_transfer,
    near_blocks,
    near_offset,
    leaf_send,
    leaf_list,
    leaf_coupling,
    pair_send,
    pair_list,
    pair_coupling,
    top_list,
    top_coupling,
):
    rows = lax.axis_size("row")
    devs = rows * lax.axis_size("col")
    cap0, cap1 = leaf_send.shape[2], pair_send.shape[2]
    lsend = jnp.transpose(leaf_send, (1, 0, 2))
    psend = jnp.transpose(pair_send, (0, 2, 1))
    offsets = near_offset.T
    llist = leaf_list.T
    plist = pair_list.T
    tops, own, sib, cross, fwd, back = up_pass(
        lsend, psend, vectors, leaf_basis, leaf_transfer, pair_transfer, rows
    )
    ring = range(devs)
    sibling = [(d, d ^ 1) for d in ring]
    sib = lax.ppermute(sib, AXES, sibling)
    cross = lax.ppermute(cross, AXES, [(d, (d + 1 if d % 2 else d - 1) % devs) for d in ring])
    fwd = lax.ppermute(fwd, AXES, [(d, (d + 2) % devs) for d in ring])
    back = lax.ppermute(back, AXES, [(d, (d - 2) % devs) for d in ring])
    mine = lax.all_to_all(tops, "row", split_axis=0, concat_axis=0)
    theirs = lax.ppermute(mine, AXES, sibling)
    near = near_pass(offsets, vectors, near_blocks, 8)
    far0, far1, edge = far_pass(
        llist, plist, offsets, own, sib, cross, fwd, back, leaf_coupling, pair_coupling, near_blocks, 8, cap0, cap1
    )
    return down_pass(
        top_list, mine, theirs, top_coupling, pair_transfer, leaf_transfer, leaf_basis, far1, far0, near, edge
    )


def solution(mesh):
    placed = P(("groups", "row", "col"))
    behind = P(None, ("groups", "row", "col"))
    return jax.shard_map(
        on_device,
        mesh=mesh,
        in_specs=(
            placed, placed, placed, placed, behind, placed, placed, placed, behind, placed, placed, behind, placed, behind,
        ),
        out_specs=behind,
        check_vma=False,
    )
```

```python
import functools

import jax
import jax.numpy as jnp
from jax import lax
from jax.experimental import pallas as pl
from jax.experimental.pallas import tpu as pltpu
from jax.sharding import PartitionSpec as P

REACH = 2
WIN = 2 * REACH + 1
HW = 2
AXES = ("row", "col")
F32 = jnp.float32
BF = jnp.bfloat16
LIMIT = 56 * 1024 * 1024

VMEM = pltpu.VMEM
SMEM = pltpu.SMEM
DMA = pltpu.SemaphoreType.DMA
HERE = pl.BlockSpec(memory_space=pl.ANY)
SCALARS = pl.BlockSpec(memory_space=SMEM)
WHOLE = pl.BlockSpec(memory_space=VMEM)


def dot(left, right):
    return jnp.dot(left, right, preferred_element_type=F32)


def beside(*parts):
    return jnp.concatenate(parts, axis=1)


def above(*parts):
    return jnp.concatenate(parts, axis=0)


def dot_t(left, right):
    return lax.dot_general(left, right, (((1,), (1,)), ((), ())), preferred_element_type=F32)


def row_of_blocks(ref, q):
    kernels, _, partners, _, _ = ref.shape
    return beside(*[above(*[ref[k, q, m] for k in range(kernels)]) for m in range(partners)])


def by_kernel(wide, rank):
    return above(*[wide[:, k * rank:(k + 1) * rank] for k in range(wide.shape[1] // rank)])


def copies(pairs, sems):
    made = [pltpu.make_async_copy(src, dst, sems.at[i]) for i, (src, dst) in enumerate(pairs)]
    for copy in made:
        copy.start()
    return made


def chunk_of(src, dst, sems, size):
    def chunk(c):
        part = pl.ds(c * size, size)
        return pltpu.make_async_copy(src.at[:, part], dst.at[:, part], sems.at[c])

    return chunk


def split(row, ref, at):
    rank = row.shape[1] // 2
    ref[at] = row[:, :rank]
    ref[at + 1] = row[:, rank:]


def call(body, name, scalars, arrays, out_shape, out_specs, scratch, cost):
    return pl.pallas_call(
        body,
        out_shape=out_shape,
        in_specs=[SCALARS] * len(scalars) + [HERE] * len(arrays),
        out_specs=out_specs,
        scratch_shapes=scratch,
        compiler_params=pltpu.CompilerParams(vmem_limit_bytes=LIMIT),
        cost_estimate=pl.CostEstimate(flops=cost[0], bytes_accessed=cost[1], transcendentals=0),
        name=name,
    )(*scalars, *arrays)


def like(x):
    return VMEM(x.shape, x.dtype)


def joined_shape(piece):
    return jax.ShapeDtypeStruct((2 * piece.shape[0],) + piece.shape[1:], piece.dtype)


def join(first_h, second_h, out_h, sems):
    count = first_h.shape[0]
    return copies([(first_h, out_h.at[pl.ds(0, count)]), (second_h, out_h.at[pl.ds(count, count)])], sems)


def up_body(lsend, psend, vec_h, basis_h, ltr_h, ptr_h, tops, own, sib, cross, fwd, back,
            vec, basis, ltr, ptr, low, mid, sems):
    leaves, vecs, rank = vec.shape
    col = lax.axis_index("col")
    cap0 = lsend.shape[2]
    cap1 = psend.shape[1]
    made = copies([(vec_h, vec), (basis_h, basis), (ltr_h, ltr), (ptr_h, ptr)], sems)
    made[0].wait()
    made[1].wait()
    for t in range(leaves):
        low[t] = dot(vec[t], basis[t]).astype(BF)
    made[2].wait()
    for j in range(leaves // 2):
        mid[j] = dot(
            beside(low[2 * j], low[2 * j + 1]), ltr[2 * j:2 * j + 2].reshape(2 * rank, rank)
        ).astype(BF)
    made[3].wait()
    high = []
    for i in range(leaves // 4):
        high.append(
            dot(beside(mid[2 * i], mid[2 * i + 1]), ptr[2 * i:2 * i + 2].reshape(2 * rank, rank)).astype(BF)
        )
    for i in range(leaves // 8):
        tops[0, i] = beside(high[2 * i], high[2 * i + 1])

    def pack(out, place):
        for c in range(cap0 // 2):
            out[c] = beside(low[lsend[place, 0, 2 * c]], low[lsend[place, 0, 2 * c + 1]])
        for c in range(cap1 // 2):
            out[cap0 // 2 + c] = beside(mid[psend[0, 2 * c, place]], mid[psend[0, 2 * c + 1, place]])

    def pack_halo(out, start):
        out[(cap0 + cap1) // 2] = beside(vec[start], vec[start + 1])

    pack(sib, 1 + 2 * col)
    pack_halo(sib, (1 - col) * (leaves - HW))
    pack(cross, 3 - 2 * col)
    pack_halo(cross, col * (leaves - HW))
    pack(fwd, 0)
    pack(back, 4)
    pack(own, REACH)


def up_pass(lsend, psend, vec, basis, ltr, ptr):
    leaves, vecs, rank = vec.shape
    count = (lsend.shape[2] + psend.shape[1]) // 2
    shape = lambda *n: jax.ShapeDtypeStruct(n + (vecs, 2 * rank), BF)
    return call(
        up_body, "up", (lsend, psend), (vec, basis, ltr, ptr),
        [shape(1, leaves // 8), shape(count), shape(count + 1), shape(count + 1), shape(count), shape(count)],
        [WHOLE] * 6,
        [
            like(vec), like(basis), like(ltr), like(ptr),
            VMEM((leaves, vecs, rank), BF), VMEM((leaves // 2, vecs, rank), BF), DMA((4,)),
        ],
        (10_000_000, 3_000_000),
    )


def near_body(start, offsets, vec_h, blocks_h, held_h, got_h, out, both_h, vec, blocks, padded, sems, chunk_sems, join_sems):
    leaves, vecs, rank = vec.shape
    half = blocks.shape[1]
    chunks = chunk_sems.shape[0]
    per = half // chunks
    chunk = chunk_of(blocks_h.at[:, pl.ds(start, half)], blocks, chunk_sems, per)
    joining = join(held_h, got_h, both_h, join_sems)
    made = copies([(vec_h, padded.at[pl.ds(HW, leaves)])], sems)
    for c in range(chunks):
        chunk(c).start()
    zero = jnp.zeros((HW, vecs, rank), BF)
    padded[0:HW] = zero
    padded[HW + leaves:] = zero
    made[0].wait()

    def body(c, _):
        chunk(c).wait()
        for q in range(per):
            t = c * per + q
            rows = beside(*[padded[start + t + HW + offsets[n, start + t]] for n in range(blocks.shape[2])])
            out[t] = by_kernel(dot_t(rows, row_of_blocks(blocks, t)), rank)
        return 0

    lax.fori_loop(0, chunks, body, 0)
    for copy in joining:
        copy.wait()


def near_pass(offsets, vec, blocks, held, got, half, chunks):
    kernels, leaves, near, rank, _ = blocks.shape
    vecs = vec.shape[1]
    count = leaves // 2
    return call(
        functools.partial(near_body, half * count), "near%d" % half, (offsets,), (vec, blocks, held, got),
        [jax.ShapeDtypeStruct((count, kernels * vecs, rank), F32), joined_shape(held)],
        [WHOLE, HERE],
        [
            like(vec), VMEM((kernels, count) + blocks.shape[2:], BF), VMEM((leaves + 2 * HW, vecs, rank), BF),
            DMA((1,)), DMA((chunks,)), DMA((2,)),
        ],
        (20_000_000, 6_000_000),
    )


def leaf_body(llist, own_h, sib_h, cross_h, fwd_h, back_h, leaf_h, held_h, got_h, far0, both_h,
              own, sib, cross, fwd, back, leaf, window, sems, chunk_sems, join_sems):
    _, vecs, rank = window.shape
    cap0 = window.shape[0] // WIN
    chunks = chunk_sems.shape[0]
    per = leaf.shape[1] // chunks
    col = lax.axis_index("col")
    joining = join(held_h, got_h, both_h, join_sems)
    made = copies([(own_h, own), (sib_h, sib), (cross_h, cross), (fwd_h, fwd), (back_h, back)], sems)
    chunk = chunk_of(leaf_h, leaf, chunk_sems, per)
    for c in range(chunks):
        chunk(c).start()
    for copy in made:
        copy.wait()
    for block, slot in ((own, REACH), (fwd, 0), (back, 4), (sib, 3 - 2 * col), (cross, 1 + 2 * col)):
        for c in range(cap0 // 2):
            split(block[c], window, slot * cap0 + 2 * c)

    def body(c, _):
        chunk(c).wait()
        for q in range(per):
            t = c * per + q
            rows = beside(*[window[llist[m, t]] for m in range(leaf.shape[2])])
            far0[t] = by_kernel(dot_t(rows, row_of_blocks(leaf, t)), rank)
        return 0

    lax.fori_loop(0, chunks, body, 0)
    for copy in joining:
        copy.wait()


def leaf_pass(llist, own, sib, cross, fwd, back, leaf, held, got, chunks, cap0):
    kernels, leaves, partners, rank, _ = leaf.shape
    vecs = own.shape[1]
    return call(
        leaf_body, "leaf", (llist,), (own, sib, cross, fwd, back, leaf, held, got),
        [jax.ShapeDtypeStruct((leaves, kernels * vecs, rank), F32), joined_shape(held)],
        [WHOLE, HERE],
        [like(x) for x in (own, sib, cross, fwd, back, leaf)]
        + [VMEM((WIN * cap0, vecs, rank), BF), DMA((5,)), DMA((chunks,)), DMA((2,))],
        (50_000_000, 9_000_000),
    )


def pair_body(plist, offsets, own_h, sib_h, cross_h, fwd_h, back_h, pair_h, near_h, far1, edge,
              own, sib, cross, fwd, back, pair, first, last, window, halo, sems, chunk_sems):
    leaves = offsets.shape[1]
    _, vecs, rank = window.shape
    cap1 = window.shape[0] // WIN
    base = own.shape[0] - cap1 // 2
    heads = first.shape[1]
    chunks = chunk_sems.shape[0]
    per = pair.shape[1] // chunks
    col = lax.axis_index("col")
    place = lax.axis_index("row") * lax.axis_size("col") + col
    last_place = lax.axis_size("row") * lax.axis_size("col") - 1
    made = copies(
        [
            (own_h, own), (sib_h, sib), (cross_h, cross), (fwd_h, fwd), (back_h, back),
            (near_h.at[:, pl.ds(0, heads)], first), (near_h.at[:, pl.ds(leaves - heads, heads)], last),
        ],
        sems,
    )
    chunk = chunk_of(pair_h, pair, chunk_sems, per)
    for c in range(chunks):
        chunk(c).start()
    for copy in made:
        copy.wait()
    for block, slot in ((own, REACH), (fwd, 0), (back, 4), (sib, 3 - 2 * col), (cross, 1 + 2 * col)):
        for c in range(cap1 // 2):
            split(block[base + c], window, slot * cap1 + 2 * c)
    zero = jnp.zeros((vecs, rank), BF)
    for block, slot in ((sib, HW - HW * col), (cross, HW * col)):
        row = block[base + cap1 // 2]
        outside = (place == 0) & (slot == 0) | (place == last_place) & (slot == HW)
        split(jnp.where(outside, jnp.zeros_like(row), row), halo, slot)
    halo[2 * HW] = zero

    for q in range(heads):
        spots = [q + offsets[n, q] for n in range(first.shape[2])]
        rows = beside(*[halo[jnp.where(at < 0, at + HW, 2 * HW)] for at in spots])
        edge[q] = by_kernel(dot_t(rows, row_of_blocks(first, q)), rank)
        t = leaves - heads + q
        spots = [t + offsets[n, t] for n in range(last.shape[2])]
        rows = beside(*[halo[jnp.where(at >= leaves, at - leaves + HW, 2 * HW)] for at in spots])
        edge[heads + q] = by_kernel(dot_t(rows, row_of_blocks(last, q)), rank)

    def body(c, _):
        chunk(c).wait()
        for q in range(per):
            j = c * per + q
            rows = beside(*[window[plist[m, j]] for m in range(pair.shape[2])])
            far1[j] = by_kernel(dot_t(rows, row_of_blocks(pair, j)), rank)
        return 0

    lax.fori_loop(0, chunks, body, 0)


def pair_pass(plist, offsets, own, sib, cross, fwd, back, pair, near, chunks, cap1):
    kernels, pairs, partners, rank, _ = pair.shape
    vecs = own.shape[1]
    ends = (kernels, HW) + near.shape[2:]
    return call(
        pair_body, "pair", (plist, offsets), (own, sib, cross, fwd, back, pair, near),
        [
            jax.ShapeDtypeStruct((pairs, kernels * vecs, rank), F32),
            jax.ShapeDtypeStruct((2 * HW, kernels * vecs, rank), F32),
        ],
        [WHOLE] * 2,
        [like(x) for x in (own, sib, cross, fwd, back, pair)] + [
            VMEM(ends, BF), VMEM(ends, BF),
            VMEM((WIN * cap1, vecs, rank), BF), VMEM((2 * HW + 1, vecs, rank), BF), DMA((7,)), DMA((chunks,)),
        ],
        (30_000_000, 5_000_000),
    )


def down_body(offs, tlist, mine_h, theirs_h, coupling_h, ptr_h, ltr_h, basis_h, far1_h, far0_h, near0_h, near1_h, edge_h, out,
              mine, theirs, coupling, ptr, ltr, basis, far1, far0, near, edge, tops, sems, top_sems):
    kernels, count, partners, rank, _ = coupling.shape
    leaves, vecs, _ = near.shape
    vecs //= kernels
    half = leaves // 2
    col = lax.axis_index("col")
    row = lax.axis_index("row")
    made = copies([(mine_h, mine), (theirs_h, theirs)], sems)
    chunk = chunk_of(coupling_h, coupling, top_sems, 1)
    for i in range(count):
        chunk(i).start()
    rest = copies(
        [
            (ptr_h, ptr), (far1_h, far1), (ltr_h, ltr), (far0_h, far0), (basis_h, basis),
            (near0_h, near.at[pl.ds(0, half)]), (near1_h, near.at[pl.ds(half, half)]), (edge_h, edge),
        ],
        sems.at[pl.ds(2, 8)],
    )
    for copy in made:
        copy.wait()
    for block, side in ((mine, col), (theirs, 1 - col)):
        for s, off in enumerate(offs):
            device = (row ^ off) * 2 + side
            for i in range(block.shape[1]):
                split(block[s, i], tops, device * count + 2 * i)

    down2 = []
    for i in range(count):
        chunk(i).wait()
        rows = beside(*[tops[tlist[i, m]] for m in range(partners)])
        down2.append(by_kernel(dot_t(rows, row_of_blocks(coupling, i)), rank).astype(BF))
    rest[0].wait()
    rest[1].wait()
    down1 = []
    for j in range(2 * count):
        down1.append((far1[j] + dot_t(down2[j // 2], ptr[j])).astype(BF))
    rest[2].wait()
    rest[3].wait()
    down0 = []
    for t in range(leaves):
        down0.append((far0[t] + dot_t(down1[t // 2], ltr[t])).astype(BF))
    for copy in rest[4:]:
        copy.wait()
    for t in range(leaves):
        points = dot_t(down0[t], basis[t]) + near[t]
        if t < HW:
            points = points + edge[t]
        if t >= leaves - HW:
            points = points + edge[HW + t - (leaves - HW)]
        points = points.astype(BF)
        for k in range(kernels):
            out[k, t] = points[k * vecs:(k + 1) * vecs]


def down_pass(offs, tlist, mine, theirs, coupling, ptr, ltr, basis, far1, far0, near0, near1, edge):
    kernels, count, partners, rank, _ = coupling.shape
    leaves = basis.shape[0]
    rows, _, vecs, _ = mine.shape
    return call(
        functools.partial(down_body, offs), "down", (tlist,),
        (mine, theirs, coupling, ptr, ltr, basis, far1, far0, near0, near1, edge),
        jax.ShapeDtypeStruct((kernels, leaves, vecs, rank), BF),
        WHOLE,
        [like(x) for x in (mine, theirs, coupling, ptr, ltr, basis, far1, far0)]
        + [VMEM((leaves,) + near0.shape[1:], F32), like(edge), VMEM((2 * rows * count, vecs, rank), BF), DMA((10,)), DMA((count,))],
        (40_000_000, 8_000_000),
    )


def on_device(
    vectors,
    leaf_basis,
    leaf_transfer,
    pair_transfer,
    near_blocks,
    near_offset,
    leaf_send,
    leaf_list,
    leaf_coupling,
    pair_send,
    pair_list,
    pair_coupling,
    top_list,
    top_coupling,
):
    rows = lax.axis_size("row")
    devs = rows * lax.axis_size("col")
    cap0, cap1 = leaf_send.shape[2], pair_send.shape[2]
    lsend = jnp.transpose(leaf_send, (1, 0, 2))
    psend = jnp.transpose(pair_send, (0, 2, 1))
    offsets = near_offset.T
    llist = leaf_list.T
    plist = pair_list.T
    held, own, sib, cross, fwd, back = up_pass(lsend, psend, vectors, leaf_basis, leaf_transfer, pair_transfer)
    ring = range(devs)
    sibling = [(d, d ^ 1) for d in ring]

    masks = []
    while rows >> (len(masks) + 1):
        masks.append(rows >> (len(masks) + 1))
    offs = [0]
    for mask in masks:
        offs = offs + [off ^ mask for off in offs]

    def exchanged(piece, mask):
        return lax.ppermute(piece, "row", [(r, r ^ mask) for r in range(rows)])

    for mask in masks[:-3]:
        held = jnp.concatenate([held, exchanged(held, mask)], axis=0)
    got = exchanged(held, masks[-3])
    sib = lax.ppermute(sib, AXES, sibling)
    cross = lax.ppermute(cross, AXES, [(d, (d + 1 if d % 2 else d - 1) % devs) for d in ring])
    fwd = lax.ppermute(fwd, AXES, [(d, (d + 2) % devs) for d in ring])
    back = lax.ppermute(back, AXES, [(d, (d - 2) % devs) for d in ring])
    near0, held = near_pass(offsets, vectors, near_blocks, held, got, 0, 2)
    got = exchanged(held, masks[-2])
    near1, held = near_pass(offsets, vectors, near_blocks, held, got, 1, 2)
    got = exchanged(held, masks[-1])
    far0, mine = leaf_pass(llist, own, sib, cross, fwd, back, leaf_coupling, held, got, 4, cap0)
    theirs = lax.ppermute(mine, AXES, sibling)
    far1, edge = pair_pass(plist, offsets, own, sib, cross, fwd, back, pair_coupling, near_blocks, 2, cap1)
    return down_pass(
        offs, top_list, mine, theirs, top_coupling, pair_transfer, leaf_transfer, leaf_basis, far1, far0, near0, near1, edge
    )


def solution(mesh):
    placed = P(("groups", "row", "col"))
    behind = P(None, ("groups", "row", "col"))
    return jax.shard_map(
        on_device,
        mesh=mesh,
        in_specs=(
            placed, placed, placed, placed, behind, placed, placed, placed, behind, placed, placed, behind, placed, behind,
        ),
        out_specs=behind,
        check_vma=False,
    )
```

```python
import jax
import jax.numpy as jnp
from jax import lax
from jax.experimental import pallas as pl
from jax.experimental.pallas import tpu as pltpu
from jax.sharding import PartitionSpec as P

REACH = 2
WIN = 2 * REACH + 1
HW = 2
AXES = ("row", "col")
F32 = jnp.float32
BF = jnp.bfloat16
LIMIT = 56 * 1024 * 1024

VMEM = pltpu.VMEM
SMEM = pltpu.SMEM
DMA = pltpu.SemaphoreType.DMA
FIXED = pl.BlockSpec(memory_space=pltpu.HBM)
WHOLE = pl.BlockSpec(memory_space=VMEM)


def dot(left, right):
    return jnp.dot(left, right, preferred_element_type=F32)


def beside(*parts):
    return jnp.concatenate(parts, axis=1)


def above(*parts):
    return jnp.concatenate(parts, axis=0)


def dot_t(left, right):
    return lax.dot_general(left, right, (((1,), (1,)), ((), ())), preferred_element_type=F32)


def row_of_blocks(ref, q):
    kernels, _, partners, _, _ = ref.shape
    return beside(*[above(*[ref[k, q, m] for k in range(kernels)]) for m in range(partners)])


def by_kernel(wide, rank):
    return above(*[wide[:, k * rank:(k + 1) * rank] for k in range(wide.shape[1] // rank)])


def copies(pairs, sems):
    made = [pltpu.make_async_copy(src, dst, sems.at[i]) for i, (src, dst) in enumerate(pairs)]
    for copy in made:
        copy.start()
    return made


def chunk_of(src, dst, sems, size):
    def chunk(c):
        part = pl.ds(c * size, size)
        return pltpu.make_async_copy(src.at[:, part], dst.at[:, part], sems.at[c])

    return chunk


def split(row, ref, at):
    rank = row.shape[1] // 2
    ref[at] = row[:, :rank]
    ref[at + 1] = row[:, rank:]


def call(body, name, params, arrays, out_shape, out_specs, scratch, cost, limit=LIMIT):
    return pl.pallas_call(
        body,
        out_shape=out_shape,
        in_specs=[FIXED] * len(params) + [WHOLE] * len(arrays),
        out_specs=out_specs,
        scratch_shapes=scratch,
        compiler_params=pltpu.CompilerParams(vmem_limit_bytes=limit),
        cost_estimate=pl.CostEstimate(flops=cost[0], bytes_accessed=cost[1], transcendentals=0),
        name=name,
    )(*params, *arrays)


def like(x):
    return VMEM(x.shape, x.dtype)


def held(x):
    return SMEM(x.shape, x.dtype)


def up_body(vec_h, basis_h, ltr_h, ptr_h, lsend_h, psend_h, tops, own, sib, cross, fwd, back,
            vec, basis, ltr, ptr, lsend, psend, low, mid, sems):
    leaves, vecs, rank = vec.shape
    col = lax.axis_index("col")
    cap0 = lsend.shape[2]
    cap1 = psend.shape[1]
    made = copies(
        [(vec_h, vec), (basis_h, basis), (ltr_h, ltr), (ptr_h, ptr), (lsend_h, lsend), (psend_h, psend)], sems
    )
    made[0].wait()
    made[1].wait()
    for t in range(leaves):
        low[t] = dot(vec[t], basis[t]).astype(BF)
    made[2].wait()
    for j in range(leaves // 2):
        mid[j] = dot(
            beside(low[2 * j], low[2 * j + 1]), ltr[2 * j:2 * j + 2].reshape(2 * rank, rank)
        ).astype(BF)
    made[3].wait()
    high = []
    for i in range(leaves // 4):
        high.append(
            dot(beside(mid[2 * i], mid[2 * i + 1]), ptr[2 * i:2 * i + 2].reshape(2 * rank, rank)).astype(BF)
        )
    for i in range(leaves // 8):
        both = beside(high[2 * i], high[2 * i + 1])
        for row in range(tops.shape[0]):
            tops[row, i] = both
    made[4].wait()
    made[5].wait()

    def pack(out, place):
        for c in range(cap0 // 2):
            out[c] = beside(low[lsend[place, 0, 2 * c]], low[lsend[place, 0, 2 * c + 1]])
        for c in range(cap1 // 2):
            out[cap0 // 2 + c] = beside(mid[psend[0, 2 * c, place]], mid[psend[0, 2 * c + 1, place]])

    def pack_halo(out, start):
        out[(cap0 + cap1) // 2] = beside(vec[start], vec[start + 1])

    pack(sib, 1 + 2 * col)
    pack_halo(sib, (1 - col) * (leaves - HW))
    pack(cross, 3 - 2 * col)
    pack_halo(cross, col * (leaves - HW))
    pack(fwd, 0)
    pack(back, 4)
    pack(own, REACH)


def up_pass(lsend, psend, vec, basis, ltr, ptr, rows):
    leaves, vecs, rank = vec.shape
    count = (lsend.shape[2] + psend.shape[1]) // 2
    shape = lambda *n: jax.ShapeDtypeStruct(n + (vecs, 2 * rank), BF)
    return call(
        up_body, "up", (vec, basis, ltr, ptr, lsend, psend), (),
        [shape(rows, leaves // 8), shape(count), shape(count + 1), shape(count + 1), shape(count), shape(count)],
        [WHOLE] * 6,
        [
            like(vec), like(basis), like(ltr), like(ptr), held(lsend), held(psend),
            VMEM((leaves, vecs, rank), BF), VMEM((leaves // 2, vecs, rank), BF), DMA((6,)),
        ],
        (10_000_000, 3_000_000),
    )


def near_body(vec_h, blocks_h, offsets_h, out, blocks, padded, offsets, sems, chunk_sems):
    leaves = blocks.shape[1]
    _, vecs, rank = padded.shape
    chunks = chunk_sems.shape[0]
    per = leaves // chunks
    made = copies([(vec_h, padded.at[pl.ds(HW, leaves)]), (offsets_h, offsets)], sems)
    chunk = chunk_of(blocks_h, blocks, chunk_sems, per)
    for c in range(chunks):
        chunk(c).start()
    zero = jnp.zeros((HW, vecs, rank), BF)
    padded[0:HW] = zero
    padded[HW + leaves:] = zero
    for copy in made:
        copy.wait()

    def body(c, _):
        chunk(c).wait()
        for q in range(per):
            t = c * per + q
            total = None
            for n in range(blocks.shape[2]):
                part = dot_t(padded[t + HW + offsets[n, t]], above(*[blocks[k, t, n] for k in range(blocks.shape[0])]))
                total = part if total is None else total + part
            out[t] = by_kernel(total, rank)
        return 0

    lax.fori_loop(0, chunks, body, 0)


def near_pass(offsets, vec, blocks, chunks):
    kernels, leaves, near, rank, _ = blocks.shape
    vecs = vec.shape[1]
    return call(
        near_body, "near", (vec, blocks, offsets), (),
        jax.ShapeDtypeStruct((leaves, kernels * vecs, rank), F32),
        WHOLE,
        [
            like(blocks), VMEM((leaves + 2 * HW, vecs, rank), BF), held(offsets), DMA((2,)), DMA((chunks,)),
        ],
        (40_000_000, 12_000_000),
    )


def rest_body(leaf_h, pair_h, coupling_h, near_h, ptr_h, ltr_h, basis_h, llist_h, plist_h, tlist_h, offsets_h,
              own, sib, cross, fwd, back, mine, theirs, near, out,
              leaf, pair, coupling, first, last, ptr, ltr, basis, llist, plist, tlist, offsets,
              wleaf, wpair, halo, tops, far0, far1, down, sems, leaf_sems, pair_sems, top_sems):
    kernels, leaves, partners, rank, _ = leaf.shape
    _, vecs, _ = wleaf.shape
    count = coupling.shape[1]
    cap0 = wleaf.shape[0] // WIN
    cap1 = wpair.shape[0] // WIN
    base = own.shape[0] - cap1 // 2
    heads = first.shape[1]
    chunks = leaf_sems.shape[0]
    per = leaves // chunks
    col = lax.axis_index("col")
    place = lax.axis_index("row") * lax.axis_size("col") + col
    last_place = lax.axis_size("row") * lax.axis_size("col") - 1
    lists = copies([(llist_h, llist), (plist_h, plist), (tlist_h, tlist), (offsets_h, offsets)], sems)
    leaf_chunk = chunk_of(leaf_h, leaf, leaf_sems, per)
    pair_chunk = chunk_of(pair_h, pair, pair_sems, per // 2)
    top_chunk = chunk_of(coupling_h, coupling, top_sems, 1)
    for c in range(chunks):
        leaf_chunk(c).start()
        pair_chunk(c).start()
    for c in range(count):
        top_chunk(c).start()
    others = copies(
        [
            (near_h.at[:, pl.ds(0, heads)], first), (near_h.at[:, pl.ds(leaves - heads, heads)], last),
            (ptr_h, ptr), (ltr_h, ltr), (basis_h, basis),
        ],
        sems.at[pl.ds(4, 5)],
    )

    for block, slot in ((own, REACH), (fwd, 0), (back, 4), (sib, 3 - 2 * col), (cross, 1 + 2 * col)):
        for c in range(cap0 // 2):
            split(block[c], wleaf, slot * cap0 + 2 * c)
        for c in range(cap1 // 2):
            split(block[base + c], wpair, slot * cap1 + 2 * c)
    zero = jnp.zeros((vecs, rank), BF)
    for block, slot in ((sib, HW - HW * col), (cross, HW * col)):
        row = block[base + cap1 // 2]
        outside = (place == 0) & (slot == 0) | (place == last_place) & (slot == HW)
        split(jnp.where(outside, jnp.zeros_like(row), row), halo, slot)
    halo[2 * HW] = zero
    for block, side in ((mine, col), (theirs, 1 - col)):
        for s in range(block.shape[0]):
            for i in range(block.shape[1]):
                split(block[s, i], tops, (s * 2 + side) * count + 2 * i)
    for copy in lists:
        copy.wait()

    def body(c, _):
        leaf_chunk(c).wait()
        pair_chunk(c).wait()
        for q in range(per):
            t = c * per + q
            rows = beside(*[wleaf[llist[m, t]] for m in range(partners)])
            far0[t] = by_kernel(dot_t(rows, row_of_blocks(leaf, t)), rank)
        for q in range(per // 2):
            j = c * (per // 2) + q
            rows = beside(*[wpair[plist[m, j]] for m in range(pair.shape[2])])
            far1[j] = by_kernel(dot_t(rows, row_of_blocks(pair, j)), rank)
        return 0

    lax.fori_loop(0, chunks, body, 0)

    for i in range(count):
        top_chunk(i).wait()
        rows = beside(*[tops[tlist[i, m]] for m in range(coupling.shape[2])])
        down[i] = by_kernel(dot_t(rows, row_of_blocks(coupling, i)), rank).astype(BF)
    for copy in others:
        copy.wait()

    def edge(t):
        if t < heads:
            ref, q = first, t
        else:
            ref, q = last, t - (leaves - heads)
        spots = [t + offsets[n, t] for n in range(ref.shape[2])]
        if t < heads:
            spots = [jnp.where(at < 0, at + HW, 2 * HW) for at in spots]
        else:
            spots = [jnp.where(at >= leaves, at - leaves + HW, 2 * HW) for at in spots]
        return by_kernel(dot_t(beside(*[halo[at] for at in spots]), row_of_blocks(ref, q)), rank)

    down1 = []
    for j in range(2 * count):
        down1.append((far1[j] + dot_t(down[j // 2], ptr[j])).astype(BF))
    down0 = []
    for t in range(leaves):
        down0.append((far0[t] + dot_t(down1[t // 2], ltr[t])).astype(BF))
    for t in range(leaves):
        points = dot_t(down0[t], basis[t]) + near[t]
        if t < heads or t >= leaves - heads:
            points = points + edge(t)
        points = points.astype(BF)
        for k in range(kernels):
            out[k, t] = points[k * vecs:(k + 1) * vecs]


def rest_pass(leaf, pair, coupling, near_blocks, ptr, ltr, basis, llist, plist, tlist, offsets,
              own, sib, cross, fwd, back, mine, theirs, near, cap0, cap1, chunks):
    kernels, leaves, _, rank, _ = leaf.shape
    count = coupling.shape[1]
    vecs = own.shape[1]
    ends = VMEM((kernels, HW) + near_blocks.shape[2:], BF)
    params = (leaf, pair, coupling, near_blocks, ptr, ltr, basis, llist, plist, tlist, offsets)
    return call(
        rest_body, "rest", params, (own, sib, cross, fwd, back, mine, theirs, near),
        jax.ShapeDtypeStruct((kernels, leaves, vecs, rank), BF),
        WHOLE,
        [like(leaf), like(pair), like(coupling), ends, ends, like(ptr), like(ltr), like(basis)]
        + [held(x) for x in (llist, plist, tlist, offsets)]
        + [VMEM((n, vecs, rank), BF) for n in (WIN * cap0, WIN * cap1, 2 * HW + 1, 2 * mine.shape[0] * count)]
        + [
            VMEM((leaves, kernels * vecs, rank), F32), VMEM((leaves // 2, kernels * vecs, rank), F32),
            VMEM((count, kernels * vecs, rank), BF), DMA((9,)), DMA((chunks,)), DMA((chunks,)), DMA((count,)),
        ],
        (100_000_000, 20_000_000),
    )


def on_device(
    vectors,
    leaf_basis,
    leaf_transfer,
    pair_transfer,
    near_blocks,
    near_offset,
    leaf_send,
    leaf_list,
    leaf_coupling,
    pair_send,
    pair_list,
    pair_coupling,
    top_list,
    top_coupling,
):
    rows = lax.axis_size("row")
    devs = rows * lax.axis_size("col")
    cap0, cap1 = leaf_send.shape[2], pair_send.shape[2]
    lsend = jnp.transpose(leaf_send, (1, 0, 2))
    psend = jnp.transpose(pair_send, (0, 2, 1))
    offsets = near_offset.T
    tops, own, sib, cross, fwd, back = up_pass(
        lsend, psend, vectors, leaf_basis, leaf_transfer, pair_transfer, rows
    )
    ring = range(devs)
    sibling = [(d, d ^ 1) for d in ring]
    mine = lax.all_to_all(tops, "row", split_axis=0, concat_axis=0)
    theirs = lax.ppermute(mine, AXES, sibling)
    sib = lax.ppermute(sib, AXES, sibling)
    cross = lax.ppermute(cross, AXES, [(d, (d + 1 if d % 2 else d - 1) % devs) for d in ring])
    fwd = lax.ppermute(fwd, AXES, [(d, (d + 2) % devs) for d in ring])
    back = lax.ppermute(back, AXES, [(d, (d - 2) % devs) for d in ring])
    near = near_pass(offsets, vectors, near_blocks, 4)
    return rest_pass(
        leaf_coupling, pair_coupling, top_coupling, near_blocks, pair_transfer, leaf_transfer, leaf_basis,
        leaf_list.T, pair_list.T, top_list, offsets,
        own, sib, cross, fwd, back, mine, theirs, near, cap0, cap1, 4,
    )


def solution(mesh):
    placed = P(("groups", "row", "col"))
    behind = P(None, ("groups", "row", "col"))
    return jax.shard_map(
        on_device,
        mesh=mesh,
        in_specs=(
            placed, placed, placed, placed, behind, placed, placed, placed, behind, placed, placed, behind, placed, behind,
        ),
        out_specs=behind,
        check_vma=False,
    )
```

```python
import jax
import jax.numpy as jnp
from jax import lax
from jax.experimental import pallas as pl
from jax.experimental.pallas import tpu as pltpu
from jax.sharding import PartitionSpec as P

REACH = 2
WIN = 2 * REACH + 1
HW = 2
AXES = ("row", "col")
F32 = jnp.float32
BF = jnp.bfloat16
LIMIT = 56 * 1024 * 1024

VMEM = pltpu.VMEM
SMEM = pltpu.SMEM
DMA = pltpu.SemaphoreType.DMA
FIXED = pl.BlockSpec(memory_space=pltpu.HBM)
WHOLE = pl.BlockSpec(memory_space=VMEM)


def dot(left, right):
    return jnp.dot(left, right, preferred_element_type=F32)


def beside(*parts):
    return jnp.concatenate(parts, axis=1)


def above(*parts):
    return jnp.concatenate(parts, axis=0)


def dot_t(left, right):
    return lax.dot_general(left, right, (((1,), (1,)), ((), ())), preferred_element_type=F32)


def row_of_blocks(ref, q):
    kernels, _, partners, _, _ = ref.shape
    return beside(*[above(*[ref[k, q, m] for k in range(kernels)]) for m in range(partners)])


def by_kernel(wide, rank):
    return above(*[wide[:, k * rank:(k + 1) * rank] for k in range(wide.shape[1] // rank)])


def copies(pairs, sems):
    made = [pltpu.make_async_copy(src, dst, sems.at[i]) for i, (src, dst) in enumerate(pairs)]
    for copy in made:
        copy.start()
    return made


class Chunk:
    def __init__(self, src, dst, sems, size, c):
        self.src, self.dst, self.sem = src, dst, sems.at[c]
        self.part = pl.ds(c * size, size)

    def start(self, turn):
        for k in range(self.dst.shape[0]):
            pltpu.make_async_copy(
                self.src.at[k, self.part], self.dst.at[k, self.part], self.sem
            ).start(priority=(turn + k) % 2)

    def wait(self):
        pltpu.make_async_copy(self.src.at[:, self.part], self.dst.at[:, self.part], self.sem).wait()


def chunk_of(src, dst, sems, size):
    return lambda c: Chunk(src, dst, sems, size, c)


def split(row, ref, at):
    rank = row.shape[1] // 2
    ref[at] = row[:, :rank]
    ref[at + 1] = row[:, rank:]


def call(body, name, params, arrays, out_shape, out_specs, scratch, cost, limit=LIMIT):
    return pl.pallas_call(
        body,
        out_shape=out_shape,
        in_specs=[FIXED] * len(params) + [WHOLE] * len(arrays),
        out_specs=out_specs,
        scratch_shapes=scratch,
        compiler_params=pltpu.CompilerParams(vmem_limit_bytes=limit),
        cost_estimate=pl.CostEstimate(flops=cost[0], bytes_accessed=cost[1], transcendentals=0),
        name=name,
    )(*params, *arrays)


def like(x):
    return VMEM(x.shape, x.dtype)


def held(x):
    return SMEM(x.shape, x.dtype)


def up_body(vec_h, basis_h, ltr_h, ptr_h, lsend_h, psend_h, tops, own, sib, cross, fwd, back,
            vec, basis, ltr, ptr, lsend, psend, low, mid, sems):
    leaves, vecs, rank = vec.shape
    col = lax.axis_index("col")
    cap0 = lsend.shape[2]
    cap1 = psend.shape[1]
    made = copies(
        [(vec_h, vec), (basis_h, basis), (ltr_h, ltr), (ptr_h, ptr), (lsend_h, lsend), (psend_h, psend)], sems
    )
    made[0].wait()
    made[1].wait()
    for t in range(leaves):
        low[t] = dot(vec[t], basis[t]).astype(BF)
    made[2].wait()
    for j in range(leaves // 2):
        mid[j] = dot(
            beside(low[2 * j], low[2 * j + 1]), ltr[2 * j:2 * j + 2].reshape(2 * rank, rank)
        ).astype(BF)
    made[3].wait()
    high = []
    for i in range(leaves // 4):
        high.append(
            dot(beside(mid[2 * i], mid[2 * i + 1]), ptr[2 * i:2 * i + 2].reshape(2 * rank, rank)).astype(BF)
        )
    for i in range(leaves // 8):
        both = beside(high[2 * i], high[2 * i + 1])
        for row in range(tops.shape[0]):
            tops[row, i] = both
    made[4].wait()
    made[5].wait()

    def pack(out, place):
        for c in range(cap0 // 2):
            out[c] = beside(low[lsend[place, 0, 2 * c]], low[lsend[place, 0, 2 * c + 1]])
        for c in range(cap1 // 2):
            out[cap0 // 2 + c] = beside(mid[psend[0, 2 * c, place]], mid[psend[0, 2 * c + 1, place]])

    def pack_halo(out, start):
        out[(cap0 + cap1) // 2] = beside(vec[start], vec[start + 1])

    pack(sib, 1 + 2 * col)
    pack_halo(sib, (1 - col) * (leaves - HW))
    pack(cross, 3 - 2 * col)
    pack_halo(cross, col * (leaves - HW))
    pack(fwd, 0)
    pack(back, 4)
    pack(own, REACH)


def up_pass(lsend, psend, vec, basis, ltr, ptr, rows):
    leaves, vecs, rank = vec.shape
    count = (lsend.shape[2] + psend.shape[1]) // 2
    shape = lambda *n: jax.ShapeDtypeStruct(n + (vecs, 2 * rank), BF)
    return call(
        up_body, "up", (vec, basis, ltr, ptr, lsend, psend), (),
        [shape(rows, leaves // 8), shape(count), shape(count + 1), shape(count + 1), shape(count), shape(count)],
        [WHOLE] * 6,
        [
            like(vec), like(basis), like(ltr), like(ptr), held(lsend), held(psend),
            VMEM((leaves, vecs, rank), BF), VMEM((leaves // 2, vecs, rank), BF), DMA((6,)),
        ],
        (10_000_000, 3_000_000),
    )


def near_body(vec_h, blocks_h, offsets_h, out, blocks, padded, offsets, sems, chunk_sems):
    leaves = blocks.shape[1]
    _, vecs, rank = padded.shape
    chunks = chunk_sems.shape[0]
    per = leaves // chunks
    made = copies([(vec_h, padded.at[pl.ds(HW, leaves)]), (offsets_h, offsets)], sems)
    chunk = chunk_of(blocks_h, blocks, chunk_sems, per)
    for c in range(chunks):
        chunk(c).start(c)
    zero = jnp.zeros((HW, vecs, rank), BF)
    padded[0:HW] = zero
    padded[HW + leaves:] = zero
    for copy in made:
        copy.wait()

    def body(c, _):
        chunk(c).wait()
        for q in range(per):
            t = c * per + q
            total = None
            for n in range(blocks.shape[2]):
                part = dot_t(padded[t + HW + offsets[n, t]], above(*[blocks[k, t, n] for k in range(blocks.shape[0])]))
                total = part if total is None else total + part
            out[t] = by_kernel(total, rank)
        return 0

    lax.fori_loop(0, chunks, body, 0)


def near_pass(offsets, vec, blocks, chunks):
    kernels, leaves, near, rank, _ = blocks.shape
    vecs = vec.shape[1]
    return call(
        near_body, "near", (vec, blocks, offsets), (),
        jax.ShapeDtypeStruct((leaves, kernels * vecs, rank), F32),
        WHOLE,
        [
            like(blocks), VMEM((leaves + 2 * HW, vecs, rank), BF), held(offsets), DMA((2,)), DMA((chunks,)),
        ],
        (40_000_000, 12_000_000),
    )


def rest_body(leaf_h, pair_h, coupling_h, near_h, ptr_h, ltr_h, basis_h, llist_h, plist_h, tlist_h, offsets_h,
              own, sib, cross, fwd, back, mine, theirs, near, out,
              leaf, pair, coupling, first, last, ptr, ltr, basis, llist, plist, tlist, offsets,
              wleaf, wpair, halo, tops, far0, far1, down, sems, leaf_sems, pair_sems, top_sems):
    kernels, leaves, partners, rank, _ = leaf.shape
    _, vecs, _ = wleaf.shape
    count = coupling.shape[1]
    cap0 = wleaf.shape[0] // WIN
    cap1 = wpair.shape[0] // WIN
    base = own.shape[0] - cap1 // 2
    heads = first.shape[1]
    chunks = leaf_sems.shape[0]
    per = leaves // chunks
    col = lax.axis_index("col")
    place = lax.axis_index("row") * lax.axis_size("col") + col
    last_place = lax.axis_size("row") * lax.axis_size("col") - 1
    lists = copies([(llist_h, llist), (plist_h, plist), (tlist_h, tlist), (offsets_h, offsets)], sems)
    leaf_chunk = chunk_of(leaf_h, leaf, leaf_sems, per)
    pair_chunk = chunk_of(pair_h, pair, pair_sems, per // 2)
    top_chunk = chunk_of(coupling_h, coupling, top_sems, 1)
    for c in range(chunks):
        leaf_chunk(c).start(c)
        pair_chunk(c).start(c + 1)
    for c in range(count):
        top_chunk(c).start(c)
    others = copies(
        [
            (near_h.at[:, pl.ds(0, heads)], first), (near_h.at[:, pl.ds(leaves - heads, heads)], last),
            (ptr_h, ptr), (ltr_h, ltr), (basis_h, basis),
        ],
        sems.at[pl.ds(4, 5)],
    )

    for block, slot in ((own, REACH), (fwd, 0), (back, 4), (sib, 3 - 2 * col), (cross, 1 + 2 * col)):
        for c in range(cap0 // 2):
            split(block[c], wleaf, slot * cap0 + 2 * c)
        for c in range(cap1 // 2):
            split(block[base + c], wpair, slot * cap1 + 2 * c)
    zero = jnp.zeros((vecs, rank), BF)
    for block, slot in ((sib, HW - HW * col), (cross, HW * col)):
        row = block[base + cap1 // 2]
        outside = (place == 0) & (slot == 0) | (place == last_place) & (slot == HW)
        split(jnp.where(outside, jnp.zeros_like(row), row), halo, slot)
    halo[2 * HW] = zero
    for block, side in ((mine, col), (theirs, 1 - col)):
        for s in range(block.shape[0]):
            for i in range(block.shape[1]):
                split(block[s, i], tops, (s * 2 + side) * count + 2 * i)
    for copy in lists:
        copy.wait()

    def body(c, _):
        leaf_chunk(c).wait()
        pair_chunk(c).wait()
        for q in range(per):
            t = c * per + q
            rows = beside(*[wleaf[llist[m, t]] for m in range(partners)])
            far0[t] = by_kernel(dot_t(rows, row_of_blocks(leaf, t)), rank)
        for q in range(per // 2):
            j = c * (per // 2) + q
            rows = beside(*[wpair[plist[m, j]] for m in range(pair.shape[2])])
            far1[j] = by_kernel(dot_t(rows, row_of_blocks(pair, j)), rank)
        return 0

    lax.fori_loop(0, chunks, body, 0)

    for i in range(count):
        top_chunk(i).wait()
        rows = beside(*[tops[tlist[i, m]] for m in range(coupling.shape[2])])
        down[i] = by_kernel(dot_t(rows, row_of_blocks(coupling, i)), rank).astype(BF)
    for copy in others:
        copy.wait()

    def edge(t):
        if t < heads:
            ref, q = first, t
        else:
            ref, q = last, t - (leaves - heads)
        spots = [t + offsets[n, t] for n in range(ref.shape[2])]
        if t < heads:
            spots = [jnp.where(at < 0, at + HW, 2 * HW) for at in spots]
        else:
            spots = [jnp.where(at >= leaves, at - leaves + HW, 2 * HW) for at in spots]
        return by_kernel(dot_t(beside(*[halo[at] for at in spots]), row_of_blocks(ref, q)), rank)

    down1 = []
    for j in range(2 * count):
        down1.append((far1[j] + dot_t(down[j // 2], ptr[j])).astype(BF))
    down0 = []
    for t in range(leaves):
        down0.append((far0[t] + dot_t(down1[t // 2], ltr[t])).astype(BF))
    for t in range(leaves):
        points = dot_t(down0[t], basis[t]) + near[t]
        if t < heads or t >= leaves - heads:
            points = points + edge(t)
        points = points.astype(BF)
        for k in range(kernels):
            out[k, t] = points[k * vecs:(k + 1) * vecs]


def rest_pass(leaf, pair, coupling, near_blocks, ptr, ltr, basis, llist, plist, tlist, offsets,
              own, sib, cross, fwd, back, mine, theirs, near, cap0, cap1, chunks):
    kernels, leaves, _, rank, _ = leaf.shape
    count = coupling.shape[1]
    vecs = own.shape[1]
    ends = VMEM((kernels, HW) + near_blocks.shape[2:], BF)
    params = (leaf, pair, coupling, near_blocks, ptr, ltr, basis, llist, plist, tlist, offsets)
    return call(
        rest_body, "rest", params, (own, sib, cross, fwd, back, mine, theirs, near),
        jax.ShapeDtypeStruct((kernels, leaves, vecs, rank), BF),
        WHOLE,
        [like(leaf), like(pair), like(coupling), ends, ends, like(ptr), like(ltr), like(basis)]
        + [held(x) for x in (llist, plist, tlist, offsets)]
        + [VMEM((n, vecs, rank), BF) for n in (WIN * cap0, WIN * cap1, 2 * HW + 1, 2 * mine.shape[0] * count)]
        + [
            VMEM((leaves, kernels * vecs, rank), F32), VMEM((leaves // 2, kernels * vecs, rank), F32),
            VMEM((count, kernels * vecs, rank), BF), DMA((9,)), DMA((chunks,)), DMA((chunks,)), DMA((count,)),
        ],
        (100_000_000, 20_000_000),
    )


def on_device(
    vectors,
    leaf_basis,
    leaf_transfer,
    pair_transfer,
    near_blocks,
    near_offset,
    leaf_send,
    leaf_list,
    leaf_coupling,
    pair_send,
    pair_list,
    pair_coupling,
    top_list,
    top_coupling,
):
    rows = lax.axis_size("row")
    devs = rows * lax.axis_size("col")
    cap0, cap1 = leaf_send.shape[2], pair_send.shape[2]
    lsend = jnp.transpose(leaf_send, (1, 0, 2))
    psend = jnp.transpose(pair_send, (0, 2, 1))
    offsets = near_offset.T
    tops, own, sib, cross, fwd, back = up_pass(
        lsend, psend, vectors, leaf_basis, leaf_transfer, pair_transfer, rows
    )
    ring = range(devs)
    sibling = [(d, d ^ 1) for d in ring]
    mine = lax.all_to_all(tops, "row", split_axis=0, concat_axis=0)
    theirs = lax.ppermute(mine, AXES, sibling)
    sib = lax.ppermute(sib, AXES, sibling)
    cross = lax.ppermute(cross, AXES, [(d, (d + 1 if d % 2 else d - 1) % devs) for d in ring])
    fwd = lax.ppermute(fwd, AXES, [(d, (d + 2) % devs) for d in ring])
    back = lax.ppermute(back, AXES, [(d, (d - 2) % devs) for d in ring])
    near = near_pass(offsets, vectors, near_blocks, 4)
    return rest_pass(
        leaf_coupling, pair_coupling, top_coupling, near_blocks, pair_transfer, leaf_transfer, leaf_basis,
        leaf_list.T, pair_list.T, top_list, offsets,
        own, sib, cross, fwd, back, mine, theirs, near, cap0, cap1, 4,
    )


def solution(mesh):
    placed = P(("groups", "row", "col"))
    behind = P(None, ("groups", "row", "col"))
    return jax.shard_map(
        on_device,
        mesh=mesh,
        in_specs=(
            placed, placed, placed, placed, behind, placed, placed, placed, behind, placed, placed, behind, placed, behind,
        ),
        out_specs=behind,
        check_vma=False,
    )
```

```python
import jax
import jax.numpy as jnp
from jax import lax
from jax.experimental import pallas as pl
from jax.experimental.pallas import tpu as pltpu
from jax.sharding import PartitionSpec as P

REACH = 2
WIN = 2 * REACH + 1
HW = 2
GROUP = 8
AXES = ("row", "col")
F32 = jnp.float32
BF = jnp.bfloat16
LIMIT = 56 * 1024 * 1024

VMEM = pltpu.VMEM
SMEM = pltpu.SMEM
DMA = pltpu.SemaphoreType.DMA
FIXED = pl.BlockSpec(memory_space=pltpu.HBM)
WHOLE = pl.BlockSpec(memory_space=VMEM)


def dot(left, right):
    return jnp.dot(left, right, preferred_element_type=F32)


def beside(*parts):
    return jnp.concatenate(parts, axis=1)


def above(*parts):
    return jnp.concatenate(parts, axis=0)


def dot_t(left, right):
    return lax.dot_general(left, right, (((1,), (1,)), ((), ())), preferred_element_type=F32)


def row_of_blocks(ref, q):
    kernels, _, partners, _, _ = ref.shape
    return beside(*[above(*[ref[k, q, m] for k in range(kernels)]) for m in range(partners)])


def by_kernel(wide, rank):
    return above(*[wide[:, k * rank:(k + 1) * rank] for k in range(wide.shape[1] // rank)])


def copies(pairs, sems):
    made = [pltpu.make_async_copy(src, dst, sems.at[i]) for i, (src, dst) in enumerate(pairs)]
    for copy in made:
        copy.start()
    return made


def split(row, ref, at):
    rank = row.shape[1] // 2
    ref[at] = row[:, :rank]
    ref[at + 1] = row[:, rank:]


def call(body, name, params, arrays, out_shape, out_specs, scratch, cost, limit=LIMIT):
    return pl.pallas_call(
        body,
        out_shape=out_shape,
        in_specs=[FIXED] * len(params) + [WHOLE] * len(arrays),
        out_specs=out_specs,
        scratch_shapes=scratch,
        compiler_params=pltpu.CompilerParams(vmem_limit_bytes=limit),
        cost_estimate=pl.CostEstimate(flops=cost[0], bytes_accessed=cost[1], transcendentals=0),
        name=name,
    )(*params, *arrays)


def like(x):
    return VMEM(x.shape, x.dtype)


def held(x):
    return SMEM(x.shape, x.dtype)


def up_body(vec_h, basis_h, ltr_h, ptr_h, lsend_h, psend_h, tops, own, sib, cross, fwd, back,
            vec, basis, ltr, ptr, lsend, psend, low, mid, sems):
    leaves, vecs, rank = vec.shape
    col = lax.axis_index("col")
    cap0 = lsend.shape[2]
    cap1 = psend.shape[1]
    made = copies(
        [(vec_h, vec), (basis_h, basis), (ltr_h, ltr), (ptr_h, ptr), (lsend_h, lsend), (psend_h, psend)], sems
    )
    made[0].wait()
    made[1].wait()
    for t in range(leaves):
        low[t] = dot(vec[t], basis[t]).astype(BF)
    made[2].wait()
    for j in range(leaves // 2):
        mid[j] = dot(
            beside(low[2 * j], low[2 * j + 1]), ltr[2 * j:2 * j + 2].reshape(2 * rank, rank)
        ).astype(BF)
    made[3].wait()
    high = []
    for i in range(leaves // 4):
        high.append(
            dot(beside(mid[2 * i], mid[2 * i + 1]), ptr[2 * i:2 * i + 2].reshape(2 * rank, rank)).astype(BF)
        )
    for i in range(leaves // 8):
        both = beside(high[2 * i], high[2 * i + 1])
        for row in range(tops.shape[0]):
            tops[row, i] = both
    made[4].wait()
    made[5].wait()

    def pack(out, place):
        for c in range(cap0 // 2):
            out[c] = beside(low[lsend[place, 0, 2 * c]], low[lsend[place, 0, 2 * c + 1]])
        for c in range(cap1 // 2):
            out[cap0 // 2 + c] = beside(mid[psend[0, 2 * c, place]], mid[psend[0, 2 * c + 1, place]])

    def pack_halo(out, start):
        out[(cap0 + cap1) // 2] = beside(vec[start], vec[start + 1])

    pack(sib, 1 + 2 * col)
    pack_halo(sib, (1 - col) * (leaves - HW))
    pack(cross, 3 - 2 * col)
    pack_halo(cross, col * (leaves - HW))
    pack(fwd, 0)
    pack(back, 4)
    pack(own, REACH)


def up_pass(lsend, psend, vec, basis, ltr, ptr, rows):
    leaves, vecs, rank = vec.shape
    count = (lsend.shape[2] + psend.shape[1]) // 2
    shape = lambda *n: jax.ShapeDtypeStruct(n + (vecs, 2 * rank), BF)
    return call(
        up_body, "up", (vec, basis, ltr, ptr, lsend, psend), (),
        [shape(rows, leaves // 8), shape(count), shape(count + 1), shape(count + 1), shape(count), shape(count)],
        [WHOLE] * 6,
        [
            like(vec), like(basis), like(ltr), like(ptr), held(lsend), held(psend),
            VMEM((leaves, vecs, rank), BF), VMEM((leaves // 2, vecs, rank), BF), DMA((6,)),
        ],
        (10_000_000, 3_000_000),
    )


def near_body(offsets_h, vec, near, close, ends, padded, offsets, sems):
    leaves, vecs, rank = vec.shape
    kernels = near.shape[0]
    made = copies([(offsets_h, offsets)], sems)
    ends[:, 0:HW] = near[:, 0:HW]
    ends[:, HW:] = near[:, leaves - HW:]
    zero = jnp.zeros((HW, vecs, rank), BF)
    padded[0:HW] = zero
    padded[HW:HW + leaves] = vec[...]
    padded[HW + leaves:] = zero
    made[0].wait()

    def body(c, _):
        for q in range(GROUP):
            t = c * GROUP + q
            total = None
            for n in range(near.shape[2]):
                part = dot_t(padded[t + HW + offsets[n, t]], above(*[near[k, t, n] for k in range(kernels)]))
                total = part if total is None else total + part
            close[t] = by_kernel(total, rank)
        return 0

    lax.fori_loop(0, leaves // GROUP, body, 0)


def near_pass(offsets, vec, blocks):
    kernels, leaves, near, rank, _ = blocks.shape
    vecs = vec.shape[1]
    return call(
        near_body, "near", (offsets,), (vec, blocks),
        [
            jax.ShapeDtypeStruct((leaves, kernels * vecs, rank), F32),
            jax.ShapeDtypeStruct((kernels, 2 * HW) + blocks.shape[2:], BF),
        ],
        [WHOLE] * 2,
        [VMEM((leaves + 2 * HW, vecs, rank), BF), held(offsets), DMA((1,))],
        (4_000_000_000, 60_000_000), 8 * 1024 * 1024,
    )


def far_sum(rows, blocks, q):
    return dot_t(beside(*rows), row_of_blocks(blocks, q))


def rest_body(llist_h, plist_h, tlist_h, offsets_h,
              leaf, pair, coupling, ends, ptr, ltr, basis, close, own, sib, cross, fwd, back, mine, theirs, out,
              llist, plist, tlist, offsets, wleaf, wpair, halo, tops, far0, far1, down, sems):
    kernels, leaves, partners, rank, _ = leaf.shape
    _, vecs, _ = wleaf.shape
    count = coupling.shape[1]
    cap0 = wleaf.shape[0] // WIN
    cap1 = wpair.shape[0] // WIN
    base = own.shape[0] - cap1 // 2
    col = lax.axis_index("col")
    place = lax.axis_index("row") * lax.axis_size("col") + col
    last_place = lax.axis_size("row") * lax.axis_size("col") - 1
    lists = copies([(llist_h, llist), (plist_h, plist), (tlist_h, tlist), (offsets_h, offsets)], sems)

    for block, slot in ((own, REACH), (fwd, 0), (back, 4), (sib, 3 - 2 * col), (cross, 1 + 2 * col)):
        for c in range(cap0 // 2):
            split(block[c], wleaf, slot * cap0 + 2 * c)
        for c in range(cap1 // 2):
            split(block[base + c], wpair, slot * cap1 + 2 * c)
    halo[2 * HW] = jnp.zeros((vecs, rank), BF)
    for block, upper in ((sib, 1 - col), (cross, col)):
        row = block[base + cap1 // 2]
        outside = (place == 0) & (upper == 0) | (place == last_place) & (upper == 1)
        split(jnp.where(outside, jnp.zeros_like(row), row), halo, upper * HW)
    for block, side in ((mine, col), (theirs, 1 - col)):
        for s in range(block.shape[0]):
            for i in range(block.shape[1]):
                split(block[s, i], tops, (s * 2 + side) * count + 2 * i)
    for copy in lists:
        copy.wait()

    def body(c, _):
        for q in range(GROUP):
            t = c * GROUP + q
            far0[t] = by_kernel(far_sum([wleaf[llist[m, t]] for m in range(partners)], leaf, t), rank)
        for q in range(GROUP // 2):
            j = c * (GROUP // 2) + q
            far1[j] = by_kernel(far_sum([wpair[plist[m, j]] for m in range(pair.shape[2])], pair, j), rank)
        for q in range(GROUP // 4):
            i = c * (GROUP // 4) + q
            rows = [tops[tlist[i, m]] for m in range(coupling.shape[2])]
            down[i] = by_kernel(far_sum(rows, coupling, i), rank).astype(BF)
        return 0

    lax.fori_loop(0, leaves // GROUP, body, 0)

    def edge(t):
        spots = [t + offsets[n, t] for n in range(ends.shape[2])]
        if t < HW:
            spots = [jnp.where(at < 0, at + HW, 2 * HW) for at in spots]
        else:
            spots = [jnp.where(at >= leaves, at - leaves + HW, 2 * HW) for at in spots]
        return by_kernel(far_sum([halo[at] for at in spots], ends, t if t < HW else t - (leaves - 2 * HW)), rank)

    down1 = []
    for j in range(2 * count):
        down1.append((far1[j] + dot_t(down[j // 2], ptr[j])).astype(BF))
    down0 = []
    for t in range(leaves):
        down0.append((far0[t] + dot_t(down1[t // 2], ltr[t])).astype(BF))
    for t in range(leaves):
        points = dot_t(down0[t], basis[t]) + close[t]
        if t < HW or t >= leaves - HW:
            points = points + edge(t)
        points = points.astype(BF)
        for k in range(kernels):
            out[k, t] = points[k * vecs:(k + 1) * vecs]


def rest_pass(lists, arrays, windows, cap0, cap1):
    leaf, pair, coupling = arrays[:3]
    kernels, leaves, _, rank, _ = leaf.shape
    count = coupling.shape[1]
    vecs = windows[0].shape[1]
    rows = kernels * vecs
    return call(
        rest_body, "rest", lists, arrays + windows,
        jax.ShapeDtypeStruct((kernels, leaves, vecs, rank), BF),
        WHOLE,
        [held(x) for x in lists]
        + [
            VMEM((n, vecs, rank), BF)
            for n in (WIN * cap0, WIN * cap1, 2 * HW + 1, 2 * windows[-1].shape[0] * count)
        ]
        + [
            VMEM((leaves, rows, rank), F32), VMEM((leaves // 2, rows, rank), F32),
            VMEM((count, rows, rank), BF), DMA((4,)),
        ],
        (150_000_000, 20_000_000), 16 * 1024 * 1024,
    )


def on_device(
    vectors,
    leaf_basis,
    leaf_transfer,
    pair_transfer,
    near_blocks,
    near_offset,
    leaf_send,
    leaf_list,
    leaf_coupling,
    pair_send,
    pair_list,
    pair_coupling,
    top_list,
    top_coupling,
):
    rows = lax.axis_size("row")
    devs = rows * lax.axis_size("col")
    cap0, cap1 = leaf_send.shape[2], pair_send.shape[2]
    lsend = jnp.transpose(leaf_send, (1, 0, 2))
    psend = jnp.transpose(pair_send, (0, 2, 1))
    tops, own, sib, cross, fwd, back = up_pass(
        lsend, psend, vectors, leaf_basis, leaf_transfer, pair_transfer, rows
    )
    ring = range(devs)
    sibling = [(d, d ^ 1) for d in ring]
    mine = lax.all_to_all(tops, "row", split_axis=0, concat_axis=0)
    theirs = lax.ppermute(mine, AXES, sibling)
    sib = lax.ppermute(sib, AXES, sibling)
    cross = lax.ppermute(cross, AXES, [(d, (d + 1 if d % 2 else d - 1) % devs) for d in ring])
    fwd = lax.ppermute(fwd, AXES, [(d, (d + 2) % devs) for d in ring])
    back = lax.ppermute(back, AXES, [(d, (d - 2) % devs) for d in ring])
    close, ends = near_pass(near_offset.T, vectors, near_blocks)
    return rest_pass(
        (leaf_list.T, pair_list.T, top_list, near_offset.T),
        (leaf_coupling, pair_coupling, top_coupling, ends, pair_transfer, leaf_transfer, leaf_basis, close),
        (own, sib, cross, fwd, back, mine, theirs), cap0, cap1,
    )


def solution(mesh):
    placed = P(("groups", "row", "col"))
    behind = P(None, ("groups", "row", "col"))
    return jax.shard_map(
        on_device,
        mesh=mesh,
        in_specs=(
            placed, placed, placed, placed, behind, placed, placed, placed, behind, placed, placed, behind, placed, behind,
        ),
        out_specs=behind,
        check_vma=False,
    )
```

```python
import jax
import jax.numpy as jnp
from jax import lax
from jax.experimental import pallas as pl
from jax.experimental.pallas import tpu as pltpu
from jax.sharding import PartitionSpec as P

REACH = 2
WIN = 2 * REACH + 1
HW = 2
GROUP = 8
AXES = ("row", "col")
F32 = jnp.float32
BF = jnp.bfloat16
LIMIT = 56 * 1024 * 1024

VMEM = pltpu.VMEM
SMEM = pltpu.SMEM
DMA = pltpu.SemaphoreType.DMA
FIXED = pl.BlockSpec(memory_space=pltpu.HBM)
WHOLE = pl.BlockSpec(memory_space=VMEM)


def dot(left, right):
    return jnp.dot(left, right, preferred_element_type=F32)


def beside(*parts):
    return jnp.concatenate(parts, axis=1)


def above(*parts):
    return jnp.concatenate(parts, axis=0)


def dot_t(left, right):
    return lax.dot_general(left, right, (((1,), (1,)), ((), ())), preferred_element_type=F32)


def row_of_blocks(ref, q):
    kernels, _, partners, _, _ = ref.shape
    return beside(*[above(*[ref[k, q, m] for k in range(kernels)]) for m in range(partners)])


def by_kernel(wide, rank):
    return above(*[wide[:, k * rank:(k + 1) * rank] for k in range(wide.shape[1] // rank)])


def copies(pairs, sems):
    made = [pltpu.make_async_copy(src, dst, sems.at[i]) for i, (src, dst) in enumerate(pairs)]
    for copy in made:
        copy.start()
    return made


def split(row, ref, at):
    rank = row.shape[1] // 2
    ref[at] = row[:, :rank]
    ref[at + 1] = row[:, rank:]


def call(body, name, params, arrays, out_shape, out_specs, scratch, cost, limit=LIMIT):
    return pl.pallas_call(
        body,
        out_shape=out_shape,
        in_specs=[FIXED] * len(params) + [WHOLE] * len(arrays),
        out_specs=out_specs,
        scratch_shapes=scratch,
        compiler_params=pltpu.CompilerParams(vmem_limit_bytes=limit),
        cost_estimate=pl.CostEstimate(flops=cost[0], bytes_accessed=cost[1], transcendentals=0),
        name=name,
    )(*params, *arrays)


def like(x):
    return VMEM(x.shape, x.dtype)


def held(x):
    return SMEM(x.shape, x.dtype)


def up_body(vec_h, basis_h, ltr_h, ptr_h, lsend_h, psend_h, tops, own, sib, cross, fwd, back,
            vec, basis, ltr, ptr, lsend, psend, low, mid, sems):
    leaves, vecs, rank = vec.shape
    col = lax.axis_index("col")
    cap0 = lsend.shape[2]
    cap1 = psend.shape[1]
    made = copies(
        [(vec_h, vec), (basis_h, basis), (ltr_h, ltr), (ptr_h, ptr), (lsend_h, lsend), (psend_h, psend)], sems
    )
    made[0].wait()
    made[1].wait()
    for t in range(leaves):
        low[t] = dot(vec[t], basis[t]).astype(BF)
    made[2].wait()
    for j in range(leaves // 2):
        mid[j] = dot(
            beside(low[2 * j], low[2 * j + 1]), ltr[2 * j:2 * j + 2].reshape(2 * rank, rank)
        ).astype(BF)
    made[3].wait()
    high = []
    for i in range(leaves // 4):
        high.append(
            dot(beside(mid[2 * i], mid[2 * i + 1]), ptr[2 * i:2 * i + 2].reshape(2 * rank, rank)).astype(BF)
        )
    for i in range(leaves // 8):
        tops[i] = beside(high[2 * i], high[2 * i + 1])
    made[4].wait()
    made[5].wait()

    def pack(out, place):
        for c in range(cap0 // 2):
            out[c] = beside(low[lsend[place, 0, 2 * c]], low[lsend[place, 0, 2 * c + 1]])
        for c in range(cap1 // 2):
            out[cap0 // 2 + c] = beside(mid[psend[0, 2 * c, place]], mid[psend[0, 2 * c + 1, place]])

    def pack_halo(out, start):
        out[(cap0 + cap1) // 2] = beside(vec[start], vec[start + 1])

    pack(sib, 1 + 2 * col)
    pack_halo(sib, (1 - col) * (leaves - HW))
    pack(cross, 3 - 2 * col)
    pack_halo(cross, col * (leaves - HW))
    pack(fwd, 0)
    pack(back, 4)
    pack(own, REACH)


def up_pass(lsend, psend, vec, basis, ltr, ptr):
    leaves, vecs, rank = vec.shape
    count = (lsend.shape[2] + psend.shape[1]) // 2
    shape = lambda *n: jax.ShapeDtypeStruct(n + (vecs, 2 * rank), BF)
    return call(
        up_body, "up", (vec, basis, ltr, ptr, lsend, psend), (),
        [shape(leaves // 8), shape(count), shape(count + 1), shape(count + 1), shape(count), shape(count)],
        [WHOLE] * 6,
        [
            like(vec), like(basis), like(ltr), like(ptr), held(lsend), held(psend),
            VMEM((leaves, vecs, rank), BF), VMEM((leaves // 2, vecs, rank), BF), DMA((6,)),
        ],
        (10_000_000, 3_000_000),
    )


def spread_body(top, out):
    for row in range(out.shape[0]):
        out[row] = top[...]


def spread_pass(top, rows):
    return call(
        spread_body, "spread", (), (top,), jax.ShapeDtypeStruct((rows,) + top.shape, top.dtype), WHOLE, [],
        (4_000_000_000, 60_000_000), 4 * 1024 * 1024,
    )


def near_body(offsets_h, vec, near, close, ends, padded, offsets, sems):
    leaves, vecs, rank = vec.shape
    kernels = near.shape[0]
    made = copies([(offsets_h, offsets)], sems)
    ends[:, 0:HW] = near[:, 0:HW]
    ends[:, HW:] = near[:, leaves - HW:]
    zero = jnp.zeros((HW, vecs, rank), BF)
    padded[0:HW] = zero
    padded[HW:HW + leaves] = vec[...]
    padded[HW + leaves:] = zero
    made[0].wait()

    def body(c, _):
        for q in range(GROUP):
            t = c * GROUP + q
            total = None
            for n in range(near.shape[2]):
                part = dot_t(padded[t + HW + offsets[n, t]], above(*[near[k, t, n] for k in range(kernels)]))
                total = part if total is None else total + part
            close[t] = by_kernel(total, rank)
        return 0

    lax.fori_loop(0, leaves // GROUP, body, 0)


def near_pass(offsets, vec, blocks):
    kernels, leaves, near, rank, _ = blocks.shape
    vecs = vec.shape[1]
    return call(
        near_body, "near", (offsets,), (vec, blocks),
        [
            jax.ShapeDtypeStruct((leaves, kernels * vecs, rank), F32),
            jax.ShapeDtypeStruct((kernels, 2 * HW) + blocks.shape[2:], BF),
        ],
        [WHOLE] * 2,
        [VMEM((leaves + 2 * HW, vecs, rank), BF), held(offsets), DMA((1,))],
        (4_000_000_000, 60_000_000), 8 * 1024 * 1024,
    )


def far_sum(rows, blocks, q):
    return dot_t(beside(*rows), row_of_blocks(blocks, q))


def rest_body(llist_h, plist_h, tlist_h, offsets_h,
              leaf, pair, coupling, ends, ptr, ltr, basis, close, own, sib, cross, fwd, back, mine, theirs, out,
              llist, plist, tlist, offsets, wleaf, wpair, halo, tops, far0, far1, down, sems):
    kernels, leaves, partners, rank, _ = leaf.shape
    _, vecs, _ = wleaf.shape
    count = coupling.shape[1]
    cap0 = wleaf.shape[0] // WIN
    cap1 = wpair.shape[0] // WIN
    base = own.shape[0] - cap1 // 2
    col = lax.axis_index("col")
    place = lax.axis_index("row") * lax.axis_size("col") + col
    last_place = lax.axis_size("row") * lax.axis_size("col") - 1
    lists = copies([(llist_h, llist), (plist_h, plist), (tlist_h, tlist), (offsets_h, offsets)], sems)

    for block, slot in ((own, REACH), (fwd, 0), (back, 4), (sib, 3 - 2 * col), (cross, 1 + 2 * col)):
        for c in range(cap0 // 2):
            split(block[c], wleaf, slot * cap0 + 2 * c)
        for c in range(cap1 // 2):
            split(block[base + c], wpair, slot * cap1 + 2 * c)
    halo[2 * HW] = jnp.zeros((vecs, rank), BF)
    for block, upper in ((sib, 1 - col), (cross, col)):
        row = block[base + cap1 // 2]
        outside = (place == 0) & (upper == 0) | (place == last_place) & (upper == 1)
        split(jnp.where(outside, jnp.zeros_like(row), row), halo, upper * HW)
    for block, side in ((mine, col), (theirs, 1 - col)):
        for s in range(block.shape[0]):
            for i in range(block.shape[1]):
                split(block[s, i], tops, (s * 2 + side) * count + 2 * i)
    for copy in lists:
        copy.wait()

    def body(c, _):
        for q in range(GROUP):
            t = c * GROUP + q
            far0[t] = by_kernel(far_sum([wleaf[llist[m, t]] for m in range(partners)], leaf, t), rank)
        for q in range(GROUP // 2):
            j = c * (GROUP // 2) + q
            far1[j] = by_kernel(far_sum([wpair[plist[m, j]] for m in range(pair.shape[2])], pair, j), rank)
        for q in range(GROUP // 4):
            i = c * (GROUP // 4) + q
            rows = [tops[tlist[i, m]] for m in range(coupling.shape[2])]
            down[i] = by_kernel(far_sum(rows, coupling, i), rank).astype(BF)
        return 0

    lax.fori_loop(0, leaves // GROUP, body, 0)

    def edge(t):
        spots = [t + offsets[n, t] for n in range(ends.shape[2])]
        if t < HW:
            spots = [jnp.where(at < 0, at + HW, 2 * HW) for at in spots]
        else:
            spots = [jnp.where(at >= leaves, at - leaves + HW, 2 * HW) for at in spots]
        return by_kernel(far_sum([halo[at] for at in spots], ends, t if t < HW else t - (leaves - 2 * HW)), rank)

    down1 = []
    for j in range(2 * count):
        down1.append((far1[j] + dot_t(down[j // 2], ptr[j])).astype(BF))
    down0 = []
    for t in range(leaves):
        down0.append((far0[t] + dot_t(down1[t // 2], ltr[t])).astype(BF))
    for t in range(leaves):
        points = dot_t(down0[t], basis[t]) + close[t]
        if t < HW or t >= leaves - HW:
            points = points + edge(t)
        points = points.astype(BF)
        for k in range(kernels):
            out[k, t] = points[k * vecs:(k + 1) * vecs]


def rest_pass(lists, arrays, windows, cap0, cap1):
    leaf, pair, coupling = arrays[:3]
    kernels, leaves, _, rank, _ = leaf.shape
    count = coupling.shape[1]
    vecs = windows[0].shape[1]
    rows = kernels * vecs
    return call(
        rest_body, "rest", lists, arrays + windows,
        jax.ShapeDtypeStruct((kernels, leaves, vecs, rank), BF),
        WHOLE,
        [held(x) for x in lists]
        + [
            VMEM((n, vecs, rank), BF)
            for n in (WIN * cap0, WIN * cap1, 2 * HW + 1, 2 * windows[-1].shape[0] * count)
        ]
        + [
            VMEM((leaves, rows, rank), F32), VMEM((leaves // 2, rows, rank), F32),
            VMEM((count, rows, rank), BF), DMA((4,)),
        ],
        (150_000_000, 20_000_000), 16 * 1024 * 1024,
    )


def on_device(
    vectors,
    leaf_basis,
    leaf_transfer,
    pair_transfer,
    near_blocks,
    near_offset,
    leaf_send,
    leaf_list,
    leaf_coupling,
    pair_send,
    pair_list,
    pair_coupling,
    top_list,
    top_coupling,
):
    rows = lax.axis_size("row")
    devs = rows * lax.axis_size("col")
    cap0, cap1 = leaf_send.shape[2], pair_send.shape[2]
    lsend = jnp.transpose(leaf_send, (1, 0, 2))
    psend = jnp.transpose(pair_send, (0, 2, 1))
    tops, own, sib, cross, fwd, back = up_pass(
        lsend, psend, vectors, leaf_basis, leaf_transfer, pair_transfer
    )
    ring = range(devs)
    sibling = [(d, d ^ 1) for d in ring]
    mine = lax.all_to_all(spread_pass(tops, rows), "row", split_axis=0, concat_axis=0)
    theirs = lax.ppermute(mine, AXES, sibling)
    sib = lax.ppermute(sib, AXES, sibling)
    cross = lax.ppermute(cross, AXES, [(d, (d + 1 if d % 2 else d - 1) % devs) for d in ring])
    fwd = lax.ppermute(fwd, AXES, [(d, (d + 2) % devs) for d in ring])
    back = lax.ppermute(back, AXES, [(d, (d - 2) % devs) for d in ring])
    close, ends = near_pass(near_offset.T, vectors, near_blocks)
    return rest_pass(
        (leaf_list.T, pair_list.T, top_list, near_offset.T),
        (leaf_coupling, pair_coupling, top_coupling, ends, pair_transfer, leaf_transfer, leaf_basis, close),
        (own, sib, cross, fwd, back, mine, theirs), cap0, cap1,
    )


def solution(mesh):
    placed = P(("groups", "row", "col"))
    behind = P(None, ("groups", "row", "col"))
    return jax.shard_map(
        on_device,
        mesh=mesh,
        in_specs=(
            placed, placed, placed, placed, behind, placed, placed, placed, behind, placed, placed, behind, placed, behind,
        ),
        out_specs=behind,
        check_vma=False,
    )
```

```python
import jax
import jax.numpy as jnp
from jax import lax
from jax.experimental import pallas as pl
from jax.experimental.pallas import tpu as pltpu
from jax.sharding import PartitionSpec as P

REACH = 2
WIN = 2 * REACH + 1
HW = 2
GROUP = 8
AXES = ("row", "col")
F32 = jnp.float32
BF = jnp.bfloat16
LIMIT = 56 * 1024 * 1024

VMEM = pltpu.VMEM
SMEM = pltpu.SMEM
DMA = pltpu.SemaphoreType.DMA
FIXED = pl.BlockSpec(memory_space=pltpu.HBM)
WHOLE = pl.BlockSpec(memory_space=VMEM)


def dot(left, right):
    return jnp.dot(left, right, preferred_element_type=F32)


def beside(*parts):
    return jnp.concatenate(parts, axis=1)


def above(*parts):
    return jnp.concatenate(parts, axis=0)


def dot_t(left, right):
    return lax.dot_general(left, right, (((1,), (1,)), ((), ())), preferred_element_type=F32)


def row_of_blocks(ref, q):
    kernels, _, partners, _, _ = ref.shape
    return beside(*[above(*[ref[k, q, m] for k in range(kernels)]) for m in range(partners)])


def by_kernel(wide, rank):
    return above(*[wide[:, k * rank:(k + 1) * rank] for k in range(wide.shape[1] // rank)])


def copies(pairs, sems):
    made = [pltpu.make_async_copy(src, dst, sems.at[i]) for i, (src, dst) in enumerate(pairs)]
    for copy in made:
        copy.start()
    return made


def split(row, ref, at):
    rank = row.shape[1] // 2
    ref[at] = row[:, :rank]
    ref[at + 1] = row[:, rank:]


def call(body, name, params, arrays, out_shape, out_specs, scratch, cost, limit=LIMIT):
    return pl.pallas_call(
        body,
        out_shape=out_shape,
        in_specs=[FIXED] * len(params) + [WHOLE] * len(arrays),
        out_specs=out_specs,
        scratch_shapes=scratch,
        compiler_params=pltpu.CompilerParams(vmem_limit_bytes=limit),
        cost_estimate=pl.CostEstimate(flops=cost[0], bytes_accessed=cost[1], transcendentals=0),
        name=name,
    )(*params, *arrays)


def like(x):
    return VMEM(x.shape, x.dtype)


def held(x):
    return SMEM(x.shape, x.dtype)


def up_body(vec_h, basis_h, ltr_h, ptr_h, lsend_h, psend_h, tops, own, windows,
            vec, basis, ltr, ptr, lsend, psend, low, mid, sems):
    leaves, vecs, rank = vec.shape
    col = lax.axis_index("col")
    cap0 = lsend.shape[2]
    cap1 = psend.shape[1]
    made = copies(
        [(vec_h, vec), (basis_h, basis), (ltr_h, ltr), (ptr_h, ptr), (lsend_h, lsend), (psend_h, psend)], sems
    )
    made[0].wait()
    made[1].wait()
    for t in range(leaves):
        low[t] = dot(vec[t], basis[t]).astype(BF)
    made[2].wait()
    for j in range(leaves // 2):
        mid[j] = dot(
            beside(low[2 * j], low[2 * j + 1]), ltr[2 * j:2 * j + 2].reshape(2 * rank, rank)
        ).astype(BF)
    made[3].wait()
    high = []
    for i in range(leaves // 4):
        high.append(
            dot(beside(mid[2 * i], mid[2 * i + 1]), ptr[2 * i:2 * i + 2].reshape(2 * rank, rank)).astype(BF)
        )
    for i in range(leaves // 8):
        both = beside(high[2 * i], high[2 * i + 1])
        for row in range(tops.shape[0]):
            tops[row, i] = both
    made[4].wait()
    made[5].wait()

    sib, cross, fwd, back = [windows.at[i] for i in range(4)]

    def pack(out, place):
        for c in range(cap0 // 2):
            out[c] = beside(low[lsend[place, 0, 2 * c]], low[lsend[place, 0, 2 * c + 1]])
        for c in range(cap1 // 2):
            out[cap0 // 2 + c] = beside(mid[psend[0, 2 * c, place]], mid[psend[0, 2 * c + 1, place]])

    def pack_halo(out, start):
        out[(cap0 + cap1) // 2] = beside(vec[start], vec[start + 1])

    pack(sib, 1 + 2 * col)
    pack_halo(sib, (1 - col) * (leaves - HW))
    pack(cross, 3 - 2 * col)
    pack_halo(cross, col * (leaves - HW))
    pack(fwd, 0)
    pack(back, 4)
    pack(own, REACH)


def up_pass(lsend, psend, vec, basis, ltr, ptr, rows):
    leaves, vecs, rank = vec.shape
    count = (lsend.shape[2] + psend.shape[1]) // 2
    shape = lambda *n: jax.ShapeDtypeStruct(n + (vecs, 2 * rank), BF)
    return call(
        up_body, "up", (vec, basis, ltr, ptr, lsend, psend), (),
        [shape(rows, leaves // 8), shape(count), shape(4, count + 1)],
        [WHOLE] * 3,
        [
            like(vec), like(basis), like(ltr), like(ptr), held(lsend), held(psend),
            VMEM((leaves, vecs, rank), BF), VMEM((leaves // 2, vecs, rank), BF), DMA((6,)),
        ],
        (10_000_000, 3_000_000),
    )


def hand_body(windows, *outs):
    for i, out in enumerate(outs):
        out[...] = windows[i, :out.shape[0]]


def hand_pass(windows, counts):
    shape = windows.shape[2:]
    return call(
        hand_body, "hand", (), (windows,),
        [jax.ShapeDtypeStruct((n,) + shape, windows.dtype) for n in counts],
        [WHOLE] * len(counts), [], (8_000_000_000, 100_000_000), 2 * 1024 * 1024,
    )


def far_sum(rows, blocks, q):
    return dot_t(beside(*rows), row_of_blocks(blocks, q))


def rest_body(llist_h, plist_h, tlist_h, offsets_h,
              leaf, pair, coupling, near, ptr, ltr, basis, vec, own, sib, cross, fwd, back, mine, theirs, out,
              llist, plist, tlist, offsets, wleaf, wpair, padded, tops, far0, far1, close, down, sems):
    kernels, leaves, partners, rank, _ = leaf.shape
    _, vecs, _ = wleaf.shape
    count = coupling.shape[1]
    cap0 = wleaf.shape[0] // WIN
    cap1 = wpair.shape[0] // WIN
    base = own.shape[0] - cap1 // 2
    col = lax.axis_index("col")
    place = lax.axis_index("row") * lax.axis_size("col") + col
    last_place = lax.axis_size("row") * lax.axis_size("col") - 1
    lists = copies([(llist_h, llist), (plist_h, plist), (tlist_h, tlist), (offsets_h, offsets)], sems)

    for block, slot in ((own, REACH), (fwd, 0), (back, 4), (sib, 3 - 2 * col), (cross, 1 + 2 * col)):
        for c in range(cap0 // 2):
            split(block[c], wleaf, slot * cap0 + 2 * c)
        for c in range(cap1 // 2):
            split(block[base + c], wpair, slot * cap1 + 2 * c)
    padded[HW:HW + leaves] = vec[...]
    for block, upper in ((sib, 1 - col), (cross, col)):
        row = block[base + cap1 // 2]
        outside = (place == 0) & (upper == 0) | (place == last_place) & (upper == 1)
        split(jnp.where(outside, jnp.zeros_like(row), row), padded, upper * (HW + leaves))
    for block, side in ((mine, col), (theirs, 1 - col)):
        for s in range(block.shape[0]):
            for i in range(block.shape[1]):
                split(block[s, i], tops, (s * 2 + side) * count + 2 * i)
    for copy in lists:
        copy.wait()

    def body(c, _):
        for q in range(GROUP):
            t = c * GROUP + q
            rows = [padded[t + HW + offsets[n, t]] for n in range(near.shape[2])]
            close[t] = by_kernel(far_sum(rows, near, t), rank)
            far0[t] = by_kernel(far_sum([wleaf[llist[m, t]] for m in range(partners)], leaf, t), rank)
        for q in range(GROUP // 2):
            j = c * (GROUP // 2) + q
            far1[j] = by_kernel(far_sum([wpair[plist[m, j]] for m in range(pair.shape[2])], pair, j), rank)
        for q in range(GROUP // 4):
            i = c * (GROUP // 4) + q
            rows = [tops[tlist[i, m]] for m in range(coupling.shape[2])]
            down[i] = by_kernel(far_sum(rows, coupling, i), rank).astype(BF)
        return 0

    lax.fori_loop(0, leaves // GROUP, body, 0)

    down1 = []
    for j in range(2 * count):
        down1.append((far1[j] + dot_t(down[j // 2], ptr[j])).astype(BF))
    down0 = []
    for t in range(leaves):
        down0.append((far0[t] + dot_t(down1[t // 2], ltr[t])).astype(BF))
    for t in range(leaves):
        points = (dot_t(down0[t], basis[t]) + close[t]).astype(BF)
        for k in range(kernels):
            out[k, t] = points[k * vecs:(k + 1) * vecs]


def rest_pass(lists, arrays, windows, cap0, cap1):
    leaf, pair, coupling = arrays[:3]
    kernels, leaves, _, rank, _ = leaf.shape
    count = coupling.shape[1]
    vecs = windows[0].shape[1]
    rows = kernels * vecs
    return call(
        rest_body, "rest", lists, arrays + windows,
        jax.ShapeDtypeStruct((kernels, leaves, vecs, rank), BF),
        WHOLE,
        [held(x) for x in lists]
        + [
            VMEM((n, vecs, rank), BF)
            for n in (WIN * cap0, WIN * cap1, 2 * HW + leaves, 2 * windows[-1].shape[0] * count)
        ]
        + [
            VMEM((leaves, rows, rank), F32), VMEM((leaves // 2, rows, rank), F32), VMEM((leaves, rows, rank), F32),
            VMEM((count, rows, rank), BF), DMA((4,)),
        ],
        (150_000_000, 20_000_000), 16 * 1024 * 1024,
    )


def on_device(
    vectors,
    leaf_basis,
    leaf_transfer,
    pair_transfer,
    near_blocks,
    near_offset,
    leaf_send,
    leaf_list,
    leaf_coupling,
    pair_send,
    pair_list,
    pair_coupling,
    top_list,
    top_coupling,
):
    rows = lax.axis_size("row")
    devs = rows * lax.axis_size("col")
    cap0, cap1 = leaf_send.shape[2], pair_send.shape[2]
    lsend = jnp.transpose(leaf_send, (1, 0, 2))
    psend = jnp.transpose(pair_send, (0, 2, 1))
    tops, own, windows = up_pass(
        lsend, psend, vectors, leaf_basis, leaf_transfer, pair_transfer, rows
    )
    count = own.shape[0]
    sib, cross, fwd, back = hand_pass(windows, (count + 1, count + 1, count, count))
    ring = range(devs)
    sibling = [(d, d ^ 1) for d in ring]
    mine = lax.all_to_all(tops, "row", split_axis=0, concat_axis=0)
    theirs = lax.ppermute(mine, AXES, sibling)
    sib = lax.ppermute(sib, AXES, sibling)
    cross = lax.ppermute(cross, AXES, [(d, (d + 1 if d % 2 else d - 1) % devs) for d in ring])
    fwd = lax.ppermute(fwd, AXES, [(d, (d + 2) % devs) for d in ring])
    back = lax.ppermute(back, AXES, [(d, (d - 2) % devs) for d in ring])
    return rest_pass(
        (leaf_list.T, pair_list.T, top_list, near_offset.T),
        (leaf_coupling, pair_coupling, top_coupling, near_blocks, pair_transfer, leaf_transfer, leaf_basis, vectors),
        (own, sib, cross, fwd, back, mine, theirs), cap0, cap1,
    )


def solution(mesh):
    placed = P(("groups", "row", "col"))
    behind = P(None, ("groups", "row", "col"))
    return jax.shard_map(
        on_device,
        mesh=mesh,
        in_specs=(
            placed, placed, placed, placed, behind, placed, placed, placed, behind, placed, placed, behind, placed, behind,
        ),
        out_specs=behind,
        check_vma=False,
    )
```

```python
import jax
import jax.numpy as jnp
from jax import lax
from jax.experimental import pallas as pl
from jax.experimental.pallas import tpu as pltpu
from jax.sharding import PartitionSpec as P

REACH = 2
WIN = 2 * REACH + 1
HW = 2
GROUP = 8
AXES = ("row", "col")
F32 = jnp.float32
BF = jnp.bfloat16
LIMIT = 56 * 1024 * 1024

VMEM = pltpu.VMEM
SMEM = pltpu.SMEM
DMA = pltpu.SemaphoreType.DMA
FIXED = pl.BlockSpec(memory_space=pltpu.HBM)
WHOLE = pl.BlockSpec(memory_space=VMEM)


def dot(left, right):
    return jnp.dot(left, right, preferred_element_type=F32)


def beside(*parts):
    return jnp.concatenate(parts, axis=1)


def above(*parts):
    return jnp.concatenate(parts, axis=0)


def dot_t(left, right):
    return lax.dot_general(left, right, (((1,), (1,)), ((), ())), preferred_element_type=F32)


def row_of_blocks(ref, q):
    kernels, _, partners, _, _ = ref.shape
    return beside(*[above(*[ref[k, q, m] for k in range(kernels)]) for m in range(partners)])


def by_kernel(wide, rank):
    return above(*[wide[:, k * rank:(k + 1) * rank] for k in range(wide.shape[1] // rank)])


def copies(pairs, sems):
    made = [pltpu.make_async_copy(src, dst, sems.at[i]) for i, (src, dst) in enumerate(pairs)]
    for copy in made:
        copy.start()
    return made


def split(row, ref, at):
    rank = row.shape[1] // 2
    ref[at] = row[:, :rank]
    ref[at + 1] = row[:, rank:]


def call(body, name, params, arrays, out_shape, out_specs, scratch, cost, limit=LIMIT):
    return pl.pallas_call(
        body,
        out_shape=out_shape,
        in_specs=[FIXED] * len(params) + [WHOLE] * len(arrays),
        out_specs=out_specs,
        scratch_shapes=scratch,
        compiler_params=pltpu.CompilerParams(vmem_limit_bytes=limit),
        cost_estimate=pl.CostEstimate(flops=cost[0], bytes_accessed=cost[1], transcendentals=0),
        name=name,
    )(*params, *arrays)


def like(x):
    return VMEM(x.shape, x.dtype)


def held(x):
    return SMEM(x.shape, x.dtype)


def up_body(vec_h, basis_h, ltr_h, ptr_h, lsend_h, psend_h, tops, own, windows,
            vec, basis, ltr, ptr, lsend, psend, low, mid, sems):
    leaves, vecs, rank = vec.shape
    col = lax.axis_index("col")
    cap0 = lsend.shape[2]
    cap1 = psend.shape[1]
    made = copies(
        [(vec_h, vec), (basis_h, basis), (ltr_h, ltr), (ptr_h, ptr), (lsend_h, lsend), (psend_h, psend)], sems
    )
    made[0].wait()
    made[1].wait()
    for t in range(leaves):
        low[t] = dot(vec[t], basis[t]).astype(BF)
    made[2].wait()
    for j in range(leaves // 2):
        mid[j] = dot(
            beside(low[2 * j], low[2 * j + 1]), ltr[2 * j:2 * j + 2].reshape(2 * rank, rank)
        ).astype(BF)
    made[3].wait()
    high = []
    for i in range(leaves // 4):
        high.append(
            dot(beside(mid[2 * i], mid[2 * i + 1]), ptr[2 * i:2 * i + 2].reshape(2 * rank, rank)).astype(BF)
        )
    for i in range(leaves // 8):
        both = beside(high[2 * i], high[2 * i + 1])
        for row in range(tops.shape[0]):
            tops[row, i] = both
    made[4].wait()
    made[5].wait()

    sib, cross, fwd, back = [windows.at[i] for i in range(4)]

    def pack(out, place):
        for c in range(cap0 // 2):
            out[c] = beside(low[lsend[place, 0, 2 * c]], low[lsend[place, 0, 2 * c + 1]])
        for c in range(cap1 // 2):
            out[cap0 // 2 + c] = beside(mid[psend[0, 2 * c, place]], mid[psend[0, 2 * c + 1, place]])

    def pack_halo(out, start):
        out[(cap0 + cap1) // 2] = beside(vec[start], vec[start + 1])

    pack(sib, 1 + 2 * col)
    pack_halo(sib, (1 - col) * (leaves - HW))
    pack(cross, 3 - 2 * col)
    pack_halo(cross, col * (leaves - HW))
    pack(fwd, 0)
    pack(back, 4)
    pack(own, REACH)


def up_pass(lsend, psend, vec, basis, ltr, ptr, rows):
    leaves, vecs, rank = vec.shape
    count = (lsend.shape[2] + psend.shape[1]) // 2
    shape = lambda *n: jax.ShapeDtypeStruct(n + (vecs, 2 * rank), BF)
    return call(
        up_body, "up", (vec, basis, ltr, ptr, lsend, psend), (),
        [shape(rows, leaves // 8), shape(count), shape(4, count + 1)],
        [WHOLE] * 3,
        [
            like(vec), like(basis), like(ltr), like(ptr), held(lsend), held(psend),
            VMEM((leaves, vecs, rank), BF), VMEM((leaves // 2, vecs, rank), BF), DMA((6,)),
        ],
        (10_000_000, 3_000_000),
    )


def hand_body(windows, *outs):
    for i, out in enumerate(outs):
        out[...] = windows[i, :out.shape[0]]


def hand_pass(windows, counts):
    shape = windows.shape[2:]
    return call(
        hand_body, "hand", (), (windows,),
        [jax.ShapeDtypeStruct((n,) + shape, windows.dtype) for n in counts],
        [WHOLE] * len(counts), [], (8_000_000_000, 100_000_000), 2 * 1024 * 1024,
    )


def near_body(offsets_h, vec, near, close, ends, padded, offsets, sems):
    leaves, vecs, rank = vec.shape
    kernels = near.shape[0]
    made = copies([(offsets_h, offsets)], sems)
    ends[:, 0:HW] = near[:, 0:HW]
    ends[:, HW:] = near[:, leaves - HW:]
    zero = jnp.zeros((HW, vecs, rank), BF)
    padded[0:HW] = zero
    padded[HW:HW + leaves] = vec[...]
    padded[HW + leaves:] = zero
    made[0].wait()

    def body(c, _):
        for q in range(GROUP):
            t = c * GROUP + q
            rows = [padded[t + HW + offsets[n, t]] for n in range(near.shape[2])]
            close[t] = by_kernel(far_sum(rows, near, t), rank)
        return 0

    lax.fori_loop(0, leaves // GROUP, body, 0)


def near_pass(offsets, vec, blocks):
    kernels, leaves, near, rank, _ = blocks.shape
    vecs = vec.shape[1]
    return call(
        near_body, "near", (offsets,), (vec, blocks),
        [
            jax.ShapeDtypeStruct((leaves, kernels * vecs, rank), F32),
            jax.ShapeDtypeStruct((kernels, 2 * HW) + blocks.shape[2:], BF),
        ],
        [WHOLE] * 2,
        [VMEM((leaves + 2 * HW, vecs, rank), BF), held(offsets), DMA((1,))],
        (4_000_000_000, 60_000_000), 8 * 1024 * 1024,
    )


def far_sum(rows, blocks, q):
    return dot_t(beside(*rows), row_of_blocks(blocks, q))


def rest_body(llist_h, plist_h, tlist_h, offsets_h,
              leaf, pair, coupling, ends, ptr, ltr, basis, close, own, sib, cross, fwd, back, mine, theirs, out,
              llist, plist, tlist, offsets, wleaf, wpair, halo, tops, far0, far1, down, sems):
    kernels, leaves, partners, rank, _ = leaf.shape
    _, vecs, _ = wleaf.shape
    count = coupling.shape[1]
    cap0 = wleaf.shape[0] // WIN
    cap1 = wpair.shape[0] // WIN
    base = own.shape[0] - cap1 // 2
    col = lax.axis_index("col")
    place = lax.axis_index("row") * lax.axis_size("col") + col
    last_place = lax.axis_size("row") * lax.axis_size("col") - 1
    lists = copies([(llist_h, llist), (plist_h, plist), (tlist_h, tlist), (offsets_h, offsets)], sems)

    for block, slot in ((own, REACH), (fwd, 0), (back, 4), (sib, 3 - 2 * col), (cross, 1 + 2 * col)):
        for c in range(cap0 // 2):
            split(block[c], wleaf, slot * cap0 + 2 * c)
        for c in range(cap1 // 2):
            split(block[base + c], wpair, slot * cap1 + 2 * c)
    halo[2 * HW] = jnp.zeros((vecs, rank), BF)
    for block, upper in ((sib, 1 - col), (cross, col)):
        row = block[base + cap1 // 2]
        outside = (place == 0) & (upper == 0) | (place == last_place) & (upper == 1)
        split(jnp.where(outside, jnp.zeros_like(row), row), halo, upper * HW)
    for block, side in ((mine, col), (theirs, 1 - col)):
        for s in range(block.shape[0]):
            for i in range(block.shape[1]):
                split(block[s, i], tops, (s * 2 + side) * count + 2 * i)
    for copy in lists:
        copy.wait()

    def body(c, _):
        for q in range(GROUP):
            t = c * GROUP + q
            far0[t] = by_kernel(far_sum([wleaf[llist[m, t]] for m in range(partners)], leaf, t), rank)
        for q in range(GROUP // 2):
            j = c * (GROUP // 2) + q
            far1[j] = by_kernel(far_sum([wpair[plist[m, j]] for m in range(pair.shape[2])], pair, j), rank)
        for q in range(GROUP // 4):
            i = c * (GROUP // 4) + q
            rows = [tops[tlist[i, m]] for m in range(coupling.shape[2])]
            down[i] = by_kernel(far_sum(rows, coupling, i), rank).astype(BF)
        return 0

    lax.fori_loop(0, leaves // GROUP, body, 0)

    def edge(t):
        spots = [t + offsets[n, t] for n in range(ends.shape[2])]
        if t < HW:
            spots = [jnp.where(at < 0, at + HW, 2 * HW) for at in spots]
        else:
            spots = [jnp.where(at >= leaves, at - leaves + HW, 2 * HW) for at in spots]
        return by_kernel(far_sum([halo[at] for at in spots], ends, t if t < HW else t - (leaves - 2 * HW)), rank)

    down1 = []
    for j in range(2 * count):
        down1.append((far1[j] + dot_t(down[j // 2], ptr[j])).astype(BF))
    down0 = []
    for t in range(leaves):
        down0.append((far0[t] + dot_t(down1[t // 2], ltr[t])).astype(BF))
    for t in range(leaves):
        points = dot_t(down0[t], basis[t]) + close[t]
        if t < HW or t >= leaves - HW:
            points = points + edge(t)
        points = points.astype(BF)
        for k in range(kernels):
            out[k, t] = points[k * vecs:(k + 1) * vecs]


def rest_pass(lists, arrays, windows, cap0, cap1):
    leaf, pair, coupling = arrays[:3]
    kernels, leaves, _, rank, _ = leaf.shape
    count = coupling.shape[1]
    vecs = windows[0].shape[1]
    rows = kernels * vecs
    return call(
        rest_body, "rest", lists, arrays + windows,
        jax.ShapeDtypeStruct((kernels, leaves, vecs, rank), BF),
        WHOLE,
        [held(x) for x in lists]
        + [
            VMEM((n, vecs, rank), BF)
            for n in (WIN * cap0, WIN * cap1, 2 * HW + 1, 2 * windows[-1].shape[0] * count)
        ]
        + [
            VMEM((leaves, rows, rank), F32), VMEM((leaves // 2, rows, rank), F32),
            VMEM((count, rows, rank), BF), DMA((4,)),
        ],
        (150_000_000, 20_000_000), 16 * 1024 * 1024,
    )


def on_device(
    vectors,
    leaf_basis,
    leaf_transfer,
    pair_transfer,
    near_blocks,
    near_offset,
    leaf_send,
    leaf_list,
    leaf_coupling,
    pair_send,
    pair_list,
    pair_coupling,
    top_list,
    top_coupling,
):
    rows = lax.axis_size("row")
    devs = rows * lax.axis_size("col")
    cap0, cap1 = leaf_send.shape[2], pair_send.shape[2]
    lsend = jnp.transpose(leaf_send, (1, 0, 2))
    psend = jnp.transpose(pair_send, (0, 2, 1))
    tops, own, windows = up_pass(
        lsend, psend, vectors, leaf_basis, leaf_transfer, pair_transfer, rows
    )
    count = own.shape[0]
    sib, cross, fwd, back = hand_pass(windows, (count + 1, count + 1, count, count))
    ring = range(devs)
    sibling = [(d, d ^ 1) for d in ring]
    mine = lax.all_to_all(tops, "row", split_axis=0, concat_axis=0)
    theirs = lax.ppermute(mine, AXES, sibling)
    sib = lax.ppermute(sib, AXES, sibling)
    cross = lax.ppermute(cross, AXES, [(d, (d + 1 if d % 2 else d - 1) % devs) for d in ring])
    fwd = lax.ppermute(fwd, AXES, [(d, (d + 2) % devs) for d in ring])
    back = lax.ppermute(back, AXES, [(d, (d - 2) % devs) for d in ring])
    close, ends = near_pass(near_offset.T, vectors, near_blocks)
    return rest_pass(
        (leaf_list.T, pair_list.T, top_list, near_offset.T),
        (leaf_coupling, pair_coupling, top_coupling, ends, pair_transfer, leaf_transfer, leaf_basis, close),
        (own, sib, cross, fwd, back, mine, theirs), cap0, cap1,
    )


def solution(mesh):
    placed = P(("groups", "row", "col"))
    behind = P(None, ("groups", "row", "col"))
    return jax.shard_map(
        on_device,
        mesh=mesh,
        in_specs=(
            placed, placed, placed, placed, behind, placed, placed, placed, behind, placed, placed, behind, placed, behind,
        ),
        out_specs=behind,
        check_vma=False,
    )
```

```python
import jax
import jax.numpy as jnp
from jax import lax
from jax.experimental import pallas as pl
from jax.experimental.pallas import tpu as pltpu
from jax.sharding import PartitionSpec as P

REACH = 2
WIN = 2 * REACH + 1
HW = 2
GROUP = 8
AXES = ("row", "col")
F32 = jnp.float32
BF = jnp.bfloat16
LIMIT = 56 * 1024 * 1024

VMEM = pltpu.VMEM
SMEM = pltpu.SMEM
DMA = pltpu.SemaphoreType.DMA
FIXED = pl.BlockSpec(memory_space=pltpu.HBM)
WHOLE = pl.BlockSpec(memory_space=VMEM)


def dot(left, right):
    return jnp.dot(left, right, preferred_element_type=F32)


def beside(*parts):
    return jnp.concatenate(parts, axis=1)


def above(*parts):
    return jnp.concatenate(parts, axis=0)


def dot_t(left, right):
    return lax.dot_general(left, right, (((1,), (1,)), ((), ())), preferred_element_type=F32)


def row_of_blocks(ref, q):
    kernels, _, partners, _, _ = ref.shape
    return beside(*[above(*[ref[k, q, m] for k in range(kernels)]) for m in range(partners)])


def by_kernel(wide, rank):
    return above(*[wide[:, k * rank:(k + 1) * rank] for k in range(wide.shape[1] // rank)])


def copies(pairs, sems):
    made = [pltpu.make_async_copy(src, dst, sems.at[i]) for i, (src, dst) in enumerate(pairs)]
    for copy in made:
        copy.start()
    return made


def split(row, ref, at):
    rank = row.shape[1] // 2
    ref[at] = row[:, :rank]
    ref[at + 1] = row[:, rank:]


def call(body, name, params, arrays, out_shape, out_specs, scratch, cost, limit=LIMIT):
    return pl.pallas_call(
        body,
        out_shape=out_shape,
        in_specs=[FIXED] * len(params) + [WHOLE] * len(arrays),
        out_specs=out_specs,
        scratch_shapes=scratch,
        compiler_params=pltpu.CompilerParams(vmem_limit_bytes=limit),
        cost_estimate=pl.CostEstimate(flops=cost[0], bytes_accessed=cost[1], transcendentals=0),
        name=name,
    )(*params, *arrays)


def like(x):
    return VMEM(x.shape, x.dtype)


def held(x):
    return SMEM(x.shape, x.dtype)


def up_body(vec_h, basis_h, ltr_h, ptr_h, lsend_h, psend_h, tops, own, windows,
            vec, basis, ltr, ptr, lsend, psend, low, mid, sems):
    leaves, vecs, rank = vec.shape
    col = lax.axis_index("col")
    cap0 = lsend.shape[2]
    cap1 = psend.shape[1]
    made = copies(
        [(vec_h, vec), (basis_h, basis), (ltr_h, ltr), (ptr_h, ptr), (lsend_h, lsend), (psend_h, psend)], sems
    )
    made[0].wait()
    made[1].wait()
    for t in range(leaves):
        low[t] = dot(vec[t], basis[t]).astype(BF)
    made[2].wait()
    for j in range(leaves // 2):
        mid[j] = dot(
            beside(low[2 * j], low[2 * j + 1]), ltr[2 * j:2 * j + 2].reshape(2 * rank, rank)
        ).astype(BF)
    made[3].wait()
    high = []
    for i in range(leaves // 4):
        high.append(
            dot(beside(mid[2 * i], mid[2 * i + 1]), ptr[2 * i:2 * i + 2].reshape(2 * rank, rank)).astype(BF)
        )
    for i in range(leaves // 8):
        both = beside(high[2 * i], high[2 * i + 1])
        for row in range(tops.shape[0]):
            tops[row, i] = both
    made[4].wait()
    made[5].wait()

    sib, cross, fwd, back = [windows.at[i] for i in range(4)]

    def pack(out, place):
        for c in range(cap0 // 2):
            out[c] = beside(low[lsend[place, 0, 2 * c]], low[lsend[place, 0, 2 * c + 1]])
        for c in range(cap1 // 2):
            out[cap0 // 2 + c] = beside(mid[psend[0, 2 * c, place]], mid[psend[0, 2 * c + 1, place]])

    def pack_halo(out, start):
        out[(cap0 + cap1) // 2] = beside(vec[start], vec[start + 1])

    pack(sib, 1 + 2 * col)
    pack_halo(sib, (1 - col) * (leaves - HW))
    pack(cross, 3 - 2 * col)
    pack_halo(cross, col * (leaves - HW))
    pack(fwd, 0)
    pack(back, 4)
    pack(own, REACH)


def up_pass(lsend, psend, vec, basis, ltr, ptr, rows):
    leaves, vecs, rank = vec.shape
    count = (lsend.shape[2] + psend.shape[1]) // 2
    shape = lambda *n: jax.ShapeDtypeStruct(n + (vecs, 2 * rank), BF)
    return call(
        up_body, "up", (vec, basis, ltr, ptr, lsend, psend), (),
        [shape(rows, leaves // 8), shape(count), shape(4, count + 1)],
        [WHOLE] * 3,
        [
            like(vec), like(basis), like(ltr), like(ptr), held(lsend), held(psend),
            VMEM((leaves, vecs, rank), BF), VMEM((leaves // 2, vecs, rank), BF), DMA((6,)),
        ],
        (10_000_000, 3_000_000),
    )


def hand_body(windows, *outs):
    for i, out in enumerate(outs):
        out[...] = windows[i, :out.shape[0]]


def hand_pass(windows, counts):
    shape = windows.shape[2:]
    return call(
        hand_body, "hand", (), (windows,),
        [jax.ShapeDtypeStruct((n,) + shape, windows.dtype) for n in counts],
        [WHOLE] * len(counts), [], (8_000_000_000, 100_000_000), 2 * 1024 * 1024,
    )


def pass_body(src, out):
    out[...] = src[...]


def pass_on(x):
    return call(
        pass_body, "pass", (), (x,), jax.ShapeDtypeStruct(x.shape, x.dtype), WHOLE, [],
        (8_000_000_000, 100_000_000), 2 * 1024 * 1024,
    )


def near_body(offsets_h, vec, near, close, ends, padded, offsets, sems):
    leaves, vecs, rank = vec.shape
    kernels = near.shape[0]
    made = copies([(offsets_h, offsets)], sems)
    ends[:, 0:HW] = near[:, 0:HW]
    ends[:, HW:] = near[:, leaves - HW:]
    zero = jnp.zeros((HW, vecs, rank), BF)
    padded[0:HW] = zero
    padded[HW:HW + leaves] = vec[...]
    padded[HW + leaves:] = zero
    made[0].wait()

    def body(c, _):
        for q in range(GROUP):
            t = c * GROUP + q
            rows = [padded[t + HW + offsets[n, t]] for n in range(near.shape[2])]
            close[t] = by_kernel(far_sum(rows, near, t), rank)
        return 0

    lax.fori_loop(0, leaves // GROUP, body, 0)


def near_pass(offsets, vec, blocks):
    kernels, leaves, near, rank, _ = blocks.shape
    vecs = vec.shape[1]
    return call(
        near_body, "near", (offsets,), (vec, blocks),
        [
            jax.ShapeDtypeStruct((leaves, kernels * vecs, rank), F32),
            jax.ShapeDtypeStruct((kernels, 2 * HW) + blocks.shape[2:], BF),
        ],
        [WHOLE] * 2,
        [VMEM((leaves + 2 * HW, vecs, rank), BF), held(offsets), DMA((1,))],
        (1_000_000_000, 20_000_000), 8 * 1024 * 1024,
    )


def far_sum(rows, blocks, q):
    return dot_t(beside(*rows), row_of_blocks(blocks, q))


def rest_body(llist_h, plist_h, tlist_h, offsets_h,
              leaf, pair, coupling, ends, ptr, ltr, basis, close, own, sib, cross, fwd, back, mine, theirs, out,
              llist, plist, tlist, offsets, wleaf, wpair, halo, tops, far0, far1, down, sems):
    kernels, leaves, partners, rank, _ = leaf.shape
    _, vecs, _ = wleaf.shape
    count = coupling.shape[1]
    cap0 = wleaf.shape[0] // WIN
    cap1 = wpair.shape[0] // WIN
    base = own.shape[0] - cap1 // 2
    col = lax.axis_index("col")
    place = lax.axis_index("row") * lax.axis_size("col") + col
    last_place = lax.axis_size("row") * lax.axis_size("col") - 1
    lists = copies([(llist_h, llist), (plist_h, plist), (tlist_h, tlist), (offsets_h, offsets)], sems)

    for block, slot in ((own, REACH), (fwd, 0), (back, 4), (sib, 3 - 2 * col), (cross, 1 + 2 * col)):
        for c in range(cap0 // 2):
            split(block[c], wleaf, slot * cap0 + 2 * c)
        for c in range(cap1 // 2):
            split(block[base + c], wpair, slot * cap1 + 2 * c)
    halo[2 * HW] = jnp.zeros((vecs, rank), BF)
    for block, upper in ((sib, 1 - col), (cross, col)):
        row = block[base + cap1 // 2]
        outside = (place == 0) & (upper == 0) | (place == last_place) & (upper == 1)
        split(jnp.where(outside, jnp.zeros_like(row), row), halo, upper * HW)
    for block, side in ((mine, col), (theirs, 1 - col)):
        for s in range(block.shape[0]):
            for i in range(block.shape[1]):
                split(block[s, i], tops, (s * 2 + side) * count + 2 * i)
    for copy in lists:
        copy.wait()

    def body(c, _):
        for q in range(GROUP):
            t = c * GROUP + q
            far0[t] = by_kernel(far_sum([wleaf[llist[m, t]] for m in range(partners)], leaf, t), rank)
        for q in range(GROUP // 2):
            j = c * (GROUP // 2) + q
            far1[j] = by_kernel(far_sum([wpair[plist[m, j]] for m in range(pair.shape[2])], pair, j), rank)
        for q in range(GROUP // 4):
            i = c * (GROUP // 4) + q
            rows = [tops[tlist[i, m]] for m in range(coupling.shape[2])]
            down[i] = by_kernel(far_sum(rows, coupling, i), rank).astype(BF)
        return 0

    lax.fori_loop(0, leaves // GROUP, body, 0)

    def edge(t):
        spots = [t + offsets[n, t] for n in range(ends.shape[2])]
        if t < HW:
            spots = [jnp.where(at < 0, at + HW, 2 * HW) for at in spots]
        else:
            spots = [jnp.where(at >= leaves, at - leaves + HW, 2 * HW) for at in spots]
        return by_kernel(far_sum([halo[at] for at in spots], ends, t if t < HW else t - (leaves - 2 * HW)), rank)

    down1 = []
    for j in range(2 * count):
        down1.append((far1[j] + dot_t(down[j // 2], ptr[j])).astype(BF))
    down0 = []
    for t in range(leaves):
        down0.append((far0[t] + dot_t(down1[t // 2], ltr[t])).astype(BF))
    for t in range(leaves):
        points = dot_t(down0[t], basis[t]) + close[t]
        if t < HW or t >= leaves - HW:
            points = points + edge(t)
        points = points.astype(BF)
        for k in range(kernels):
            out[k, t] = points[k * vecs:(k + 1) * vecs]


def rest_pass(lists, arrays, windows, cap0, cap1):
    leaf, pair, coupling = arrays[:3]
    kernels, leaves, _, rank, _ = leaf.shape
    count = coupling.shape[1]
    vecs = windows[0].shape[1]
    rows = kernels * vecs
    return call(
        rest_body, "rest", lists, arrays + windows,
        jax.ShapeDtypeStruct((kernels, leaves, vecs, rank), BF),
        WHOLE,
        [held(x) for x in lists]
        + [
            VMEM((n, vecs, rank), BF)
            for n in (WIN * cap0, WIN * cap1, 2 * HW + 1, 2 * windows[-1].shape[0] * count)
        ]
        + [
            VMEM((leaves, rows, rank), F32), VMEM((leaves // 2, rows, rank), F32),
            VMEM((count, rows, rank), BF), DMA((4,)),
        ],
        (150_000_000, 20_000_000), 16 * 1024 * 1024,
    )


def on_device(
    vectors,
    leaf_basis,
    leaf_transfer,
    pair_transfer,
    near_blocks,
    near_offset,
    leaf_send,
    leaf_list,
    leaf_coupling,
    pair_send,
    pair_list,
    pair_coupling,
    top_list,
    top_coupling,
):
    rows = lax.axis_size("row")
    devs = rows * lax.axis_size("col")
    cap0, cap1 = leaf_send.shape[2], pair_send.shape[2]
    lsend = jnp.transpose(leaf_send, (1, 0, 2))
    psend = jnp.transpose(pair_send, (0, 2, 1))
    tops, own, windows = up_pass(
        lsend, psend, vectors, leaf_basis, leaf_transfer, pair_transfer, rows
    )
    count = own.shape[0]
    sib, cross, fwd, back = hand_pass(windows, (count + 1, count + 1, count, count))
    ring = range(devs)
    sibling = [(d, d ^ 1) for d in ring]
    mine = lax.all_to_all(tops, "row", split_axis=0, concat_axis=0)
    mine = pass_on(mine)
    theirs = lax.ppermute(mine, AXES, sibling)
    sib = lax.ppermute(sib, AXES, sibling)
    cross = lax.ppermute(cross, AXES, [(d, (d + 1 if d % 2 else d - 1) % devs) for d in ring])
    fwd = lax.ppermute(fwd, AXES, [(d, (d + 2) % devs) for d in ring])
    back = lax.ppermute(back, AXES, [(d, (d - 2) % devs) for d in ring])
    close, ends = near_pass(near_offset.T, vectors, near_blocks)
    return rest_pass(
        (leaf_list.T, pair_list.T, top_list, near_offset.T),
        (leaf_coupling, pair_coupling, top_coupling, ends, pair_transfer, leaf_transfer, leaf_basis, close),
        (own, sib, cross, fwd, back, mine, theirs), cap0, cap1,
    )


def solution(mesh):
    placed = P(("groups", "row", "col"))
    behind = P(None, ("groups", "row", "col"))
    return jax.shard_map(
        on_device,
        mesh=mesh,
        in_specs=(
            placed, placed, placed, placed, behind, placed, placed, placed, behind, placed, placed, behind, placed, behind,
        ),
        out_specs=behind,
        check_vma=False,
    )
```

```python
import functools

import jax
import jax.numpy as jnp
from jax import lax
from jax.experimental import pallas as pl
from jax.experimental.pallas import tpu as pltpu
from jax.sharding import PartitionSpec as P

REACH = 2
WIN = 2 * REACH + 1
HW = 2
GROUP = 8
AXES = ("row", "col")
F32 = jnp.float32
BF = jnp.bfloat16
LIMIT = 56 * 1024 * 1024

VMEM = pltpu.VMEM
SMEM = pltpu.SMEM
DMA = pltpu.SemaphoreType.DMA
FIXED = pl.BlockSpec(memory_space=pltpu.HBM)
WHOLE = pl.BlockSpec(memory_space=VMEM)


def dot(left, right):
    return jnp.dot(left, right, preferred_element_type=F32)


def beside(*parts):
    return jnp.concatenate(parts, axis=1)


def above(*parts):
    return jnp.concatenate(parts, axis=0)


def dot_t(left, right):
    return lax.dot_general(left, right, (((1,), (1,)), ((), ())), preferred_element_type=F32)


def row_of_blocks(ref, q):
    kernels, _, partners, _, _ = ref.shape
    return beside(*[above(*[ref[k, q, m] for k in range(kernels)]) for m in range(partners)])


def by_kernel(wide, rank):
    return above(*[wide[:, k * rank:(k + 1) * rank] for k in range(wide.shape[1] // rank)])


def copies(pairs, sems):
    made = [pltpu.make_async_copy(src, dst, sems.at[i]) for i, (src, dst) in enumerate(pairs)]
    for copy in made:
        copy.start()
    return made


def split(row, ref, at):
    rank = row.shape[1] // 2
    ref[at] = row[:, :rank]
    ref[at + 1] = row[:, rank:]


def call(body, name, params, arrays, out_shape, out_specs, scratch, cost, limit=LIMIT):
    return pl.pallas_call(
        body,
        out_shape=out_shape,
        in_specs=[FIXED] * len(params) + [WHOLE] * len(arrays),
        out_specs=out_specs,
        scratch_shapes=scratch,
        compiler_params=pltpu.CompilerParams(vmem_limit_bytes=limit),
        cost_estimate=pl.CostEstimate(flops=cost[0], bytes_accessed=cost[1], transcendentals=0),
        name=name,
    )(*params, *arrays)


def like(x):
    return VMEM(x.shape, x.dtype)


def held(x):
    return SMEM(x.shape, x.dtype)


def up_body(vec_h, basis_h, ltr_h, ptr_h, lsend_h, psend_h, tops, own, windows,
            vec, basis, ltr, ptr, lsend, psend, low, mid, sems):
    leaves, vecs, rank = vec.shape
    col = lax.axis_index("col")
    cap0 = lsend.shape[2]
    cap1 = psend.shape[1]
    made = copies(
        [(vec_h, vec), (basis_h, basis), (ltr_h, ltr), (ptr_h, ptr), (lsend_h, lsend), (psend_h, psend)], sems
    )
    made[0].wait()
    made[1].wait()
    for t in range(leaves):
        low[t] = dot(vec[t], basis[t]).astype(BF)
    made[2].wait()
    for j in range(leaves // 2):
        mid[j] = dot(
            beside(low[2 * j], low[2 * j + 1]), ltr[2 * j:2 * j + 2].reshape(2 * rank, rank)
        ).astype(BF)
    made[3].wait()
    high = []
    for i in range(leaves // 4):
        high.append(
            dot(beside(mid[2 * i], mid[2 * i + 1]), ptr[2 * i:2 * i + 2].reshape(2 * rank, rank)).astype(BF)
        )
    for i in range(leaves // 8):
        tops[0, i] = beside(high[2 * i], high[2 * i + 1])
    made[4].wait()
    made[5].wait()

    sib, cross, fwd, back = [windows.at[i] for i in range(4)]

    def pack(out, place):
        for c in range(cap0 // 2):
            out[c] = beside(low[lsend[place, 0, 2 * c]], low[lsend[place, 0, 2 * c + 1]])
        for c in range(cap1 // 2):
            out[cap0 // 2 + c] = beside(mid[psend[0, 2 * c, place]], mid[psend[0, 2 * c + 1, place]])

    def pack_halo(out, start):
        out[(cap0 + cap1) // 2] = beside(vec[start], vec[start + 1])

    pack(sib, 1 + 2 * col)
    pack_halo(sib, (1 - col) * (leaves - HW))
    pack(cross, 3 - 2 * col)
    pack_halo(cross, col * (leaves - HW))
    pack(fwd, 0)
    pack(back, 4)
    pack(own, REACH)


def up_pass(lsend, psend, vec, basis, ltr, ptr):
    leaves, vecs, rank = vec.shape
    count = (lsend.shape[2] + psend.shape[1]) // 2
    shape = lambda *n: jax.ShapeDtypeStruct(n + (vecs, 2 * rank), BF)
    return call(
        up_body, "up", (vec, basis, ltr, ptr, lsend, psend), (),
        [shape(1, leaves // 8), shape(count), shape(4, count + 1)],
        [WHOLE] * 3,
        [
            like(vec), like(basis), like(ltr), like(ptr), held(lsend), held(psend),
            VMEM((leaves, vecs, rank), BF), VMEM((leaves // 2, vecs, rank), BF), DMA((6,)),
        ],
        (10_000_000, 3_000_000),
    )


def hand_body(windows, top, *outs):
    for i, out in enumerate(outs[:-1]):
        out[...] = windows[i, :out.shape[0]]
    outs[-1][...] = top[...]


def hand_pass(windows, top, counts):
    shape = windows.shape[2:]
    return call(
        hand_body, "hand", (), (windows, top),
        [jax.ShapeDtypeStruct((n,) + shape, windows.dtype) for n in counts] + [jax.ShapeDtypeStruct(top.shape, top.dtype)],
        [WHOLE] * (len(counts) + 1), [], (8_000_000_000, 100_000_000), 2 * 1024 * 1024,
    )


def join_body(first, second, out):
    out[:first.shape[0]] = first[...]
    out[first.shape[0]:] = second[...]


def join_pass(first, second):
    return call(
        join_body, "join", (), (first, second),
        jax.ShapeDtypeStruct((2 * first.shape[0],) + first.shape[1:], first.dtype), WHOLE, [],
        (100_000, 500_000), 2 * 1024 * 1024,
    )


def near_body(offsets_h, vec, near, close, ends, padded, offsets, sems):
    leaves, vecs, rank = vec.shape
    kernels = near.shape[0]
    made = copies([(offsets_h, offsets)], sems)
    ends[:, 0:HW] = near[:, 0:HW]
    ends[:, HW:] = near[:, leaves - HW:]
    zero = jnp.zeros((HW, vecs, rank), BF)
    padded[0:HW] = zero
    padded[HW:HW + leaves] = vec[...]
    padded[HW + leaves:] = zero
    made[0].wait()

    def body(c, _):
        for q in range(GROUP):
            t = c * GROUP + q
            rows = [padded[t + HW + offsets[n, t]] for n in range(near.shape[2])]
            close[t] = by_kernel(far_sum(rows, near, t), rank)
        return 0

    lax.fori_loop(0, leaves // GROUP, body, 0)


def near_pass(offsets, vec, blocks):
    kernels, leaves, near, rank, _ = blocks.shape
    vecs = vec.shape[1]
    return call(
        near_body, "near", (offsets,), (vec, blocks),
        [
            jax.ShapeDtypeStruct((leaves, kernels * vecs, rank), F32),
            jax.ShapeDtypeStruct((kernels, 2 * HW) + blocks.shape[2:], BF),
        ],
        [WHOLE] * 2,
        [VMEM((leaves + 2 * HW, vecs, rank), BF), held(offsets), DMA((1,))],
        (1_000_000_000, 20_000_000), 8 * 1024 * 1024,
    )


def far_sum(rows, blocks, q):
    return dot_t(beside(*rows), row_of_blocks(blocks, q))


def rest_body(offs, llist_h, plist_h, tlist_h, offsets_h,
              leaf, pair, coupling, ends, ptr, ltr, basis, close, own, sib, cross, fwd, back, held0, held1, held2, held3, out,
              llist, plist, tlist, offsets, wleaf, wpair, halo, tops, far0, far1, down, sems):
    kernels, leaves, partners, rank, _ = leaf.shape
    _, vecs, _ = wleaf.shape
    count = coupling.shape[1]
    cap0 = wleaf.shape[0] // WIN
    cap1 = wpair.shape[0] // WIN
    base = own.shape[0] - cap1 // 2
    col = lax.axis_index("col")
    place = lax.axis_index("row") * lax.axis_size("col") + col
    last_place = lax.axis_size("row") * lax.axis_size("col") - 1
    lists = copies([(llist_h, llist), (plist_h, plist), (tlist_h, tlist), (offsets_h, offsets)], sems)

    for block, slot in ((own, REACH), (fwd, 0), (back, 4), (sib, 3 - 2 * col), (cross, 1 + 2 * col)):
        for c in range(cap0 // 2):
            split(block[c], wleaf, slot * cap0 + 2 * c)
        for c in range(cap1 // 2):
            split(block[base + c], wpair, slot * cap1 + 2 * c)
    halo[2 * HW] = jnp.zeros((vecs, rank), BF)
    for block, upper in ((sib, 1 - col), (cross, col)):
        row = block[base + cap1 // 2]
        outside = (place == 0) & (upper == 0) | (place == last_place) & (upper == 1)
        split(jnp.where(outside, jnp.zeros_like(row), row), halo, upper * HW)
    row = lax.axis_index("row")
    for h, block in enumerate((held0, held1, held2, held3)):
        side = col if h < 2 else 1 - col
        for s, off in enumerate(offs):
            for i in range(block.shape[1]):
                split(block[s, i], tops, (((row ^ (off + h % 2)) * 2) + side) * count + 2 * i)
    for copy in lists:
        copy.wait()

    def body(c, _):
        for q in range(GROUP):
            t = c * GROUP + q
            far0[t] = by_kernel(far_sum([wleaf[llist[m, t]] for m in range(partners)], leaf, t), rank)
        for q in range(GROUP // 2):
            j = c * (GROUP // 2) + q
            far1[j] = by_kernel(far_sum([wpair[plist[m, j]] for m in range(pair.shape[2])], pair, j), rank)
        for q in range(GROUP // 4):
            i = c * (GROUP // 4) + q
            rows = [tops[tlist[i, m]] for m in range(coupling.shape[2])]
            down[i] = by_kernel(far_sum(rows, coupling, i), rank).astype(BF)
        return 0

    lax.fori_loop(0, leaves // GROUP, body, 0)

    def edge(t):
        spots = [t + offsets[n, t] for n in range(ends.shape[2])]
        if t < HW:
            spots = [jnp.where(at < 0, at + HW, 2 * HW) for at in spots]
        else:
            spots = [jnp.where(at >= leaves, at - leaves + HW, 2 * HW) for at in spots]
        return by_kernel(far_sum([halo[at] for at in spots], ends, t if t < HW else t - (leaves - 2 * HW)), rank)

    down1 = []
    for j in range(2 * count):
        down1.append((far1[j] + dot_t(down[j // 2], ptr[j])).astype(BF))
    down0 = []
    for t in range(leaves):
        down0.append((far0[t] + dot_t(down1[t // 2], ltr[t])).astype(BF))
    for t in range(leaves):
        points = dot_t(down0[t], basis[t]) + close[t]
        if t < HW or t >= leaves - HW:
            points = points + edge(t)
        points = points.astype(BF)
        for k in range(kernels):
            out[k, t] = points[k * vecs:(k + 1) * vecs]


def rest_pass(lists, arrays, windows, offs, cap0, cap1):
    leaf, pair, coupling = arrays[:3]
    kernels, leaves, _, rank, _ = leaf.shape
    count = coupling.shape[1]
    vecs = windows[0].shape[1]
    rows = kernels * vecs
    return call(
        functools.partial(rest_body, offs), "rest", lists, arrays + windows,
        jax.ShapeDtypeStruct((kernels, leaves, vecs, rank), BF),
        WHOLE,
        [held(x) for x in lists]
        + [
            VMEM((n, vecs, rank), BF)
            for n in (WIN * cap0, WIN * cap1, 2 * HW + 1, 4 * windows[-1].shape[0] * count)
        ]
        + [
            VMEM((leaves, rows, rank), F32), VMEM((leaves // 2, rows, rank), F32),
            VMEM((count, rows, rank), BF), DMA((4,)),
        ],
        (150_000_000, 20_000_000), 16 * 1024 * 1024,
    )


def on_device(
    vectors,
    leaf_basis,
    leaf_transfer,
    pair_transfer,
    near_blocks,
    near_offset,
    leaf_send,
    leaf_list,
    leaf_coupling,
    pair_send,
    pair_list,
    pair_coupling,
    top_list,
    top_coupling,
):
    rows = lax.axis_size("row")
    devs = rows * lax.axis_size("col")
    cap0, cap1 = leaf_send.shape[2], pair_send.shape[2]
    lsend = jnp.transpose(leaf_send, (1, 0, 2))
    psend = jnp.transpose(pair_send, (0, 2, 1))
    held, own, windows = up_pass(lsend, psend, vectors, leaf_basis, leaf_transfer, pair_transfer)
    count = own.shape[0]
    sib, cross, fwd, back, held = hand_pass(windows, held, (count + 1, count + 1, count, count))
    ring = range(devs)

    def sent(piece, target):
        return lax.ppermute(piece, AXES, [(d, target(d)) for d in ring])

    offs = [0]
    mask = rows // 2
    while mask > 1:
        held = join_pass(held, sent(held, lambda d: d ^ (2 * mask)))
        offs = offs + [off ^ mask for off in offs]
        mask //= 2
    sib = sent(sib, lambda d: d ^ 1)
    cross = sent(cross, lambda d: (d + 1 if d % 2 else d - 1) % devs)
    fwd = sent(fwd, lambda d: (d + 2) % devs)
    back = sent(back, lambda d: (d - 2) % devs)
    pieces = (held, sent(held, lambda d: d ^ 2), sent(held, lambda d: d ^ 1), sent(held, lambda d: d ^ 3))
    close, ends = near_pass(near_offset.T, vectors, near_blocks)
    return rest_pass(
        (leaf_list.T, pair_list.T, top_list, near_offset.T),
        (leaf_coupling, pair_coupling, top_coupling, ends, pair_transfer, leaf_transfer, leaf_basis, close),
        (own, sib, cross, fwd, back) + pieces, offs, cap0, cap1,
    )


def solution(mesh):
    placed = P(("groups", "row", "col"))
    behind = P(None, ("groups", "row", "col"))
    return jax.shard_map(
        on_device,
        mesh=mesh,
        in_specs=(
            placed, placed, placed, placed, behind, placed, placed, placed, behind, placed, placed, behind, placed, behind,
        ),
        out_specs=behind,
        check_vma=False,
    )
```

```python
import functools

import jax
import jax.numpy as jnp
from jax import lax
from jax.experimental import pallas as pl
from jax.experimental.pallas import tpu as pltpu
from jax.sharding import PartitionSpec as P

REACH = 2
WIN = 2 * REACH + 1
HW = 2
GROUP = 16
AXES = ("row", "col")
F32 = jnp.float32
BF = jnp.bfloat16
LIMIT = 56 * 1024 * 1024

VMEM = pltpu.VMEM
SMEM = pltpu.SMEM
DMA = pltpu.SemaphoreType.DMA
FIXED = pl.BlockSpec(memory_space=pltpu.HBM)
WHOLE = pl.BlockSpec(memory_space=VMEM)


def dot(left, right):
    return jnp.dot(left, right, preferred_element_type=F32)


def beside(*parts):
    return jnp.concatenate(parts, axis=1)


def above(*parts):
    return jnp.concatenate(parts, axis=0)


def dot_t(left, right):
    return lax.dot_general(left, right, (((1,), (1,)), ((), ())), preferred_element_type=F32)


def row_of_blocks(ref, q):
    kernels, _, partners, _, _ = ref.shape
    return beside(*[above(*[ref[k, q, m] for k in range(kernels)]) for m in range(partners)])


def by_kernel(wide, rank):
    return above(*[wide[:, k * rank:(k + 1) * rank] for k in range(wide.shape[1] // rank)])


def copies(pairs, sems):
    made = [pltpu.make_async_copy(src, dst, sems.at[i]) for i, (src, dst) in enumerate(pairs)]
    for copy in made:
        copy.start()
    return made


def split(row, ref, at):
    rank = row.shape[1] // 2
    ref[at] = row[:, :rank]
    ref[at + 1] = row[:, rank:]


def call(body, name, params, arrays, out_shape, out_specs, scratch, cost, limit=LIMIT):
    return pl.pallas_call(
        body,
        out_shape=out_shape,
        in_specs=[FIXED] * len(params) + [WHOLE] * len(arrays),
        out_specs=out_specs,
        scratch_shapes=scratch,
        compiler_params=pltpu.CompilerParams(vmem_limit_bytes=limit),
        cost_estimate=pl.CostEstimate(flops=cost[0], bytes_accessed=cost[1], transcendentals=0),
        name=name,
    )(*params, *arrays)


def like(x):
    return VMEM(x.shape, x.dtype)


def held(x):
    return SMEM(x.shape, x.dtype)


def up_body(vec_h, basis_h, ltr_h, ptr_h, lsend_h, psend_h, tops, own, sib, cross, fwd, back,
            vec, basis, ltr, ptr, lsend, psend, low, mid, sems):
    leaves, vecs, rank = vec.shape
    col = lax.axis_index("col")
    cap0 = lsend.shape[2]
    cap1 = psend.shape[1]
    made = copies(
        [(vec_h, vec), (basis_h, basis), (ltr_h, ltr), (ptr_h, ptr), (lsend_h, lsend), (psend_h, psend)], sems
    )
    made[0].wait()
    made[1].wait()
    for t in range(leaves):
        low[t] = dot(vec[t], basis[t]).astype(BF)
    made[2].wait()
    for j in range(leaves // 2):
        mid[j] = dot(
            beside(low[2 * j], low[2 * j + 1]), ltr[2 * j:2 * j + 2].reshape(2 * rank, rank)
        ).astype(BF)
    made[3].wait()
    high = []
    for i in range(leaves // 4):
        high.append(
            dot(beside(mid[2 * i], mid[2 * i + 1]), ptr[2 * i:2 * i + 2].reshape(2 * rank, rank)).astype(BF)
        )
    for i in range(leaves // 8):
        tops[0, i] = beside(high[2 * i], high[2 * i + 1])
    made[4].wait()
    made[5].wait()

    def pack(out, place):
        for c in range(cap0 // 2):
            out[c] = beside(low[lsend[place, 0, 2 * c]], low[lsend[place, 0, 2 * c + 1]])
        for c in range(cap1 // 2):
            out[cap0 // 2 + c] = beside(mid[psend[0, 2 * c, place]], mid[psend[0, 2 * c + 1, place]])

    def pack_halo(out, start):
        out[(cap0 + cap1) // 2] = beside(vec[start], vec[start + 1])

    pack(sib, 1 + 2 * col)
    pack_halo(sib, (1 - col) * (leaves - HW))
    pack(cross, 3 - 2 * col)
    pack_halo(cross, col * (leaves - HW))
    pack(fwd, 0)
    pack(back, 4)
    pack(own, REACH)


def up_pass(lsend, psend, vec, basis, ltr, ptr):
    leaves, vecs, rank = vec.shape
    count = (lsend.shape[2] + psend.shape[1]) // 2
    shape = lambda *n: jax.ShapeDtypeStruct(n + (vecs, 2 * rank), BF)
    return call(
        up_body, "up", (vec, basis, ltr, ptr, lsend, psend), (),
        [shape(1, leaves // 8), shape(count), shape(count + 1), shape(count + 1), shape(count), shape(count)],
        [WHOLE] * 6,
        [
            like(vec), like(basis), like(ltr), like(ptr), held(lsend), held(psend),
            VMEM((leaves, vecs, rank), BF), VMEM((leaves // 2, vecs, rank), BF), DMA((6,)),
        ],
        (10_000_000, 3_000_000),
    )


def join_body(first, second, *rest):
    out = rest[-1]
    out[:first.shape[0]] = first[...]
    out[first.shape[0]:] = second[...]


def join_pass(first, second, *others):
    return call(
        join_body, "join", (), (first, second) + others,
        jax.ShapeDtypeStruct((2 * first.shape[0],) + first.shape[1:], first.dtype), WHOLE, [],
        (8_000_000_000, 100_000_000) if others else (100_000, 500_000), 2 * 1024 * 1024,
    )


def near_body(offsets_h, vec, near, close, ends, padded, offsets, sems):
    leaves, vecs, rank = vec.shape
    kernels = near.shape[0]
    made = copies([(offsets_h, offsets)], sems)
    ends[:, 0:HW] = near[:, 0:HW]
    ends[:, HW:] = near[:, leaves - HW:]
    zero = jnp.zeros((HW, vecs, rank), BF)
    padded[0:HW] = zero
    padded[HW:HW + leaves] = vec[...]
    padded[HW + leaves:] = zero
    made[0].wait()

    def body(c, _):
        for q in range(GROUP):
            t = c * GROUP + q
            rows = [padded[t + HW + offsets[n, t]] for n in range(near.shape[2])]
            close[t] = by_kernel(far_sum(rows, near, t), rank)
        return 0

    lax.fori_loop(0, leaves // GROUP, body, 0)


def near_pass(offsets, vec, blocks):
    kernels, leaves, near, rank, _ = blocks.shape
    vecs = vec.shape[1]
    return call(
        near_body, "near", (offsets,), (vec, blocks),
        [
            jax.ShapeDtypeStruct((leaves, kernels * vecs, rank), F32),
            jax.ShapeDtypeStruct((kernels, 2 * HW) + blocks.shape[2:], BF),
        ],
        [WHOLE] * 2,
        [VMEM((leaves + 2 * HW, vecs, rank), BF), held(offsets), DMA((1,))],
        (1_000_000_000, 20_000_000), 8 * 1024 * 1024,
    )


def far_sum(rows, blocks, q):
    return dot_t(beside(*rows), row_of_blocks(blocks, q))


def rest_body(offs, llist_h, plist_h, tlist_h, offsets_h,
              leaf, pair, coupling, ends, ptr, ltr, basis, close, own, sib, cross, fwd, back, held0, held1, held2, held3, out,
              llist, plist, tlist, offsets, wleaf, wpair, halo, tops, far0, far1, down, sems):
    kernels, leaves, partners, rank, _ = leaf.shape
    _, vecs, _ = wleaf.shape
    count = coupling.shape[1]
    cap0 = wleaf.shape[0] // WIN
    cap1 = wpair.shape[0] // WIN
    base = own.shape[0] - cap1 // 2
    col = lax.axis_index("col")
    place = lax.axis_index("row") * lax.axis_size("col") + col
    last_place = lax.axis_size("row") * lax.axis_size("col") - 1
    lists = copies([(llist_h, llist), (plist_h, plist), (tlist_h, tlist), (offsets_h, offsets)], sems)

    for block, slot in ((own, REACH), (fwd, 0), (back, 4), (sib, 3 - 2 * col), (cross, 1 + 2 * col)):
        for c in range(cap0 // 2):
            split(block[c], wleaf, slot * cap0 + 2 * c)
        for c in range(cap1 // 2):
            split(block[base + c], wpair, slot * cap1 + 2 * c)
    halo[2 * HW] = jnp.zeros((vecs, rank), BF)
    for block, upper in ((sib, 1 - col), (cross, col)):
        row = block[base + cap1 // 2]
        outside = (place == 0) & (upper == 0) | (place == last_place) & (upper == 1)
        split(jnp.where(outside, jnp.zeros_like(row), row), halo, upper * HW)
    row = lax.axis_index("row")
    for h, block in enumerate((held0, held1, held2, held3)):
        side = col if h < 2 else 1 - col
        for s, off in enumerate(offs):
            for i in range(block.shape[1]):
                split(block[s, i], tops, (((row ^ (off + h % 2)) * 2) + side) * count + 2 * i)
    for copy in lists:
        copy.wait()

    def body(c, _):
        for q in range(GROUP):
            t = c * GROUP + q
            far0[t] = by_kernel(far_sum([wleaf[llist[m, t]] for m in range(partners)], leaf, t), rank)
        for q in range(GROUP // 2):
            j = c * (GROUP // 2) + q
            far1[j] = by_kernel(far_sum([wpair[plist[m, j]] for m in range(pair.shape[2])], pair, j), rank)
        for q in range(GROUP // 4):
            i = c * (GROUP // 4) + q
            rows = [tops[tlist[i, m]] for m in range(coupling.shape[2])]
            down[i] = by_kernel(far_sum(rows, coupling, i), rank).astype(BF)
        return 0

    lax.fori_loop(0, leaves // GROUP, body, 0)

    def edge(t):
        spots = [t + offsets[n, t] for n in range(ends.shape[2])]
        if t < HW:
            spots = [jnp.where(at < 0, at + HW, 2 * HW) for at in spots]
        else:
            spots = [jnp.where(at >= leaves, at - leaves + HW, 2 * HW) for at in spots]
        return by_kernel(far_sum([halo[at] for at in spots], ends, t if t < HW else t - (leaves - 2 * HW)), rank)

    down1 = []
    for j in range(2 * count):
        down1.append((far1[j] + dot_t(down[j // 2], ptr[j])).astype(BF))
    down0 = []
    for t in range(leaves):
        down0.append((far0[t] + dot_t(down1[t // 2], ltr[t])).astype(BF))
    for t in range(leaves):
        points = dot_t(down0[t], basis[t]) + close[t]
        if t < HW or t >= leaves - HW:
            points = points + edge(t)
        points = points.astype(BF)
        for k in range(kernels):
            out[k, t] = points[k * vecs:(k + 1) * vecs]


def rest_pass(lists, arrays, windows, offs, cap0, cap1):
    leaf, pair, coupling = arrays[:3]
    kernels, leaves, _, rank, _ = leaf.shape
    count = coupling.shape[1]
    vecs = windows[0].shape[1]
    rows = kernels * vecs
    return call(
        functools.partial(rest_body, offs), "rest", lists, arrays + windows,
        jax.ShapeDtypeStruct((kernels, leaves, vecs, rank), BF),
        WHOLE,
        [held(x) for x in lists]
        + [
            VMEM((n, vecs, rank), BF)
            for n in (WIN * cap0, WIN * cap1, 2 * HW + 1, 4 * windows[-1].shape[0] * count)
        ]
        + [
            VMEM((leaves, rows, rank), F32), VMEM((leaves // 2, rows, rank), F32),
            VMEM((count, rows, rank), BF), DMA((4,)),
        ],
        (150_000_000, 20_000_000), 16 * 1024 * 1024,
    )


def on_device(
    vectors,
    leaf_basis,
    leaf_transfer,
    pair_transfer,
    near_blocks,
    near_offset,
    leaf_send,
    leaf_list,
    leaf_coupling,
    pair_send,
    pair_list,
    pair_coupling,
    top_list,
    top_coupling,
):
    rows = lax.axis_size("row")
    devs = rows * lax.axis_size("col")
    cap0, cap1 = leaf_send.shape[2], pair_send.shape[2]
    lsend = jnp.transpose(leaf_send, (1, 0, 2))
    psend = jnp.transpose(pair_send, (0, 2, 1))
    held, own, sib, cross, fwd, back = up_pass(
        lsend, psend, vectors, leaf_basis, leaf_transfer, pair_transfer
    )
    ring = range(devs)

    def sent(piece, target):
        return lax.ppermute(piece, AXES, [(d, target(d)) for d in ring])

    offs = [0]
    mask = rows // 2
    got = sent(held, lambda d: d ^ (2 * mask))
    fwd = sent(fwd, lambda d: (d + 2) % devs)
    back = sent(back, lambda d: (d - 2) % devs)
    others = (fwd, back)
    while mask > 1:
        held = join_pass(held, got, *others)
        offs = offs + [off ^ mask for off in offs]
        mask //= 2
        got = sent(held, lambda d: d ^ (2 * mask))
        others = ()
    sib = sent(sib, lambda d: d ^ 1)
    cross = sent(cross, lambda d: (d + 1 if d % 2 else d - 1) % devs)
    pieces = (held, got, sent(held, lambda d: d ^ 1), sent(held, lambda d: d ^ 3))
    close, ends = near_pass(near_offset.T, vectors, near_blocks)
    return rest_pass(
        (leaf_list.T, pair_list.T, top_list, near_offset.T),
        (leaf_coupling, pair_coupling, top_coupling, ends, pair_transfer, leaf_transfer, leaf_basis, close),
        (own, sib, cross, fwd, back) + pieces, offs, cap0, cap1,
    )


def solution(mesh):
    placed = P(("groups", "row", "col"))
    behind = P(None, ("groups", "row", "col"))
    return jax.shard_map(
        on_device,
        mesh=mesh,
        in_specs=(
            placed, placed, placed, placed, behind, placed, placed, placed, behind, placed, placed, behind, placed, behind,
        ),
        out_specs=behind,
        check_vma=False,
    )
```

```python
import functools

import jax
import jax.numpy as jnp
from jax import lax
from jax.experimental import pallas as pl
from jax.experimental.pallas import tpu as pltpu
from jax.sharding import PartitionSpec as P

REACH = 2
WIN = 2 * REACH + 1
HW = 2
AXES = ("row", "col")
F32 = jnp.float32
BF = jnp.bfloat16
LIMIT = 56 * 1024 * 1024

VMEM = pltpu.VMEM
SMEM = pltpu.SMEM
DMA = pltpu.SemaphoreType.DMA
FIXED = pl.BlockSpec(memory_space=pltpu.HBM)
WHOLE = pl.BlockSpec(memory_space=VMEM)


def dot(left, right):
    return jnp.dot(left, right, preferred_element_type=F32)


def beside(*parts):
    return jnp.concatenate(parts, axis=1)


def above(*parts):
    return jnp.concatenate(parts, axis=0)


def dot_t(left, right):
    return lax.dot_general(left, right, (((1,), (1,)), ((), ())), preferred_element_type=F32)


def row_of_blocks(ref, q):
    kernels, _, partners, _, _ = ref.shape
    return beside(*[above(*[ref[k, q, m] for k in range(kernels)]) for m in range(partners)])


def by_kernel(wide, rank):
    return above(*[wide[:, k * rank:(k + 1) * rank] for k in range(wide.shape[1] // rank)])


def copies(pairs, sems):
    made = [pltpu.make_async_copy(src, dst, sems.at[i]) for i, (src, dst) in enumerate(pairs)]
    for copy in made:
        copy.start()
    return made


def split(row, ref, at):
    rank = row.shape[1] // 2
    ref[at] = row[:, :rank]
    ref[at + 1] = row[:, rank:]


def call(body, name, params, arrays, out_shape, out_specs, scratch, cost, limit=LIMIT):
    return pl.pallas_call(
        body,
        out_shape=out_shape,
        in_specs=[FIXED] * len(params) + [WHOLE] * len(arrays),
        out_specs=out_specs,
        scratch_shapes=scratch,
        compiler_params=pltpu.CompilerParams(vmem_limit_bytes=limit),
        cost_estimate=pl.CostEstimate(flops=cost[0], bytes_accessed=cost[1], transcendentals=0),
        name=name,
    )(*params, *arrays)


def like(x):
    return VMEM(x.shape, x.dtype)


def held(x):
    return SMEM(x.shape, x.dtype)


def up_body(vec_h, basis_h, ltr_h, ptr_h, lsend_h, psend_h, tops, own, sib, cross, fwd, back,
            vec, basis, ltr, ptr, lsend, psend, low, mid, sems):
    leaves, vecs, rank = vec.shape
    col = lax.axis_index("col")
    cap0 = lsend.shape[2]
    cap1 = psend.shape[1]
    made = copies(
        [(vec_h, vec), (basis_h, basis), (ltr_h, ltr), (ptr_h, ptr), (lsend_h, lsend), (psend_h, psend)], sems
    )
    made[0].wait()
    made[1].wait()
    for t in range(leaves):
        low[t] = dot(vec[t], basis[t]).astype(BF)
    made[2].wait()
    for j in range(leaves // 2):
        mid[j] = dot(
            beside(low[2 * j], low[2 * j + 1]), ltr[2 * j:2 * j + 2].reshape(2 * rank, rank)
        ).astype(BF)
    made[3].wait()
    high = []
    for i in range(leaves // 4):
        high.append(
            dot(beside(mid[2 * i], mid[2 * i + 1]), ptr[2 * i:2 * i + 2].reshape(2 * rank, rank)).astype(BF)
        )
    for i in range(leaves // 8):
        tops[0, i] = beside(high[2 * i], high[2 * i + 1])
    made[4].wait()
    made[5].wait()

    def pack(out, place):
        for c in range(cap0 // 2):
            out[c] = beside(low[lsend[place, 0, 2 * c]], low[lsend[place, 0, 2 * c + 1]])
        for c in range(cap1 // 2):
            out[cap0 // 2 + c] = beside(mid[psend[0, 2 * c, place]], mid[psend[0, 2 * c + 1, place]])

    def pack_halo(out, start):
        out[(cap0 + cap1) // 2] = beside(vec[start], vec[start + 1])

    pack(sib, 1 + 2 * col)
    pack_halo(sib, (1 - col) * (leaves - HW))
    pack(cross, 3 - 2 * col)
    pack_halo(cross, col * (leaves - HW))
    pack(fwd, 0)
    pack(back, 4)
    pack(own, REACH)


def up_pass(lsend, psend, vec, basis, ltr, ptr):
    leaves, vecs, rank = vec.shape
    count = (lsend.shape[2] + psend.shape[1]) // 2
    shape = lambda *n: jax.ShapeDtypeStruct(n + (vecs, 2 * rank), BF)
    return call(
        up_body, "up", (vec, basis, ltr, ptr, lsend, psend), (),
        [shape(1, leaves // 8), shape(count), shape(count + 1), shape(count + 1), shape(count), shape(count)],
        [WHOLE] * 6,
        [
            like(vec), like(basis), like(ltr), like(ptr), held(lsend), held(psend),
            VMEM((leaves, vecs, rank), BF), VMEM((leaves // 2, vecs, rank), BF), DMA((6,)),
        ],
        (10_000_000, 3_000_000),
    )


def join_body(first, second, *rest):
    out = rest[-1]
    out[:first.shape[0]] = first[...]
    out[first.shape[0]:] = second[...]


def join_pass(first, second, *others):
    return call(
        join_body, "join", (), (first, second) + others,
        jax.ShapeDtypeStruct((2 * first.shape[0],) + first.shape[1:], first.dtype), WHOLE, [],
        (8_000_000_000, 100_000_000) if others else (100_000, 500_000), 2 * 1024 * 1024,
    )


def far_sum(rows, blocks, q):
    return dot_t(beside(*rows), row_of_blocks(blocks, q))


def near_body(offsets_h, llist_h, plist_h, vec, near, leaf, pair, own, sib, cross, fwd, back, close, far0, far1,
              offsets, llist, plist, padded, wleaf, wpair, sems):
    leaves, vecs, rank = vec.shape
    partners = leaf.shape[2]
    cap0 = wleaf.shape[0] // WIN
    cap1 = wpair.shape[0] // WIN
    base = own.shape[0] - cap1 // 2
    col = lax.axis_index("col")
    place = lax.axis_index("row") * lax.axis_size("col") + col
    last_place = lax.axis_size("row") * lax.axis_size("col") - 1
    made = copies([(offsets_h, offsets), (llist_h, llist), (plist_h, plist)], sems)

    for block, slot in ((own, REACH), (fwd, 0), (back, 4), (sib, 3 - 2 * col), (cross, 1 + 2 * col)):
        for c in range(cap0 // 2):
            split(block[c], wleaf, slot * cap0 + 2 * c)
        for c in range(cap1 // 2):
            split(block[base + c], wpair, slot * cap1 + 2 * c)
    padded[HW:HW + leaves] = vec[...]
    for block, upper in ((sib, 1 - col), (cross, col)):
        row = block[base + cap1 // 2]
        outside = (place == 0) & (upper == 0) | (place == last_place) & (upper == 1)
        split(jnp.where(outside, jnp.zeros_like(row), row), padded, upper * (HW + leaves))
    for copy in made:
        copy.wait()

    for t in range(leaves):
        rows = [padded[t + HW + offsets[n, t]] for n in range(near.shape[2])]
        close[t] = by_kernel(far_sum(rows, near, t), rank)
        far0[t] = by_kernel(far_sum([wleaf[llist[m, t]] for m in range(partners)], leaf, t), rank)
        if t % 2:
            j = t // 2
            far1[j] = by_kernel(far_sum([wpair[plist[m, j]] for m in range(pair.shape[2])], pair, j), rank)


def near_pass(lists, arrays, windows, cap0, cap1):
    vec, blocks = arrays[:2]
    leaves, vecs, rank = vec.shape
    rows = blocks.shape[0] * vecs
    sums = [jax.ShapeDtypeStruct((n, rows, rank), F32) for n in (leaves, leaves, leaves // 2)]
    return call(
        near_body, "near", lists, arrays + windows, sums, [WHOLE] * 3,
        [held(x) for x in lists]
        + [VMEM((n, vecs, rank), BF) for n in (leaves + 2 * HW, WIN * cap0, WIN * cap1)] + [DMA((3,))],
        (1_000_000_000, 20_000_000), 8 * 1024 * 1024,
    )


def rest_body(offs, tlist_h, coupling, ptr, ltr, basis, close, far0, far1, held0, held1, held2, held3, out,
              tlist, tops, sems):
    kernels, count, partners, rank, _ = coupling.shape
    leaves = basis.shape[0]
    vecs = tops.shape[1]
    col = lax.axis_index("col")
    row = lax.axis_index("row")
    made = copies([(tlist_h, tlist)], sems)
    for h, block in enumerate((held0, held1, held2, held3)):
        side = col if h < 2 else 1 - col
        for s, off in enumerate(offs):
            for i in range(block.shape[1]):
                split(block[s, i], tops, (((row ^ (off + h % 2)) * 2) + side) * count + 2 * i)
    made[0].wait()

    down2 = []
    for i in range(count):
        rows = [tops[tlist[i, m]] for m in range(partners)]
        down2.append(by_kernel(far_sum(rows, coupling, i), rank).astype(BF))
    down1 = []
    for j in range(2 * count):
        down1.append((far1[j] + dot_t(down2[j // 2], ptr[j])).astype(BF))
    down0 = []
    for t in range(leaves):
        down0.append((far0[t] + dot_t(down1[t // 2], ltr[t])).astype(BF))
    for t in range(leaves):
        points = (dot_t(down0[t], basis[t]) + close[t]).astype(BF)
        for k in range(kernels):
            out[k, t] = points[k * vecs:(k + 1) * vecs]


def rest_pass(tlist, arrays, pieces, offs):
    coupling = arrays[0]
    kernels, count, _, rank, _ = coupling.shape
    leaves = arrays[3].shape[0]
    vecs = pieces[0].shape[2]
    return call(
        functools.partial(rest_body, offs), "rest", (tlist,), arrays + pieces,
        jax.ShapeDtypeStruct((kernels, leaves, vecs, rank), BF),
        WHOLE,
        [held(tlist), VMEM((4 * pieces[0].shape[0] * count, vecs, rank), BF), DMA((1,))],
        (150_000_000, 20_000_000), 16 * 1024 * 1024,
    )


def on_device(
    vectors,
    leaf_basis,
    leaf_transfer,
    pair_transfer,
    near_blocks,
    near_offset,
    leaf_send,
    leaf_list,
    leaf_coupling,
    pair_send,
    pair_list,
    pair_coupling,
    top_list,
    top_coupling,
):
    rows = lax.axis_size("row")
    devs = rows * lax.axis_size("col")
    cap0, cap1 = leaf_send.shape[2], pair_send.shape[2]
    lsend = jnp.transpose(leaf_send, (1, 0, 2))
    psend = jnp.transpose(pair_send, (0, 2, 1))
    held, own, sib, cross, fwd, back = up_pass(
        lsend, psend, vectors, leaf_basis, leaf_transfer, pair_transfer
    )
    ring = range(devs)

    def sent(piece, target):
        return lax.ppermute(piece, AXES, [(d, target(d)) for d in ring])

    offs = [0]
    mask = rows // 2
    got = sent(held, lambda d: d ^ (2 * mask))
    fwd = sent(fwd, lambda d: (d + 2) % devs)
    back = sent(back, lambda d: (d - 2) % devs)
    others = (fwd, back)
    while mask > 1:
        held = join_pass(held, got, *others)
        offs = offs + [off ^ mask for off in offs]
        mask //= 2
        got = sent(held, lambda d: d ^ (2 * mask))
        others = ()
    sib = sent(sib, lambda d: d ^ 1)
    cross = sent(cross, lambda d: (d + 1 if d % 2 else d - 1) % devs)
    pieces = (held, got, sent(held, lambda d: d ^ 1), sent(held, lambda d: d ^ 3))
    close, far0, far1 = near_pass(
        (near_offset.T, leaf_list.T, pair_list.T),
        (vectors, near_blocks, leaf_coupling, pair_coupling), (own, sib, cross, fwd, back), cap0, cap1,
    )
    return rest_pass(
        top_list, (top_coupling, pair_transfer, leaf_transfer, leaf_basis, close, far0, far1), pieces, offs
    )


def solution(mesh):
    placed = P(("groups", "row", "col"))
    behind = P(None, ("groups", "row", "col"))
    return jax.shard_map(
        on_device,
        mesh=mesh,
        in_specs=(
            placed, placed, placed, placed, behind, placed, placed, placed, behind, placed, placed, behind, placed, behind,
        ),
        out_specs=behind,
        check_vma=False,
    )
```

```python
import functools

import jax
import jax.numpy as jnp
from jax import lax
from jax.experimental import pallas as pl
from jax.experimental.pallas import tpu as pltpu
from jax.sharding import PartitionSpec as P

REACH = 2
WIN = 2 * REACH + 1
HW = 2
AXES = ("row", "col")
F32 = jnp.float32
BF = jnp.bfloat16
LIMIT = 56 * 1024 * 1024

VMEM = pltpu.VMEM
SMEM = pltpu.SMEM
DMA = pltpu.SemaphoreType.DMA
FIXED = pl.BlockSpec(memory_space=pltpu.HBM)
WHOLE = pl.BlockSpec(memory_space=VMEM)


def dot(left, right):
    return jnp.dot(left, right, preferred_element_type=F32)


def beside(*parts):
    return jnp.concatenate(parts, axis=1)


def above(*parts):
    return jnp.concatenate(parts, axis=0)


def dot_t(left, right):
    return lax.dot_general(left, right, (((1,), (1,)), ((), ())), preferred_element_type=F32)


def row_of_blocks(ref, q):
    kernels, _, partners, _, _ = ref.shape
    return beside(*[above(*[ref[k, q, m] for k in range(kernels)]) for m in range(partners)])


def by_kernel(wide, rank):
    return above(*[wide[:, k * rank:(k + 1) * rank] for k in range(wide.shape[1] // rank)])


def copies(pairs, sems):
    made = [pltpu.make_async_copy(src, dst, sems.at[i]) for i, (src, dst) in enumerate(pairs)]
    for copy in made:
        copy.start()
    return made


def split(row, ref, at):
    rank = row.shape[1] // 2
    ref[at] = row[:, :rank]
    ref[at + 1] = row[:, rank:]


def call(body, name, params, arrays, out_shape, out_specs, scratch, cost, limit=LIMIT):
    return pl.pallas_call(
        body,
        out_shape=out_shape,
        in_specs=[FIXED] * len(params) + [WHOLE] * len(arrays),
        out_specs=out_specs,
        scratch_shapes=scratch,
        compiler_params=pltpu.CompilerParams(vmem_limit_bytes=limit),
        cost_estimate=pl.CostEstimate(flops=cost[0], bytes_accessed=cost[1], transcendentals=0),
        name=name,
    )(*params, *arrays)


def like(x):
    return VMEM(x.shape, x.dtype)


def held(x):
    return SMEM(x.shape, x.dtype)


def up_body(vec_h, basis_h, ltr_h, ptr_h, lsend_h, psend_h, tops, own, sib, cross, fwd, back,
            vec, basis, ltr, ptr, lsend, psend, low, mid, sems):
    leaves, vecs, rank = vec.shape
    col = lax.axis_index("col")
    cap0 = lsend.shape[2]
    cap1 = psend.shape[1]
    made = copies(
        [(vec_h, vec), (basis_h, basis), (ltr_h, ltr), (ptr_h, ptr), (lsend_h, lsend), (psend_h, psend)], sems
    )
    made[0].wait()
    made[1].wait()
    for t in range(leaves):
        low[t] = dot(vec[t], basis[t]).astype(BF)
    made[2].wait()
    for j in range(leaves // 2):
        mid[j] = dot(
            beside(low[2 * j], low[2 * j + 1]), ltr[2 * j:2 * j + 2].reshape(2 * rank, rank)
        ).astype(BF)
    made[3].wait()
    high = []
    for i in range(leaves // 4):
        high.append(
            dot(beside(mid[2 * i], mid[2 * i + 1]), ptr[2 * i:2 * i + 2].reshape(2 * rank, rank)).astype(BF)
        )
    for i in range(leaves // 8):
        tops[0, i] = beside(high[2 * i], high[2 * i + 1])
    made[4].wait()
    made[5].wait()

    def pack(out, place):
        for c in range(cap0 // 2):
            out[c] = beside(low[lsend[place, 0, 2 * c]], low[lsend[place, 0, 2 * c + 1]])
        for c in range(cap1 // 2):
            out[cap0 // 2 + c] = beside(mid[psend[0, 2 * c, place]], mid[psend[0, 2 * c + 1, place]])

    def pack_halo(out, start):
        out[(cap0 + cap1) // 2] = beside(vec[start], vec[start + 1])

    pack(sib, 1 + 2 * col)
    pack_halo(sib, (1 - col) * (leaves - HW))
    pack(cross, 3 - 2 * col)
    pack_halo(cross, col * (leaves - HW))
    pack(fwd, 0)
    pack(back, 4)
    pack(own, REACH)


def up_pass(lsend, psend, vec, basis, ltr, ptr):
    leaves, vecs, rank = vec.shape
    count = (lsend.shape[2] + psend.shape[1]) // 2
    shape = lambda *n: jax.ShapeDtypeStruct(n + (vecs, 2 * rank), BF)
    return call(
        up_body, "up", (vec, basis, ltr, ptr, lsend, psend), (),
        [shape(1, leaves // 8), shape(count), shape(count + 1), shape(count + 1), shape(count), shape(count)],
        [WHOLE] * 6,
        [
            like(vec), like(basis), like(ltr), like(ptr), held(lsend), held(psend),
            VMEM((leaves, vecs, rank), BF), VMEM((leaves // 2, vecs, rank), BF), DMA((6,)),
        ],
        (10_000_000, 3_000_000),
    )


def pass_body(src, out):
    out[...] = src[...]


def pass_on(x):
    return call(
        pass_body, "pass", (), (x,), jax.ShapeDtypeStruct(x.shape, x.dtype), WHOLE, [],
        (8_000_000_000, 100_000_000), 2 * 1024 * 1024,
    )


def join_body(first, second, *rest):
    out = rest[-1]
    out[:first.shape[0]] = first[...]
    out[first.shape[0]:] = second[...]


def join_pass(first, second, *others):
    return call(
        join_body, "join", (), (first, second) + others,
        jax.ShapeDtypeStruct((2 * first.shape[0],) + first.shape[1:], first.dtype), WHOLE, [],
        (8_000_000_000, 100_000_000) if others else (100_000, 500_000), 2 * 1024 * 1024,
    )


def far_sum(rows, blocks, q):
    return dot_t(beside(*rows), row_of_blocks(blocks, q))


def near_body(offsets_h, llist_h, plist_h, vec, near, leaf, pair, own, sib, cross, fwd, back, close, far0, far1,
              offsets, llist, plist, padded, wleaf, wpair, sems):
    leaves, vecs, rank = vec.shape
    partners = leaf.shape[2]
    cap0 = wleaf.shape[0] // WIN
    cap1 = wpair.shape[0] // WIN
    base = own.shape[0] - cap1 // 2
    col = lax.axis_index("col")
    place = lax.axis_index("row") * lax.axis_size("col") + col
    last_place = lax.axis_size("row") * lax.axis_size("col") - 1
    made = copies([(offsets_h, offsets), (llist_h, llist), (plist_h, plist)], sems)

    for block, slot in ((own, REACH), (fwd, 0), (back, 4), (sib, 3 - 2 * col), (cross, 1 + 2 * col)):
        for c in range(cap0 // 2):
            split(block[c], wleaf, slot * cap0 + 2 * c)
        for c in range(cap1 // 2):
            split(block[base + c], wpair, slot * cap1 + 2 * c)
    padded[HW:HW + leaves] = vec[...]
    for block, upper in ((sib, 1 - col), (cross, col)):
        row = block[base + cap1 // 2]
        outside = (place == 0) & (upper == 0) | (place == last_place) & (upper == 1)
        split(jnp.where(outside, jnp.zeros_like(row), row), padded, upper * (HW + leaves))
    for copy in made:
        copy.wait()

    for t in range(leaves):
        rows = [padded[t + HW + offsets[n, t]] for n in range(near.shape[2])]
        close[t] = by_kernel(far_sum(rows, near, t), rank)
        far0[t] = by_kernel(far_sum([wleaf[llist[m, t]] for m in range(partners)], leaf, t), rank)
        if t % 2:
            j = t // 2
            far1[j] = by_kernel(far_sum([wpair[plist[m, j]] for m in range(pair.shape[2])], pair, j), rank)


def near_pass(lists, arrays, windows, cap0, cap1):
    vec, blocks = arrays[:2]
    leaves, vecs, rank = vec.shape
    rows = blocks.shape[0] * vecs
    sums = [jax.ShapeDtypeStruct((n, rows, rank), F32) for n in (leaves, leaves, leaves // 2)]
    return call(
        near_body, "near", lists, arrays + windows, sums, [WHOLE] * 3,
        [held(x) for x in lists]
        + [VMEM((n, vecs, rank), BF) for n in (leaves + 2 * HW, WIN * cap0, WIN * cap1)] + [DMA((3,))],
        (1_000_000_000, 20_000_000), 8 * 1024 * 1024,
    )


def rest_body(offs, tlist_h, coupling, ptr, ltr, basis, close, far0, far1, held0, held1, held2, held3, out,
              tlist, tops, sems):
    kernels, count, partners, rank, _ = coupling.shape
    leaves = basis.shape[0]
    vecs = tops.shape[1]
    col = lax.axis_index("col")
    row = lax.axis_index("row")
    made = copies([(tlist_h, tlist)], sems)
    for h, block in enumerate((held0, held1, held2, held3)):
        side = col if h < 2 else 1 - col
        for s, off in enumerate(offs):
            for i in range(block.shape[1]):
                split(block[s, i], tops, (((row ^ (off + h % 2)) * 2) + side) * count + 2 * i)
    made[0].wait()

    down2 = []
    for i in range(count):
        rows = [tops[tlist[i, m]] for m in range(partners)]
        down2.append(by_kernel(far_sum(rows, coupling, i), rank).astype(BF))
    down1 = []
    for j in range(2 * count):
        down1.append((far1[j] + dot_t(down2[j // 2], ptr[j])).astype(BF))
    down0 = []
    for t in range(leaves):
        down0.append((far0[t] + dot_t(down1[t // 2], ltr[t])).astype(BF))
    for t in range(leaves):
        points = (dot_t(down0[t], basis[t]) + close[t]).astype(BF)
        for k in range(kernels):
            out[k, t] = points[k * vecs:(k + 1) * vecs]


def rest_pass(tlist, arrays, pieces, offs):
    coupling = arrays[0]
    kernels, count, _, rank, _ = coupling.shape
    leaves = arrays[3].shape[0]
    vecs = pieces[0].shape[2]
    return call(
        functools.partial(rest_body, offs), "rest", (tlist,), arrays + pieces,
        jax.ShapeDtypeStruct((kernels, leaves, vecs, rank), BF),
        WHOLE,
        [held(tlist), VMEM((4 * pieces[0].shape[0] * count, vecs, rank), BF), DMA((1,))],
        (150_000_000, 20_000_000), 16 * 1024 * 1024,
    )


def on_device(
    vectors,
    leaf_basis,
    leaf_transfer,
    pair_transfer,
    near_blocks,
    near_offset,
    leaf_send,
    leaf_list,
    leaf_coupling,
    pair_send,
    pair_list,
    pair_coupling,
    top_list,
    top_coupling,
):
    rows = lax.axis_size("row")
    devs = rows * lax.axis_size("col")
    cap0, cap1 = leaf_send.shape[2], pair_send.shape[2]
    lsend = jnp.transpose(leaf_send, (1, 0, 2))
    psend = jnp.transpose(pair_send, (0, 2, 1))
    held, own, sib, cross, fwd, back = up_pass(
        lsend, psend, vectors, leaf_basis, leaf_transfer, pair_transfer
    )
    ring = range(devs)

    def sent(piece, target):
        return lax.ppermute(piece, AXES, [(d, target(d)) for d in ring])

    offs = [0]
    mask = rows // 2
    got = sent(held, lambda d: d ^ (2 * mask))
    fwd = sent(fwd, lambda d: (d + 2) % devs)
    back = sent(back, lambda d: (d - 2) % devs)
    sib = sent(sib, lambda d: d ^ 1)
    cross = sent(cross, lambda d: (d + 1 if d % 2 else d - 1) % devs)
    others = (sib, cross, fwd, back)
    held = pass_on(held)
    while mask > 1:
        held = join_pass(held, got, *others)
        offs = offs + [off ^ mask for off in offs]
        mask //= 2
        got = sent(held, lambda d: d ^ (2 * mask))
        others = ()
    pieces = (held, got, sent(held, lambda d: d ^ 1), sent(held, lambda d: d ^ 3))
    close, far0, far1 = near_pass(
        (near_offset.T, leaf_list.T, pair_list.T),
        (vectors, near_blocks, leaf_coupling, pair_coupling), (own, sib, cross, fwd, back), cap0, cap1,
    )
    return rest_pass(
        top_list, (top_coupling, pair_transfer, leaf_transfer, leaf_basis, close, far0, far1), pieces, offs
    )


def solution(mesh):
    placed = P(("groups", "row", "col"))
    behind = P(None, ("groups", "row", "col"))
    return jax.shard_map(
        on_device,
        mesh=mesh,
        in_specs=(
            placed, placed, placed, placed, behind, placed, placed, placed, behind, placed, placed, behind, placed, behind,
        ),
        out_specs=behind,
        check_vma=False,
    )
```

```python
import functools

import jax
import jax.numpy as jnp
from jax import lax
from jax.experimental import pallas as pl
from jax.experimental.pallas import tpu as pltpu
from jax.sharding import PartitionSpec as P

REACH = 2
WIN = 2 * REACH + 1
HW = 2
AXES = ("row", "col")
F32 = jnp.float32
BF = jnp.bfloat16
LIMIT = 56 * 1024 * 1024

VMEM = pltpu.VMEM
SMEM = pltpu.SMEM
DMA = pltpu.SemaphoreType.DMA
FIXED = pl.BlockSpec(memory_space=pltpu.HBM)
WHOLE = pl.BlockSpec(memory_space=VMEM)


def dot(left, right):
    return jnp.dot(left, right, preferred_element_type=F32)


def beside(*parts):
    return jnp.concatenate(parts, axis=1)


def above(*parts):
    return jnp.concatenate(parts, axis=0)


def dot_t(left, right):
    return lax.dot_general(left, right, (((1,), (1,)), ((), ())), preferred_element_type=F32)


def row_of_blocks(ref, q):
    kernels, _, partners, _, _ = ref.shape
    return beside(*[above(*[ref[k, q, m] for k in range(kernels)]) for m in range(partners)])


def by_kernel(wide, rank):
    return above(*[wide[:, k * rank:(k + 1) * rank] for k in range(wide.shape[1] // rank)])


def copies(pairs, sems):
    made = [pltpu.make_async_copy(src, dst, sems.at[i]) for i, (src, dst) in enumerate(pairs)]
    for copy in made:
        copy.start()
    return made


def split(row, ref, at):
    rank = row.shape[1] // 2
    ref[at] = row[:, :rank]
    ref[at + 1] = row[:, rank:]


def call(body, name, params, arrays, out_shape, out_specs, scratch, cost, limit=LIMIT):
    return pl.pallas_call(
        body,
        out_shape=out_shape,
        in_specs=[FIXED] * len(params) + [WHOLE] * len(arrays),
        out_specs=out_specs,
        scratch_shapes=scratch,
        compiler_params=pltpu.CompilerParams(vmem_limit_bytes=limit),
        cost_estimate=pl.CostEstimate(flops=cost[0], bytes_accessed=cost[1], transcendentals=0),
        name=name,
    )(*params, *arrays)


def like(x):
    return VMEM(x.shape, x.dtype)


def held(x):
    return SMEM(x.shape, x.dtype)


def up_body(vec_h, basis_h, ltr_h, ptr_h, lsend_h, psend_h, tops, own, sib, cross, fwd, back,
            vec, basis, ltr, ptr, lsend, psend, low, mid, sems):
    leaves, vecs, rank = vec.shape
    col = lax.axis_index("col")
    cap0 = lsend.shape[2]
    cap1 = psend.shape[1]
    made = copies(
        [(vec_h, vec), (basis_h, basis), (ltr_h, ltr), (ptr_h, ptr), (lsend_h, lsend), (psend_h, psend)], sems
    )
    made[0].wait()
    made[1].wait()
    for t in range(leaves):
        low[t] = dot(vec[t], basis[t]).astype(BF)
    made[2].wait()
    for j in range(leaves // 2):
        mid[j] = dot(
            beside(low[2 * j], low[2 * j + 1]), ltr[2 * j:2 * j + 2].reshape(2 * rank, rank)
        ).astype(BF)
    made[3].wait()
    high = []
    for i in range(leaves // 4):
        high.append(
            dot(beside(mid[2 * i], mid[2 * i + 1]), ptr[2 * i:2 * i + 2].reshape(2 * rank, rank)).astype(BF)
        )
    for i in range(leaves // 8):
        tops[0, i] = beside(high[2 * i], high[2 * i + 1])
    made[4].wait()
    made[5].wait()

    def pack(out, place):
        for c in range(cap0 // 2):
            out[c] = beside(low[lsend[place, 0, 2 * c]], low[lsend[place, 0, 2 * c + 1]])
        for c in range(cap1 // 2):
            out[cap0 // 2 + c] = beside(mid[psend[0, 2 * c, place]], mid[psend[0, 2 * c + 1, place]])

    def pack_halo(out, start):
        out[(cap0 + cap1) // 2] = beside(vec[start], vec[start + 1])

    pack(sib, 1 + 2 * col)
    pack_halo(sib, (1 - col) * (leaves - HW))
    pack(cross, 3 - 2 * col)
    pack_halo(cross, col * (leaves - HW))
    pack(fwd, 0)
    pack(back, 4)
    pack(own, REACH)


def up_pass(lsend, psend, vec, basis, ltr, ptr):
    leaves, vecs, rank = vec.shape
    count = (lsend.shape[2] + psend.shape[1]) // 2
    shape = lambda *n: jax.ShapeDtypeStruct(n + (vecs, 2 * rank), BF)
    return call(
        up_body, "up", (vec, basis, ltr, ptr, lsend, psend), (),
        [shape(1, leaves // 8), shape(count), shape(count + 1), shape(count + 1), shape(count), shape(count)],
        [WHOLE] * 6,
        [
            like(vec), like(basis), like(ltr), like(ptr), held(lsend), held(psend),
            VMEM((leaves, vecs, rank), BF), VMEM((leaves // 2, vecs, rank), BF), DMA((6,)),
        ],
        (10_000_000, 3_000_000),
    )


def pass_body(src, out):
    out[...] = src[...]


def pass_on(x):
    return call(
        pass_body, "pass", (), (x,), jax.ShapeDtypeStruct(x.shape, x.dtype), WHOLE, [],
        (8_000_000_000, 100_000_000), 2 * 1024 * 1024,
    )


def join_body(first, second, *rest):
    out = rest[-1]
    out[:first.shape[0]] = first[...]
    out[first.shape[0]:] = second[...]


def join_pass(first, second, *others):
    return call(
        join_body, "join", (), (first, second) + others,
        jax.ShapeDtypeStruct((2 * first.shape[0],) + first.shape[1:], first.dtype), WHOLE, [],
        (8_000_000_000, 100_000_000) if others else (100_000, 500_000), 2 * 1024 * 1024,
    )


def far_sum(rows, blocks, q):
    return dot_t(beside(*rows), row_of_blocks(blocks, q))


def near_body(offsets_h, llist_h, plist_h, vec, near, leaf, pair, own, sib, cross, fwd, back, close, far0, far1,
              offsets, llist, plist, padded, wleaf, wpair, sems):
    leaves, vecs, rank = vec.shape
    partners = leaf.shape[2]
    cap0 = wleaf.shape[0] // WIN
    cap1 = wpair.shape[0] // WIN
    base = own.shape[0] - cap1 // 2
    col = lax.axis_index("col")
    place = lax.axis_index("row") * lax.axis_size("col") + col
    last_place = lax.axis_size("row") * lax.axis_size("col") - 1
    made = copies([(offsets_h, offsets), (llist_h, llist), (plist_h, plist)], sems)

    for block, slot in ((own, REACH), (fwd, 0), (back, 4), (sib, 3 - 2 * col), (cross, 1 + 2 * col)):
        for c in range(cap0 // 2):
            split(block[c], wleaf, slot * cap0 + 2 * c)
        for c in range(cap1 // 2):
            split(block[base + c], wpair, slot * cap1 + 2 * c)
    padded[HW:HW + leaves] = vec[...]
    for block, upper in ((sib, 1 - col), (cross, col)):
        row = block[base + cap1 // 2]
        outside = (place == 0) & (upper == 0) | (place == last_place) & (upper == 1)
        split(jnp.where(outside, jnp.zeros_like(row), row), padded, upper * (HW + leaves))
    for copy in made:
        copy.wait()

    for t in range(leaves):
        rows = [padded[t + HW + offsets[n, t]] for n in range(near.shape[2])]
        close[t] = by_kernel(far_sum(rows, near, t), rank)
        far0[t] = by_kernel(far_sum([wleaf[llist[m, t]] for m in range(partners)], leaf, t), rank)
        if t % 2:
            j = t // 2
            far1[j] = by_kernel(far_sum([wpair[plist[m, j]] for m in range(pair.shape[2])], pair, j), rank)


def near_pass(lists, arrays, windows, cap0, cap1):
    vec, blocks = arrays[:2]
    leaves, vecs, rank = vec.shape
    rows = blocks.shape[0] * vecs
    sums = [jax.ShapeDtypeStruct((n, rows, rank), F32) for n in (leaves, leaves, leaves // 2)]
    return call(
        near_body, "near", lists, arrays + windows, sums, [WHOLE] * 3,
        [held(x) for x in lists]
        + [VMEM((n, vecs, rank), BF) for n in (leaves + 2 * HW, WIN * cap0, WIN * cap1)] + [DMA((3,))],
        (1_000_000_000, 20_000_000), 8 * 1024 * 1024,
    )


def rest_body(offs, tlist_h, coupling, ptr, ltr, basis, close, far0, far1, held0, held1, held2, held3, out,
              tlist, tops, sems):
    kernels, count, partners, rank, _ = coupling.shape
    leaves = basis.shape[0]
    vecs = tops.shape[1]
    col = lax.axis_index("col")
    row = lax.axis_index("row")
    made = copies([(tlist_h, tlist)], sems)
    for h, block in enumerate((held0, held1, held2, held3)):
        side = col if h < 2 else 1 - col
        for s, off in enumerate(offs):
            for i in range(block.shape[1]):
                split(block[s, i], tops, (((row ^ (off + h % 2)) * 2) + side) * count + 2 * i)
    made[0].wait()

    down2 = []
    for i in range(count):
        rows = [tops[tlist[i, m]] for m in range(partners)]
        down2.append(by_kernel(far_sum(rows, coupling, i), rank).astype(BF))
    down1 = []
    for j in range(2 * count):
        down1.append((far1[j] + dot_t(down2[j // 2], ptr[j])).astype(BF))
    down0 = []
    for t in range(leaves):
        down0.append((far0[t] + dot_t(down1[t // 2], ltr[t])).astype(BF))
    for t in range(leaves):
        points = (dot_t(down0[t], basis[t]) + close[t]).astype(BF)
        for k in range(kernels):
            out[k, t] = points[k * vecs:(k + 1) * vecs]


def rest_pass(tlist, arrays, pieces, offs):
    coupling = arrays[0]
    kernels, count, _, rank, _ = coupling.shape
    leaves = arrays[3].shape[0]
    vecs = pieces[0].shape[2]
    return call(
        functools.partial(rest_body, offs), "rest", (tlist,), arrays + pieces,
        jax.ShapeDtypeStruct((kernels, leaves, vecs, rank), BF),
        WHOLE,
        [held(tlist), VMEM((4 * pieces[0].shape[0] * count, vecs, rank), BF), DMA((1,))],
        (150_000_000, 20_000_000), 16 * 1024 * 1024,
    )


def on_device(
    vectors,
    leaf_basis,
    leaf_transfer,
    pair_transfer,
    near_blocks,
    near_offset,
    leaf_send,
    leaf_list,
    leaf_coupling,
    pair_send,
    pair_list,
    pair_coupling,
    top_list,
    top_coupling,
):
    rows = lax.axis_size("row")
    devs = rows * lax.axis_size("col")
    cap0, cap1 = leaf_send.shape[2], pair_send.shape[2]
    lsend = jnp.transpose(leaf_send, (1, 0, 2))
    psend = jnp.transpose(pair_send, (0, 2, 1))
    held, own, sib, cross, fwd, back = up_pass(
        lsend, psend, vectors, leaf_basis, leaf_transfer, pair_transfer
    )
    ring = range(devs)

    def sent(piece, target):
        return lax.ppermute(piece, AXES, [(d, target(d)) for d in ring])

    offs = [0]
    mask = rows // 2
    got = sent(held, lambda d: d ^ (2 * mask))
    fwd = sent(fwd, lambda d: (d + 2) % devs)
    back = sent(back, lambda d: (d - 2) % devs)
    others = (fwd, back)
    held = pass_on(held)
    while mask > 1:
        held = join_pass(held, got, *others)
        offs = offs + [off ^ mask for off in offs]
        mask //= 2
        got = sent(held, lambda d: d ^ (2 * mask))
        others = ()
    sib = sent(sib, lambda d: d ^ 1)
    cross = sent(cross, lambda d: (d + 1 if d % 2 else d - 1) % devs)
    pieces = (held, got, sent(held, lambda d: d ^ 1), sent(held, lambda d: d ^ 3))
    close, far0, far1 = near_pass(
        (near_offset.T, leaf_list.T, pair_list.T),
        (vectors, near_blocks, leaf_coupling, pair_coupling), (own, sib, cross, fwd, back), cap0, cap1,
    )
    return rest_pass(
        top_list, (top_coupling, pair_transfer, leaf_transfer, leaf_basis, close, far0, far1), pieces, offs
    )


def solution(mesh):
    placed = P(("groups", "row", "col"))
    behind = P(None, ("groups", "row", "col"))
    return jax.shard_map(
        on_device,
        mesh=mesh,
        in_specs=(
            placed, placed, placed, placed, behind, placed, placed, placed, behind, placed, placed, behind, placed, behind,
        ),
        out_specs=behind,
        check_vma=False,
    )
```
